32 devices in a mesh: grp: 2 (over core), shard: 16 (over z, y, x).
Axes of the slice: x: 2, y: 2, z: 4, core: 2. Of those that a mesh axis runs over, the one named last changes fastest.
Arguments:
- inputs: bfloat16 [4096, 2048], P(('grp', 'shard')), may hold values from -6 to 6
- positions: int32 [4096], P(('grp', 'shard')), may hold values from 0 to 1023, as said below
- cotangent: bfloat16 [4096, 2048], P(('grp', 'shard')), may hold values from -6 to 6
- w_query: bfloat16 [2048, 2048], P('shard'), may hold values from -0.125 to 0.125
- w_key: bfloat16 [2048, 2048], P('shard'), may hold values from -0.125 to 0.125
- w_value: bfloat16 [2048, 2048], P('shard'), may hold values from -0.125 to 0.125
- w_out: bfloat16 [2048, 2048], P('shard'), may hold values from -0.125 to 0.125
- query_gain: bfloat16 [2048], P('shard'), may hold values from 0.25 to 1.75
- key_gain: bfloat16 [2048], P('shard'), may hold values from 0.25 to 1.75
- attn_gain: bfloat16 [2048], P('shard'), may hold values from 0.5 to 1.5
- w_gate: bfloat16 [2048, 8192], P('shard'), may hold values from -0.125 to 0.125
- w_up: bfloat16 [2048, 8192], P('shard'), may hold values from -0.125 to 0.125
- w_down: bfloat16 [8192, 2048], P('shard'), may hold values from -0.0625 to 0.0625
- mlp_gain: bfloat16 [2048], P('shard'), may hold values from 0.5 to 1.5
Outputs:
- output: bfloat16 [4096, 2048], P(('grp', 'shard'))
- input_grad: float32 [4096, 2048], P(('grp', 'shard'))
- query_grad: float32 [2048, 2048], P('shard')
- key_grad: float32 [2048, 2048], P('shard')
- value_grad: float32 [2048, 2048], P('shard')
- out_grad: float32 [2048, 2048], P('shard')
- querygain_grad: float32 [2048], P('shard')
- keygain_grad: float32 [2048], P('shard')
- attngain_grad: float32 [2048], P('shard')
- gate_grad: float32 [2048, 8192], P('shard')
- up_grad: float32 [2048, 8192], P('shard')
- down_grad: float32 [8192, 2048], P('shard')
- mlpgain_grad: float32 [2048], P('shard')
The draws below stay inside these ranges and needn't reach their ends.
Inputs may be any that keep to these rules, and one draw needn't show every extreme that they name: positions[t] is t minus the first index of the document that holds token t; documents are contiguous runs of 1 to 1024 tokens, at least one of exactly 1024; positions[0] = 0.
All inputs are finite; a program needn't handle non-finite values.
Results may differ from the reference program's by a relative error of at most 0.02.
Values may be sent and summed in bfloat16 or wider, within the bound.
No kernel may reach another device: no remote copies, remote signals or barrier semaphores. Data moves between devices by JAX's collectives and lax.ppermute only.
A program may use at most 512 MiB of HBM per device.

```python
import math
import jax
import jax.numpy as jnp
from jax import lax

D = 2048
HEADS = 16
HEAD = 128
FF = 8192
DOC_LEN = 1024
TOKENS = 4096


def draw_positions(key, part):
    key = jax.random.fold_in(key, 11)
    block_count = (TOKENS + DOC_LEN - 1) // DOC_LEN
    key_cuts, key_flags, key_whole = jax.random.split(key, 3)
    cut_points = jax.random.randint(key_cuts, (block_count, 2), 1, DOC_LEN)
    cut_flags = jax.random.randint(key_flags, (block_count, 2), 0, 2)
    whole_block = jax.random.randint(key_whole, (), 0, TOKENS // DOC_LEN)
    cut_flags = jnp.where((jnp.arange(block_count) == whole_block)[:, None], 0, cut_flags)
    stream = jnp.arange(TOKENS, dtype=jnp.int32)
    block_index = stream // DOC_LEN
    offset_in = stream % DOC_LEN
    starting = offset_in == 0
    starting = starting | (offset_in == cut_points[block_index, 0]) & (cut_flags[block_index, 0] == 1)
    starting = starting | (offset_in == cut_points[block_index, 1]) & (cut_flags[block_index, 1] == 1)
    marks = jnp.where(starting, stream, 0)
    first_index = lax.cummax(marks, axis=0)
    return (stream - first_index).astype(jnp.int32)


def levels(key, shape, cuts, low, largest):
    level = 1.0
    for position, parts in cuts:
        heights = jax.random.uniform(jax.random.fold_in(jax.random.fold_in(key, 6), position), (parts,), jnp.float32, low / len(cuts), largest / len(cuts))
        level = level * jnp.repeat(jnp.exp(heights), shape[position] // parts).reshape((-1,) + (1,) * (len(shape) - 1 - position))
    return level


def gaussian(own_key, shape, scale, bound, cuts=(), kind=jnp.bfloat16):
    factor_of = levels(own_key, shape, cuts, -0.22, 0.18) if cuts else 1.0
    array = jax.random.normal(own_key, shape, jnp.float32) * scale * factor_of
    return jnp.minimum(jnp.maximum(array, -bound), bound).astype(kind)


def setup_inputs(seed: int = 0) -> dict:
    arg_keys = jax.random.split(jax.random.key(seed), 15)
    return {
        "inputs": gaussian(arg_keys[0], (TOKENS, D), 1.0, 6.0, ((0, 32),)),
        "positions": draw_positions(jax.random.fold_in(arg_keys[14], 71), 0),
        "cotangent": gaussian(arg_keys[2], (TOKENS, D), 1.0, 6.0, ((0, 32),)),
        "w_query": gaussian(arg_keys[3], (D, D), D ** -0.5, 0.125, ((0, 16),)),
        "w_key": gaussian(arg_keys[4], (D, D), D ** -0.5, 0.125, ((0, 16),)),
        "w_value": gaussian(arg_keys[5], (D, D), D ** -0.5, 0.125, ((0, 16),)),
        "w_out": gaussian(arg_keys[6], (D, D), D ** -0.5, 0.125, ((0, 16),)),
        "query_gain": jnp.clip(1.0 + 0.15 * jax.random.normal(arg_keys[7], (D,), jnp.float32), 0.25, 1.75).astype(jnp.bfloat16),
        "key_gain": jnp.clip(1.0 + 0.15 * jax.random.normal(arg_keys[8], (D,), jnp.float32), 0.25, 1.75).astype(jnp.bfloat16),
        "attn_gain": jnp.clip(1.0 + 0.1 * jax.random.normal(arg_keys[9], (D,), jnp.float32), 0.5, 1.5).astype(jnp.bfloat16),
        "w_gate": gaussian(arg_keys[10], (D, FF), D ** -0.5, 0.125, ((0, 16),)),
        "w_up": gaussian(arg_keys[11], (D, FF), D ** -0.5, 0.125, ((0, 16),)),
        "w_down": gaussian(arg_keys[12], (FF, D), FF ** -0.5, 0.0625, ((0, 16),)),
        "mlp_gain": jnp.clip(1.0 + 0.1 * jax.random.normal(arg_keys[13], (D,), jnp.float32), 0.5, 1.5).astype(jnp.bfloat16),
    }


@jax.custom_vjp
def low(v):
    return lax.optimization_barrier(v.astype(jnp.bfloat16)).astype(jnp.float32)

@jax.custom_vjp
def low_back(v):
    return v

def low_keep(v):
    return (low(v), None)

def low_pass(kept, grad):
    return (grad,)

def back_keep(v):
    return (v, None)

def back_low(kept, grad):
    return (low(grad),)
low.defvjp(low_keep, low_pass)
low_back.defvjp(back_keep, back_low)

def norm_rows(values, scales):
    return values * lax.rsqrt(lax.optimization_barrier(jnp.mean(values * values, axis=-1, keepdims=True)) + 1e-06) * scales

def rotate(values, positions):
    middle = HEAD // 2
    shaped = values.reshape(values.shape[0], HEADS, HEAD)
    frequency = jnp.power(500000.0, -2.0 * jnp.arange(middle).astype(jnp.float32) / HEAD)
    angles = positions.astype(jnp.float32)[:, None] * frequency[None, :]
    cosines = jnp.cos(angles)[:, None, :]
    sines = jnp.sin(angles)[:, None, :]
    first_half = shaped[..., :middle]
    second_half = shaped[..., middle:]
    turned = jnp.concatenate([first_half * cosines - second_half * sines, second_half * cosines + first_half * sines], axis=-1)
    return turned.reshape(values.shape)

def attend(queries, keys, values, positions):
    highest = lax.Precision.HIGHEST
    block_rows = math.gcd(TOKENS, 512)
    back_rows = DOC_LEN
    scaling = 1.0 / math.sqrt(HEAD)
    query_heads = queries.reshape(TOKENS, HEADS, HEAD)
    key_heads = jnp.pad(keys.reshape(TOKENS, HEADS, HEAD), ((back_rows, 0), (0, 0), (0, 0)))
    value_heads = jnp.pad(values.reshape(TOKENS, HEADS, HEAD), ((back_rows, 0), (0, 0), (0, 0)))
    distance = jnp.arange(block_rows)[:, None] + back_rows - jnp.arange(block_rows + back_rows)[None, :]

    def attend_block(start):
        query_block = lax.dynamic_slice_in_dim(query_heads, start, block_rows, 0)
        key_block = lax.dynamic_slice_in_dim(key_heads, start, block_rows + back_rows, 0)
        value_block = lax.dynamic_slice_in_dim(value_heads, start, block_rows + back_rows, 0)
        place = lax.dynamic_slice_in_dim(positions, start, block_rows, 0)
        scores = low_back(jnp.einsum('qhd,khd->hqk', query_block, key_block, precision=highest)) * scaling
        visible = (distance >= 0) & (distance <= place[:, None])
        scores = jnp.where(visible[None], scores, -jnp.inf)
        probs = jax.nn.softmax(scores, axis=-1)
        mixed = jnp.einsum('hqk,khd->qhd', low(probs), value_block, precision=highest)
        return mixed.reshape(block_rows, HEADS * HEAD)
    starts = (jnp.arange(TOKENS // block_rows) * block_rows).astype(jnp.int32)
    return lax.map(jax.checkpoint(attend_block), starts).reshape(TOKENS, HEADS * HEAD)

def reference(inputs, positions, cotangent, w_query, w_key, w_value, w_out, query_gain, key_gain, attn_gain, w_gate, w_up, w_down, mlp_gain):
    highest = lax.Precision.HIGHEST

    def project(left, right):
        return jnp.dot(left, right, precision=highest)

    def layer_forward(inputs_float, query_w, key_w, value_w, out_w, query_scale, key_scale, attn_scale, gate_w, up_w, down_w, mlp_scale):
        q_raw = low_back(project(inputs_float, query_w))
        k_raw = low_back(project(inputs_float, key_w))
        value_low = low(low_back(project(inputs_float, value_w)))
        query_low = low(rotate(norm_rows(q_raw, query_scale), positions))
        key_low = low(rotate(norm_rows(k_raw, key_scale), positions))
        mixed = low(low_back(attend(query_low, key_low, value_low, positions)))
        branch = low_back(project(mixed, out_w))
        hidden_state = inputs_float + norm_rows(branch, attn_scale)
        state_low = low(hidden_state)
        gate_val = low_back(project(state_low, gate_w))
        up_val = low_back(project(state_low, up_w))
        activated = low(jax.nn.silu(gate_val) * up_val)
        mlp_out = low_back(project(activated, down_w))
        return hidden_state + norm_rows(mlp_out, mlp_scale)
    result, pull_back = jax.vjp(layer_forward, inputs.astype(jnp.float32), w_query.astype(jnp.float32), w_key.astype(jnp.float32), w_value.astype(jnp.float32), w_out.astype(jnp.float32), query_gain.astype(jnp.float32), key_gain.astype(jnp.float32), attn_gain.astype(jnp.float32), w_gate.astype(jnp.float32), w_up.astype(jnp.float32), w_down.astype(jnp.float32), mlp_gain.astype(jnp.float32))
    grads = pull_back(cotangent.astype(jnp.float32))
    return (result.astype(jnp.bfloat16), grads[0], grads[1], grads[2], grads[3], grads[4], grads[5], grads[6], grads[7], grads[8], grads[9], grads[10], grads[11])
```

```python
import math

import jax
import jax.numpy as jnp
from jax import lax
from jax.experimental import pallas as pl
from jax.experimental.pallas import tpu as pltpu
from jax.sharding import PartitionSpec as P

HEADS = 16
HEAD = 128
DOC_LEN = 1024


def from_behind(value, axis, steps):
    count = lax.axis_size(axis)
    leading, last = (max(0, -steps), min(count, count - steps))
    return lax.ppermute(value, axis, [(source, source + steps) for source in range(leading, last)])


def norm_rows(values, scales):
    return values * lax.rsqrt(jnp.mean(values * values, axis=-1, keepdims=True) + 1e-06) * scales


def rotate(values, cosines, sines):
    row_count = values.shape[0]
    middle = HEAD // 2
    shaped = values.reshape(row_count, HEADS, HEAD)
    first_half = shaped[..., :middle]
    second_half = shaped[..., middle:]
    turned = jnp.concatenate(
        [first_half * cosines - second_half * sines, second_half * cosines + first_half * sines],
        axis=-1,
    )
    return turned.reshape(row_count, HEADS * HEAD)


def activate(gate_in, up_in):
    return jax.nn.silu(gate_in) * up_in


def along_last(left, right):
    return lax.dot_general(
        left, right, (((1,), (1,)), ((), ())), preferred_element_type=jnp.float32
    )


def along_first(left, right):
    return lax.dot_general(
        left, right, (((0,), (0,)), ((), ())), preferred_element_type=jnp.float32
    )


def reduce_three(first_term, second_term, third_term):
    return (
        lax.psum_scatter(first_term, "shard", scatter_dimension=0, tiled=True),
        lax.psum_scatter(second_term, "shard", scatter_dimension=0, tiled=True),
        lax.psum_scatter(third_term, "shard", scatter_dimension=0, tiled=True),
    )


def local_general(
    inputs,
    positions,
    cotangent,
    w_query,
    w_key,
    w_value,
    w_out,
    query_gain,
    key_gain,
    attn_gain,
    w_gate,
    w_up,
    w_down,
    mlp_gain,
):
    row_count, feature_width = inputs.shape
    reach_back = (DOC_LEN - 2) // row_count + 1
    span_rows = min(row_count, 512)
    key_rows = span_rows + reach_back * row_count
    scaling = 1.0 / math.sqrt(HEAD)
    middle = HEAD // 2
    frequency = jnp.power(500000.0, -2.0 * jnp.arange(middle).astype(jnp.float32) / HEAD)
    angles = positions.astype(jnp.float32)[:, None] * frequency[None, :]
    cosines = jnp.cos(angles)[:, None, :]
    sines = jnp.sin(angles)[:, None, :]
    pieces = (
        lax.all_gather(w_query, "shard", axis=0, tiled=True),
        lax.all_gather(w_key, "shard", axis=0, tiled=True),
        lax.all_gather(w_value, "shard", axis=0, tiled=True),
        lax.all_gather(w_out, "shard", axis=0, tiled=True),
        lax.all_gather(query_gain, "shard", axis=0, tiled=True),
        lax.all_gather(key_gain, "shard", axis=0, tiled=True),
        lax.all_gather(attn_gain, "shard", axis=0, tiled=True),
        lax.all_gather(mlp_gain, "shard", axis=0, tiled=True),
    )
    columns_in = inputs
    acc_query = jnp.dot(columns_in, pieces[0], preferred_element_type=jnp.float32)
    acc_key = jnp.dot(columns_in, pieces[1], preferred_element_type=jnp.float32)
    acc_value = jnp.dot(columns_in, pieces[2], preferred_element_type=jnp.float32)
    out_full = pieces[3]
    gain_block = jnp.stack([pieces[4], pieces[5], pieces[6], pieces[7]]).astype(jnp.float32)
    gain_table = gain_block
    q_raw, k_raw, v_raw, out_full, gain_table = (
        acc_query,
        acc_key,
        acc_value,
        out_full,
        gain_table,
    )

    def prepare(query_in, key_in, query_scale, key_scale):
        return (
            rotate(norm_rows(query_in, query_scale), cosines, sines),
            rotate(norm_rows(key_in, key_scale), cosines, sines),
        )

    rotated, prepare_pull = jax.vjp(prepare, q_raw, k_raw, gain_table[0], gain_table[1])
    query_low = rotated[0].astype(jnp.bfloat16)
    key_value = jnp.stack([rotated[1].astype(jnp.bfloat16), v_raw.astype(jnp.bfloat16)])
    earlier = [
        from_behind(key_value, ("grp", "shard"), distance_back)
        for distance_back in range(reach_back, 0, -1)
    ]
    key_window = jnp.concatenate(earlier + [key_value], axis=1)
    distance = (
        jnp.arange(span_rows)[:, None] + reach_back * row_count - jnp.arange(key_rows)[None, :]
    )

    def block_scores(block_start):
        query_block = query_low.reshape(span_rows, HEADS, HEAD)
        key_block = key_window[0, block_start : block_start + key_rows].reshape(
            key_rows, HEADS, HEAD
        )
        value_block = key_window[1, block_start : block_start + key_rows].reshape(
            key_rows, HEADS, HEAD
        )
        visible = (distance >= 0) & (distance <= positions[:, None])
        scores = (
            jnp.einsum("qhd,khd->hqk", query_block, key_block, preferred_element_type=jnp.float32)
            * scaling
        )
        return (query_block, key_block, value_block, visible, scores)

    block_start = 0
    query_block, key_block, value_block, visible, scores = block_scores(block_start)
    masked = jnp.where(visible[None], scores, -jnp.inf)
    top_score = jnp.max(masked, axis=-1, keepdims=True)
    expo = jnp.exp(masked - top_score)
    totals = jnp.sum(expo, axis=-1, keepdims=True)
    probs_low = (expo / totals).astype(jnp.bfloat16)
    lse_parts = [top_score + jnp.log(totals)]
    mixed = jnp.einsum("hqk,khd->qhd", probs_low, value_block, preferred_element_type=jnp.float32)
    mixed_parts = mixed.reshape(span_rows, feature_width)
    mixed_low = mixed_parts.astype(jnp.bfloat16)
    branch = jnp.dot(mixed_low, out_full, preferred_element_type=jnp.float32)
    branch_normed, attn_pull = jax.vjp(norm_rows, branch, gain_table[2])
    hidden_state = inputs.astype(jnp.float32) + branch_normed
    state_low = hidden_state.astype(jnp.bfloat16)
    pieces = (
        lax.all_gather(w_gate, "shard", axis=0, tiled=True),
        lax.all_gather(w_up, "shard", axis=0, tiled=True),
    )
    columns_in = state_low
    gate_val = jnp.dot(columns_in, pieces[0], preferred_element_type=jnp.float32)
    up_val = jnp.dot(columns_in, pieces[1], preferred_element_type=jnp.float32)
    activated, act_pull = jax.vjp(activate, gate_val, up_val)
    activated_low = activated.astype(jnp.bfloat16)
    columns_in = activated_low
    mlp_out = jnp.dot(
        columns_in,
        lax.all_gather(w_down, "shard", axis=0, tiled=True),
        preferred_element_type=jnp.float32,
    )
    mlp_normed, mlp_pull = jax.vjp(norm_rows, mlp_out, gain_table[3])
    output = (hidden_state + mlp_normed).astype(jnp.bfloat16)
    cot_float = cotangent.astype(jnp.float32)
    d_mlp, d_mlp_gain = mlp_pull(cot_float)
    d_mlp_low = d_mlp.astype(jnp.bfloat16)
    d_hidden = along_last(d_mlp_low, lax.all_gather(w_down, "shard", axis=0, tiled=True))
    d_gate, d_up = act_pull(d_hidden)
    d_gate_low = d_gate.astype(jnp.bfloat16)
    d_up_low = d_up.astype(jnp.bfloat16)
    pieces = lax.all_gather((w_gate, w_up), "shard", axis=0, tiled=True)
    d_state = along_last(d_gate_low, pieces[0]) + along_last(d_up_low, pieces[1])
    d_resid = cot_float + d_state
    gate_term = along_first(state_low, d_gate_low)
    up_term = along_first(state_low, d_up_low)
    down_term = along_first(activated_low, d_mlp_low)
    ffn_sums = reduce_three(gate_term, up_term, down_term)
    d_branch, d_attn_gain = attn_pull(d_resid)
    d_branch_low = d_branch.astype(jnp.bfloat16)
    d_mixed_low = along_last(
        d_branch_low, lax.all_gather(w_out, "shard", axis=0, tiled=True)
    ).astype(jnp.bfloat16)
    dq_parts = []
    grad_window = jnp.zeros((2, (reach_back + 1) * row_count, feature_width), jnp.float32)
    for block_number, block_start in enumerate(range(0, row_count, span_rows)):
        query_block, key_block, value_block, visible, scores = block_scores(block_start)
        probs = jnp.where(visible[None], jnp.exp(scores - lse_parts[block_number]), 0.0)
        grad_block = d_mixed_low.reshape(span_rows, HEADS, HEAD)
        d_probs = jnp.einsum(
            "qhd,khd->hqk", grad_block, value_block, preferred_element_type=jnp.float32
        )
        inner = jnp.sum(probs * d_probs, axis=-1, keepdims=True)
        d_scores = (probs * (d_probs - inner) * scaling).astype(jnp.bfloat16)
        dq_block = jnp.einsum(
            "hqk,khd->qhd", d_scores, key_block, preferred_element_type=jnp.float32
        )
        dq_parts.append(dq_block.reshape(span_rows, feature_width))
        d_keys = jnp.einsum(
            "hqk,qhd->khd", d_scores, query_block, preferred_element_type=jnp.float32
        ).reshape(key_rows, feature_width)
        d_values = jnp.einsum(
            "hqk,qhd->khd",
            probs.astype(jnp.bfloat16),
            grad_block,
            preferred_element_type=jnp.float32,
        ).reshape(key_rows, feature_width)
        grad_window = grad_window.at[:, block_start : block_start + key_rows].add(
            jnp.stack([d_keys, d_values])
        )
    own_grads = grad_window[:, reach_back * row_count :]
    for distance_back in range(1, reach_back + 1):
        lower_row = (reach_back - distance_back) * row_count
        own_grads = own_grads + from_behind(
            grad_window[:, lower_row : lower_row + row_count].astype(jnp.bfloat16),
            ("grp", "shard"),
            -distance_back,
        ).astype(jnp.float32)
    d_query_raw, d_key_raw, d_query_gain, d_key_gain = prepare_pull((dq_parts[0], own_grads[0]))
    d_query_low = d_query_raw.astype(jnp.bfloat16)
    d_key_low = d_key_raw.astype(jnp.bfloat16)
    d_value_low = own_grads[1].astype(jnp.bfloat16)
    pieces = lax.all_gather((w_query, w_key, w_value), "shard", axis=0, tiled=True)
    d_inputs = (
        along_last(d_query_low, pieces[0])
        + along_last(d_key_low, pieces[1])
        + along_last(d_value_low, pieces[2])
    )
    input_grad = d_resid + d_inputs
    qkv_term = along_first(inputs, jnp.concatenate([d_query_low, d_key_low, d_value_low], axis=1))
    out_term = along_first(mixed_low, d_branch_low)
    gain_term = jnp.stack([d_query_gain, d_key_gain, d_attn_gain, d_mlp_gain], axis=1)
    attn_sums = reduce_three(qkv_term, out_term, gain_term)
    gate_sum, up_sum, down_sum, qkv_sum, out_sum, gain_sum = (
        lax.psum(ffn_sums[0].astype(jnp.bfloat16), "grp").astype(jnp.float32),
        lax.psum(ffn_sums[1].astype(jnp.bfloat16), "grp").astype(jnp.float32),
        lax.psum(ffn_sums[2].astype(jnp.bfloat16), "grp").astype(jnp.float32),
        lax.psum(attn_sums[0].astype(jnp.bfloat16), "grp").astype(jnp.float32),
        lax.psum(attn_sums[1].astype(jnp.bfloat16), "grp").astype(jnp.float32),
        lax.psum(attn_sums[2].astype(jnp.bfloat16), "grp").astype(jnp.float32),
    )
    return (
        output,
        input_grad,
        qkv_sum[:, :feature_width],
        qkv_sum[:, feature_width : 2 * feature_width],
        qkv_sum[:, 2 * feature_width :],
        out_sum,
        gain_sum[:, 0],
        gain_sum[:, 1],
        gain_sum[:, 2],
        gate_sum,
        up_sum,
        down_sum,
        gain_sum[:, 3],
    )


X, Y, Z, FAR = 1, 2, 4, 8
AXIS = {Z: 0, Y: 1, X: 2}
TRIPLE = ((X, Y, Z), (Y, Z, X), (Z, X, Y))
CUTS = (0, 768, 1408, 2048)
ROWS = 128
SLOTS = 16
WINDOW = 1152
SCALING = 1.0 / math.sqrt(HEAD)


def swap(value, bit):
    return lax.ppermute(value, "shard", [(source, source ^ bit) for source in range(16)])


def swap_core(value):
    return lax.ppermute(value, "grp", [(0, 1), (1, 0)])


def bit_of(bit):
    return (lax.axis_index("shard") & bit) != 0


def half(value, axis, number):
    return lax.slice_in_dim(value, number, number + 1, axis=axis)


def pick(value, axis, flag):
    return jnp.where(flag, half(value, axis, 1), half(value, axis, 0))


def ordered(mine, other, flag, axis):
    return jnp.concatenate(
        [jnp.where(flag, other, mine), jnp.where(flag, mine, other)], axis=axis
    )


def cube_gather(value):
    pieces = []
    for number, order in enumerate(TRIPLE):
        part = value[:, CUTS[number] : CUTS[number + 1]][None, None, None]
        for bit in order:
            part = jnp.concatenate([part, swap(part, bit)], axis=AXIS[bit])
        pieces.append(part)
    full = jnp.concatenate(pieces, axis=-1)
    return full.reshape(8 * value.shape[0], value.shape[1])


def cube_scatter(value):
    rows, width = value.shape[0] // 8, value.shape[1]
    shaped = value.reshape(2, 2, 2, rows, width)
    pieces = []
    for number, order in enumerate(TRIPLE):
        part = shaped[..., CUTS[number] : CUTS[number + 1]]
        for bit in order:
            part = part.astype(jnp.bfloat16)
            came = swap(half(part, AXIS[bit], 1), bit)
            part = half(part, AXIS[bit], 0).astype(jnp.float32) + came.astype(jnp.float32)
        pieces.append(part.reshape(rows, -1))
    return jnp.concatenate(pieces, axis=-1)


def turn(value, order):
    for bit in order:
        axis, flag = AXIS[bit], bit_of(bit)
        kept = pick(value, axis, flag)
        came = swap(pick(value, axis, ~flag), bit)
        value = ordered(kept, came, flag, axis)
    return value


def columns_weight(block, order):
    rows, width = block.shape[1:]
    turned = turn(block.reshape(2, 2, 2, rows, width), order)[None]
    whole = ordered(turned, swap(turned, FAR), bit_of(FAR), 0)
    return whole.reshape(16 * rows, width)


def columns_grad(grad, order, core):
    rows, width = grad.shape[0] // 16, grad.shape[1]
    shaped = grad.reshape(2, 2, 2, 2, rows, width)
    far = bit_of(FAR)
    came = swap(pick(shaped, 0, ~far).astype(jnp.bfloat16), FAR)
    summed = (pick(shaped, 0, far) + came.astype(jnp.float32)).astype(jnp.bfloat16)
    turned = turn(summed[0], order)[None]
    both = ordered(turned, swap_core(turned), core, 0)
    return both.reshape(2, 8, rows, width)


def add_up(value):
    came = swap_core(value)
    value = value + jnp.flip(came, 1)
    for bit, axis in ((Z, 2), (Y, 3), (X, 4)):
        value = value + jnp.flip(swap(value, bit), axis)
    return value


def visible_of(place):
    row = lax.broadcasted_iota(jnp.int32, (ROWS, WINDOW), 0)
    column = lax.broadcasted_iota(jnp.int32, (ROWS, WINDOW), 1)
    distance = row - column + (WINDOW - ROWS)
    return (distance >= 0) & (distance <= place)


def dot_last(left, right):
    return lax.dot_general(
        left, right, (((1,), (1,)), ((), ())), preferred_element_type=jnp.float32
    )


def fill(me, source, before, target):
    def put(number, carry):
        group, place = number // 8, number % 8
        slot = number ^ me
        target[group, pl.ds(pl.multiple_of(place * ROWS, ROWS), ROWS), :] = before[slot]
        target[group, pl.ds(pl.multiple_of((place + 8) * ROWS, ROWS), ROWS), :] = source[slot]
        return carry

    lax.fori_loop(0, SLOTS, put, 0)


def attend_kernel(me_ref, q_ref, k_ref, v_ref, pk_ref, pv_ref, pos_ref, o_ref, lse_ref, keys, values):
    me = me_ref[0]
    fill(me, k_ref, pk_ref, keys)
    fill(me, v_ref, pv_ref, values)

    def step(slot, carry):
        number = slot ^ me
        group, place = number // 8, number % 8
        rows = pl.ds(pl.multiple_of(place * ROWS, ROWS), WINDOW)
        scores = dot_last(q_ref[slot], keys[group, rows, :]) * SCALING
        masked = jnp.where(visible_of(pos_ref[slot]), scores, -jnp.inf)
        top = jnp.max(masked, axis=-1, keepdims=True)
        expo = jnp.exp(masked - top)
        total = jnp.sum(expo, axis=-1, keepdims=True)
        probs = (expo / total).astype(jnp.bfloat16)
        mixed = jnp.dot(probs, values[group, rows, :], preferred_element_type=jnp.float32)
        o_ref[slot] = mixed.astype(jnp.bfloat16)
        lse_ref[slot] = top + jnp.log(total)
        return carry

    lax.fori_loop(0, SLOTS, step, 0)


def attend_back_kernel(
    me_ref,
    q_ref,
    k_ref,
    v_ref,
    pk_ref,
    pv_ref,
    pos_ref,
    lse_ref,
    do_ref,
    dq_ref,
    dk_ref,
    dv_ref,
    dpk_ref,
    dpv_ref,
    keys,
    values,
    d_keys,
    d_values,
):
    me = me_ref[0]
    fill(me, k_ref, pk_ref, keys)
    fill(me, v_ref, pv_ref, values)
    d_keys[...] = jnp.zeros_like(d_keys)
    d_values[...] = jnp.zeros_like(d_values)

    def step(slot, carry):
        number = slot ^ me
        group, place = number // 8, number % 8
        rows = pl.ds(pl.multiple_of(place * ROWS, ROWS), WINDOW)
        query, grad = q_ref[slot], do_ref[slot]
        key, value = keys[group, rows, :], values[group, rows, :]
        scores = dot_last(query, key) * SCALING
        probs = jnp.where(visible_of(pos_ref[slot]), jnp.exp(scores - lse_ref[slot]), 0.0)
        d_probs = dot_last(grad, value)
        inner = jnp.sum(probs * d_probs, axis=-1, keepdims=True)
        d_scores = (probs * (d_probs - inner) * SCALING).astype(jnp.bfloat16)
        dq_ref[slot] = jnp.dot(d_scores, key, preferred_element_type=jnp.float32)
        d_keys[group, rows, :] += along_first(d_scores, query)
        d_values[group, rows, :] += along_first(probs.astype(jnp.bfloat16), grad)
        return carry

    lax.fori_loop(0, SLOTS, step, 0)

    def take(number, carry):
        group, place = number // 8, number % 8
        slot = number ^ me
        before = pl.ds(pl.multiple_of(place * ROWS, ROWS), ROWS)
        own = pl.ds(pl.multiple_of((place + 8) * ROWS, ROWS), ROWS)
        dpk_ref[slot] = d_keys[group, before, :].astype(jnp.bfloat16)
        dpv_ref[slot] = d_values[group, before, :].astype(jnp.bfloat16)
        dk_ref[slot] = d_keys[group, own, :]
        dv_ref[slot] = d_values[group, own, :]
        return carry

    lax.fori_loop(0, SLOTS, take, 0)


def in_vmem(count):
    return [pl.BlockSpec(memory_space=pltpu.SMEM)] + [pl.BlockSpec(memory_space=pltpu.VMEM)] * count


def attend(me, query, key, value, key_before, value_before, place):
    shape = (SLOTS, ROWS, HEAD)
    return pl.pallas_call(
        attend_kernel,
        out_shape=(
            jax.ShapeDtypeStruct(shape, jnp.bfloat16),
            jax.ShapeDtypeStruct((SLOTS, ROWS, 1), jnp.float32),
        ),
        in_specs=in_vmem(6),
        out_specs=[pl.BlockSpec(memory_space=pltpu.VMEM)] * 2,
        scratch_shapes=[pltpu.VMEM((2, 2048, HEAD), jnp.bfloat16)] * 2,
        compiler_params=pltpu.CompilerParams(vmem_limit_bytes=40 * 2**20),
        cost_estimate=pl.CostEstimate(
            flops=4 * 2048 * WINDOW * HEAD,
            bytes_accessed=6 * 2**20,
            transcendentals=2048 * WINDOW,
        ),
    )(me, query, key, value, key_before, value_before, place)


def attend_back(me, query, key, value, key_before, value_before, place, lse, grad):
    shape = (SLOTS, ROWS, HEAD)
    wide = jax.ShapeDtypeStruct(shape, jnp.float32)
    narrow = jax.ShapeDtypeStruct(shape, jnp.bfloat16)
    return pl.pallas_call(
        attend_back_kernel,
        out_shape=(wide, wide, wide, narrow, narrow),
        in_specs=in_vmem(8),
        out_specs=[pl.BlockSpec(memory_space=pltpu.VMEM)] * 5,
        scratch_shapes=[pltpu.VMEM((2, 2048, HEAD), jnp.bfloat16)] * 2
        + [pltpu.VMEM((2, 2048, HEAD), jnp.float32)] * 2,
        compiler_params=pltpu.CompilerParams(vmem_limit_bytes=40 * 2**20),
        cost_estimate=pl.CostEstimate(
            flops=10 * 2048 * WINDOW * HEAD,
            bytes_accessed=12 * 2**20,
            transcendentals=2048 * WINDOW,
        ),
    )(me, query, key, value, key_before, value_before, place, lse, grad)


def local_cube(
    inputs,
    positions,
    cotangent,
    w_query,
    w_key,
    w_value,
    w_out,
    query_gain,
    key_gain,
    attn_gain,
    w_gate,
    w_up,
    w_down,
    mlp_gain,
):
    bf16, f32 = jnp.bfloat16, jnp.float32
    width = inputs.shape[1]
    core_index = lax.axis_index("grp")
    shard_index = lax.axis_index("shard")
    core = core_index == 1
    far = bit_of(FAR)
    cube_index = shard_index % 8
    me = (core_index * 8 + cube_index).astype(jnp.int32).reshape(1)
    head = core_index * 8 + cube_index
    hidden = w_down.shape[0]

    def with_other(own):
        return own, swap_core(own)

    def head_columns(weight, order):
        blocks = weight.reshape(ROWS, 2, 8, HEAD).transpose(1, 2, 0, 3)
        return columns_weight(pick(blocks, 0, core)[0], order)

    def hidden_columns(weight, order):
        part = hidden // 2
        blocks = weight.reshape(ROWS, 2, 8, 2, part).transpose(3, 2, 0, 1, 4)
        return columns_weight(pick(blocks, 0, core)[0].reshape(8, ROWS, 2 * part), order)

    key_w = head_columns(w_key, TRIPLE[0])
    value_w = head_columns(w_value, TRIPLE[1])
    query_w = head_columns(w_query, TRIPLE[2])
    qkv_w = jnp.concatenate([query_w, key_w, value_w], axis=1)
    gate_w = hidden_columns(w_gate, TRIPLE[0])
    up_w = hidden_columns(w_up, TRIPLE[1])
    down_own = pick(w_down.reshape(2, hidden // 2, width), 0, core)
    down_w = ordered(down_own, swap(down_own, FAR), far, 0).reshape(hidden, width)
    to_far = [(s, s + 8) for s in range(8)] + [(24 + s, 16 + s) for s in range(8)]
    out_came = lax.ppermute(w_out, ("grp", "shard"), to_far)
    out_w = jnp.where(core == far, w_out, out_came)

    gains = jnp.stack([query_gain, key_gain, attn_gain, mlp_gain])[None]
    for bit in (X, Y, Z, FAR):
        gains = ordered(gains, swap(gains, bit), bit_of(bit), 0)
    gains = gains.astype(f32)
    head_gain = lax.dynamic_index_in_dim(gains, head, 0, keepdims=False)[:2]
    gains = gains.transpose(1, 0, 2).reshape(4, width)

    place = positions.reshape(1, 1, 1, ROWS)
    for bit in (X, Y, Z):
        place = jnp.concatenate([place, swap(place, bit)], axis=AXIS[bit])
    place = jnp.concatenate([place[None], swap_core(place)[None]], axis=0).reshape(SLOTS, ROWS, 1)

    middle = HEAD // 2
    frequency = jnp.power(500000.0, -2.0 * jnp.arange(middle).astype(f32) / HEAD)
    angles = place.astype(f32).reshape(SLOTS * ROWS, 1) * frequency[None, :]
    cosines = jnp.cos(angles)
    sines = jnp.sin(angles)
    cosines = jnp.concatenate([cosines, cosines], axis=1)
    sines = jnp.concatenate([-sines, sines], axis=1)

    def rotated(values):
        return values * cosines + jnp.roll(values, middle, axis=1) * sines

    def rotated_back(values):
        return values * cosines - jnp.roll(values, middle, axis=1) * sines

    def row_sums(first, second):
        sums = jnp.stack([jnp.sum(first, axis=-1), jnp.sum(second, axis=-1)])
        total = add_up(sums.reshape(2, 2, 2, 2, 2, ROWS))
        return total.reshape(2, SLOTS * ROWS, 1) / width

    x_own, x_other = with_other(cube_gather(inputs))
    raw = jnp.concatenate(
        [
            jnp.dot(x_own, qkv_w, preferred_element_type=f32),
            jnp.dot(x_other, qkv_w, preferred_element_type=f32),
        ]
    )
    q_raw, k_raw, v_raw = raw[:, :HEAD], raw[:, HEAD : 2 * HEAD], raw[:, 2 * HEAD :]
    means = row_sums(q_raw * q_raw, k_raw * k_raw)
    q_scale, k_scale = lax.rsqrt(means[0] + 1e-06), lax.rsqrt(means[1] + 1e-06)
    shape = (SLOTS, ROWS, HEAD)
    query = rotated(q_raw * q_scale * head_gain[0]).astype(bf16).reshape(shape)
    key = rotated(k_raw * k_scale * head_gain[1]).astype(bf16).reshape(shape)
    value = v_raw.astype(bf16).reshape(shape)

    onward = [(s, s + 8) for s in range(8)]
    backward = [(s + 8, s) for s in range(8)]

    def before(values):
        own, other = values[:8], values[8:]
        first, second = jnp.where(core, other, own), jnp.where(core, own, other)
        came_first = swap(first, FAR)
        came_second = lax.ppermute(second, "shard", onward)
        second = jnp.where(far, came_second, came_first)
        return jnp.concatenate(
            [jnp.where(core, second, came_first), jnp.where(core, came_first, second)]
        )

    def after(values):
        own, other = values[:8], values[8:]
        first, second = jnp.where(core, other, own), jnp.where(core, own, other)
        came_first = swap(jnp.where(far, first, second), FAR)
        came_second = lax.ppermute(second, "shard", backward)
        return jnp.concatenate(
            [jnp.where(core, came_second, came_first), jnp.where(core, came_first, came_second)]
        )

    value_before = before(value)
    key_before = before(key)
    mixed, lse = attend(me, query, key, value, key_before, value_before, place)
    mixed = mixed.reshape(SLOTS * ROWS, HEAD)
    block = 8 * ROWS

    def reduce_rows(other_part, own_part):
        came = swap_core(other_part.astype(bf16))
        return cube_scatter((own_part + came.astype(f32)).astype(bf16))

    branch = reduce_rows(
        jnp.dot(mixed[block:], out_w, preferred_element_type=f32),
        jnp.dot(mixed[:block], out_w, preferred_element_type=f32),
    )
    branch_scale = lax.rsqrt(jnp.mean(branch * branch, axis=-1, keepdims=True) + 1e-06)
    hidden_state = inputs.astype(f32) + branch * branch_scale * gains[2]
    state_low = hidden_state.astype(bf16)

    state = with_other(cube_gather(state_low))
    gate = [jnp.dot(part, gate_w, preferred_element_type=f32) for part in state]
    up = [jnp.dot(part, up_w, preferred_element_type=f32) for part in state]
    active = [(jax.nn.silu(g) * u).astype(bf16) for g, u in zip(gate, up)]
    mlp = reduce_rows(
        jnp.dot(active[1], down_w, preferred_element_type=f32),
        jnp.dot(active[0], down_w, preferred_element_type=f32),
    )
    mlp_scale = lax.rsqrt(jnp.mean(mlp * mlp, axis=-1, keepdims=True) + 1e-06)
    output = (hidden_state + mlp * mlp_scale * gains[3]).astype(bf16)

    cot = cotangent.astype(f32)
    mlp_gain_part = jnp.sum(cot * mlp * mlp_scale, axis=0)
    scaled = cot * gains[3]
    d_mlp = mlp_scale * scaled - mlp * mlp_scale**3 * jnp.mean(mlp * scaled, axis=-1, keepdims=True)
    d_mlp = with_other(cube_gather(d_mlp.astype(bf16)))
    d_gate, d_up = [], []
    for part, g, u in zip(d_mlp, gate, up):
        d_active = along_last(part, down_w)
        sigma = jax.nn.sigmoid(g)
        d_gate.append((d_active * u * sigma * (1.0 + g * (1.0 - sigma))).astype(bf16))
        d_up.append((d_active * g * sigma).astype(bf16))
    d_state = reduce_rows(
        along_last(d_gate[1], gate_w) + along_last(d_up[1], up_w),
        along_last(d_gate[0], gate_w) + along_last(d_up[0], up_w),
    )

    def over_tokens(left, right):
        return along_first(left[0], right[0]) + along_first(left[1], right[1])

    down_grad = over_tokens(active, d_mlp).reshape(2, hidden // 2, width)
    came = swap(pick(down_grad, 0, ~far).astype(bf16), FAR)
    down_part = (pick(down_grad, 0, far) + came.astype(f32)).astype(bf16)
    down_grad = ordered(down_part, swap_core(down_part), core, 0).reshape(hidden, width).astype(f32)

    def hidden_grad(grad, order):
        both = columns_grad(grad, order, core).reshape(2, 8, ROWS, 2, hidden // 2)
        return both.transpose(2, 3, 1, 0, 4).reshape(ROWS, -1).astype(f32)

    gate_grad = hidden_grad(over_tokens(state, d_gate), TRIPLE[0])
    up_grad = hidden_grad(over_tokens(state, d_up), TRIPLE[1])

    d_resid = cot + d_state
    attn_gain_part = jnp.sum(d_resid * branch * branch_scale, axis=0)
    scaled = d_resid * gains[2]
    d_branch = branch_scale * scaled - branch * branch_scale**3 * jnp.mean(
        branch * scaled, axis=-1, keepdims=True
    )
    d_branch = with_other(cube_gather(d_branch.astype(bf16)))
    d_mixed = jnp.concatenate([along_last(part, out_w).astype(bf16) for part in d_branch])
    d_query, d_key, d_value, d_key_before, d_value_before = attend_back(
        me, query, key, value, key_before, value_before, place, lse, d_mixed.reshape(shape)
    )
    flat = (SLOTS * ROWS, HEAD)
    d_value = (d_value + after(d_value_before).astype(f32)).reshape(flat)
    d_key = (d_key + after(d_key_before).astype(f32)).reshape(flat)
    d_query = rotated_back(d_query.reshape(flat))
    d_key = rotated_back(d_key)
    query_gain_part = jnp.sum(d_query * q_raw * q_scale, axis=0)
    key_gain_part = jnp.sum(d_key * k_raw * k_scale, axis=0)
    d_query = d_query * head_gain[0]
    d_key = d_key * head_gain[1]
    means = row_sums(d_query * q_raw, d_key * k_raw)
    d_query = d_query * q_scale - q_raw * q_scale**3 * means[0]
    d_key = d_key * k_scale - k_raw * k_scale**3 * means[1]
    d_qkv = jnp.concatenate([d_query, d_key, d_value], axis=1).astype(bf16)
    d_inputs = reduce_rows(along_last(d_qkv[block:], qkv_w), along_last(d_qkv[:block], qkv_w))
    input_grad = d_resid + d_inputs

    qkv_grad = over_tokens((x_own, x_other), (d_qkv[:block], d_qkv[block:]))

    def head_grad(grad, order):
        both = columns_grad(grad, order, core)
        return both.transpose(2, 0, 1, 3).reshape(ROWS, -1).astype(f32)

    query_grad = head_grad(qkv_grad[:, :HEAD], TRIPLE[0])
    key_grad = head_grad(qkv_grad[:, HEAD : 2 * HEAD], TRIPLE[1])
    value_grad = head_grad(qkv_grad[:, 2 * HEAD :], TRIPLE[2])

    out_grad = over_tokens((mixed[:block], mixed[block:]), d_branch)
    to_owner = [(s + 8, s) for s in range(8)] + [(16 + s, 24 + s) for s in range(8)]
    out_grad = (
        out_grad + lax.ppermute(out_grad.astype(bf16), ("grp", "shard"), to_owner).astype(f32)
    ).astype(bf16)
    to_core = [(s, 16 + s) for s in range(8)] + [(24 + s, 8 + s) for s in range(8)]
    out_came = lax.ppermute(out_grad, ("grp", "shard"), to_core)
    out_grad = jnp.where(core == far, out_grad, out_came).astype(f32)

    gain_part = jnp.stack([query_gain_part, key_gain_part])
    gain_part = gain_part + swap(gain_part, FAR)
    gain_came = swap_core(gain_part)
    head_grads = jnp.where(core == far, gain_part, gain_came)
    norm_part = jnp.stack([attn_gain_part, mlp_gain_part])
    norm_part = norm_part + swap_core(norm_part)
    norm_part = norm_part.reshape(2, 2, 2, 2, 2, ROWS)
    for bit, axis in ((FAR, 1), (Z, 2), (Y, 3), (X, 4)):
        flag = bit_of(bit)
        norm_part = pick(norm_part, axis, flag) + swap(pick(norm_part, axis, ~flag), bit)
    norm_grads = norm_part.reshape(2, ROWS)

    return (
        output,
        input_grad,
        query_grad,
        key_grad,
        value_grad,
        out_grad,
        head_grads[0],
        head_grads[1],
        norm_grads[0],
        gate_grad,
        up_grad,
        down_grad,
        norm_grads[1],
    )


def solution(mesh):
    in_cube = mesh.shape["grp"] == 2 and mesh.shape["shard"] == 16
    placed = (
        P(("grp", "shard"), None),
        P(("grp", "shard")),
        P(("grp", "shard"), None),
        P("shard", None),
        P("shard", None),
        P("shard", None),
        P("shard", None),
        P("shard"),
        P("shard"),
        P("shard"),
        P("shard", None),
        P("shard", None),
        P("shard", None),
        P("shard"),
    )
    return jax.shard_map(
        local_cube if in_cube else local_general,
        mesh=mesh,
        in_specs=placed,
        out_specs=(
            P(("grp", "shard"), None),
            P(("grp", "shard"), None),
            P("shard", None),
            P("shard", None),
            P("shard", None),
            P("shard", None),
            P("shard"),
            P("shard"),
            P("shard"),
            P("shard", None),
            P("shard", None),
            P("shard", None),
            P("shard"),
        ),
        check_vma=False,
    )
```

```python
import functools
import math

import jax
import jax.numpy as jnp
from jax import lax
from jax.experimental import pallas as pl
from jax.experimental.pallas import tpu as pltpu
from jax.sharding import PartitionSpec as P

HEADS = 16
HEAD = 128
DOC_LEN = 1024


def from_behind(value, axis, steps):
    count = lax.axis_size(axis)
    leading, last = (max(0, -steps), min(count, count - steps))
    return lax.ppermute(value, axis, [(source, source + steps) for source in range(leading, last)])


def norm_rows(values, scales):
    return values * lax.rsqrt(jnp.mean(values * values, axis=-1, keepdims=True) + 1e-06) * scales


def rotate(values, cosines, sines):
    row_count = values.shape[0]
    middle = HEAD // 2
    shaped = values.reshape(row_count, HEADS, HEAD)
    first_half = shaped[..., :middle]
    second_half = shaped[..., middle:]
    turned = jnp.concatenate(
        [first_half * cosines - second_half * sines, second_half * cosines + first_half * sines],
        axis=-1,
    )
    return turned.reshape(row_count, HEADS * HEAD)


def activate(gate_in, up_in):
    return jax.nn.silu(gate_in) * up_in


def along_last(left, right):
    return lax.dot_general(
        left, right, (((1,), (1,)), ((), ())), preferred_element_type=jnp.float32
    )


def along_first(left, right):
    return lax.dot_general(
        left, right, (((0,), (0,)), ((), ())), preferred_element_type=jnp.float32
    )


def reduce_three(first_term, second_term, third_term):
    return (
        lax.psum_scatter(first_term, "shard", scatter_dimension=0, tiled=True),
        lax.psum_scatter(second_term, "shard", scatter_dimension=0, tiled=True),
        lax.psum_scatter(third_term, "shard", scatter_dimension=0, tiled=True),
    )


def local_general(
    inputs,
    positions,
    cotangent,
    w_query,
    w_key,
    w_value,
    w_out,
    query_gain,
    key_gain,
    attn_gain,
    w_gate,
    w_up,
    w_down,
    mlp_gain,
):
    row_count, feature_width = inputs.shape
    reach_back = (DOC_LEN - 2) // row_count + 1
    span_rows = min(row_count, 512)
    key_rows = span_rows + reach_back * row_count
    scaling = 1.0 / math.sqrt(HEAD)
    middle = HEAD // 2
    frequency = jnp.power(500000.0, -2.0 * jnp.arange(middle).astype(jnp.float32) / HEAD)
    angles = positions.astype(jnp.float32)[:, None] * frequency[None, :]
    cosines = jnp.cos(angles)[:, None, :]
    sines = jnp.sin(angles)[:, None, :]
    pieces = (
        lax.all_gather(w_query, "shard", axis=0, tiled=True),
        lax.all_gather(w_key, "shard", axis=0, tiled=True),
        lax.all_gather(w_value, "shard", axis=0, tiled=True),
        lax.all_gather(w_out, "shard", axis=0, tiled=True),
        lax.all_gather(query_gain, "shard", axis=0, tiled=True),
        lax.all_gather(key_gain, "shard", axis=0, tiled=True),
        lax.all_gather(attn_gain, "shard", axis=0, tiled=True),
        lax.all_gather(mlp_gain, "shard", axis=0, tiled=True),
    )
    columns_in = inputs
    acc_query = jnp.dot(columns_in, pieces[0], preferred_element_type=jnp.float32)
    acc_key = jnp.dot(columns_in, pieces[1], preferred_element_type=jnp.float32)
    acc_value = jnp.dot(columns_in, pieces[2], preferred_element_type=jnp.float32)
    out_full = pieces[3]
    gain_block = jnp.stack([pieces[4], pieces[5], pieces[6], pieces[7]]).astype(jnp.float32)
    gain_table = gain_block
    q_raw, k_raw, v_raw, out_full, gain_table = (
        acc_query,
        acc_key,
        acc_value,
        out_full,
        gain_table,
    )

    def prepare(query_in, key_in, query_scale, key_scale):
        return (
            rotate(norm_rows(query_in, query_scale), cosines, sines),
            rotate(norm_rows(key_in, key_scale), cosines, sines),
        )

    rotated, prepare_pull = jax.vjp(prepare, q_raw, k_raw, gain_table[0], gain_table[1])
    query_low = rotated[0].astype(jnp.bfloat16)
    key_value = jnp.stack([rotated[1].astype(jnp.bfloat16), v_raw.astype(jnp.bfloat16)])
    earlier = [
        from_behind(key_value, ("grp", "shard"), distance_back)
        for distance_back in range(reach_back, 0, -1)
    ]
    key_window = jnp.concatenate(earlier + [key_value], axis=1)
    distance = (
        jnp.arange(span_rows)[:, None] + reach_back * row_count - jnp.arange(key_rows)[None, :]
    )

    def block_scores(block_start):
        query_block = query_low.reshape(span_rows, HEADS, HEAD)
        key_block = key_window[0, block_start : block_start + key_rows].reshape(
            key_rows, HEADS, HEAD
        )
        value_block = key_window[1, block_start : block_start + key_rows].reshape(
            key_rows, HEADS, HEAD
        )
        visible = (distance >= 0) & (distance <= positions[:, None])
        scores = (
            jnp.einsum("qhd,khd->hqk", query_block, key_block, preferred_element_type=jnp.float32)
            * scaling
        )
        return (query_block, key_block, value_block, visible, scores)

    block_start = 0
    query_block, key_block, value_block, visible, scores = block_scores(block_start)
    masked = jnp.where(visible[None], scores, -jnp.inf)
    top_score = jnp.max(masked, axis=-1, keepdims=True)
    expo = jnp.exp(masked - top_score)
    totals = jnp.sum(expo, axis=-1, keepdims=True)
    probs_low = (expo / totals).astype(jnp.bfloat16)
    lse_parts = [top_score + jnp.log(totals)]
    mixed = jnp.einsum("hqk,khd->qhd", probs_low, value_block, preferred_element_type=jnp.float32)
    mixed_parts = mixed.reshape(span_rows, feature_width)
    mixed_low = mixed_parts.astype(jnp.bfloat16)
    branch = jnp.dot(mixed_low, out_full, preferred_element_type=jnp.float32)
    branch_normed, attn_pull = jax.vjp(norm_rows, branch, gain_table[2])
    hidden_state = inputs.astype(jnp.float32) + branch_normed
    state_low = hidden_state.astype(jnp.bfloat16)
    pieces = (
        lax.all_gather(w_gate, "shard", axis=0, tiled=True),
        lax.all_gather(w_up, "shard", axis=0, tiled=True),
    )
    columns_in = state_low
    gate_val = jnp.dot(columns_in, pieces[0], preferred_element_type=jnp.float32)
    up_val = jnp.dot(columns_in, pieces[1], preferred_element_type=jnp.float32)
    activated, act_pull = jax.vjp(activate, gate_val, up_val)
    activated_low = activated.astype(jnp.bfloat16)
    columns_in = activated_low
    mlp_out = jnp.dot(
        columns_in,
        lax.all_gather(w_down, "shard", axis=0, tiled=True),
        preferred_element_type=jnp.float32,
    )
    mlp_normed, mlp_pull = jax.vjp(norm_rows, mlp_out, gain_table[3])
    output = (hidden_state + mlp_normed).astype(jnp.bfloat16)
    cot_float = cotangent.astype(jnp.float32)
    d_mlp, d_mlp_gain = mlp_pull(cot_float)
    d_mlp_low = d_mlp.astype(jnp.bfloat16)
    d_hidden = along_last(d_mlp_low, lax.all_gather(w_down, "shard", axis=0, tiled=True))
    d_gate, d_up = act_pull(d_hidden)
    d_gate_low = d_gate.astype(jnp.bfloat16)
    d_up_low = d_up.astype(jnp.bfloat16)
    pieces = lax.all_gather((w_gate, w_up), "shard", axis=0, tiled=True)
    d_state = along_last(d_gate_low, pieces[0]) + along_last(d_up_low, pieces[1])
    d_resid = cot_float + d_state
    gate_term = along_first(state_low, d_gate_low)
    up_term = along_first(state_low, d_up_low)
    down_term = along_first(activated_low, d_mlp_low)
    ffn_sums = reduce_three(gate_term, up_term, down_term)
    d_branch, d_attn_gain = attn_pull(d_resid)
    d_branch_low = d_branch.astype(jnp.bfloat16)
    d_mixed_low = along_last(
        d_branch_low, lax.all_gather(w_out, "shard", axis=0, tiled=True)
    ).astype(jnp.bfloat16)
    dq_parts = []
    grad_window = jnp.zeros((2, (reach_back + 1) * row_count, feature_width), jnp.float32)
    for block_number, block_start in enumerate(range(0, row_count, span_rows)):
        query_block, key_block, value_block, visible, scores = block_scores(block_start)
        probs = jnp.where(visible[None], jnp.exp(scores - lse_parts[block_number]), 0.0)
        grad_block = d_mixed_low.reshape(span_rows, HEADS, HEAD)
        d_probs = jnp.einsum(
            "qhd,khd->hqk", grad_block, value_block, preferred_element_type=jnp.float32
        )
        inner = jnp.sum(probs * d_probs, axis=-1, keepdims=True)
        d_scores = (probs * (d_probs - inner) * scaling).astype(jnp.bfloat16)
        dq_block = jnp.einsum(
            "hqk,khd->qhd", d_scores, key_block, preferred_element_type=jnp.float32
        )
        dq_parts.append(dq_block.reshape(span_rows, feature_width))
        d_keys = jnp.einsum(
            "hqk,qhd->khd", d_scores, query_block, preferred_element_type=jnp.float32
        ).reshape(key_rows, feature_width)
        d_values = jnp.einsum(
            "hqk,qhd->khd",
            probs.astype(jnp.bfloat16),
            grad_block,
            preferred_element_type=jnp.float32,
        ).reshape(key_rows, feature_width)
        grad_window = grad_window.at[:, block_start : block_start + key_rows].add(
            jnp.stack([d_keys, d_values])
        )
    own_grads = grad_window[:, reach_back * row_count :]
    for distance_back in range(1, reach_back + 1):
        lower_row = (reach_back - distance_back) * row_count
        own_grads = own_grads + from_behind(
            grad_window[:, lower_row : lower_row + row_count].astype(jnp.bfloat16),
            ("grp", "shard"),
            -distance_back,
        ).astype(jnp.float32)
    d_query_raw, d_key_raw, d_query_gain, d_key_gain = prepare_pull((dq_parts[0], own_grads[0]))
    d_query_low = d_query_raw.astype(jnp.bfloat16)
    d_key_low = d_key_raw.astype(jnp.bfloat16)
    d_value_low = own_grads[1].astype(jnp.bfloat16)
    pieces = lax.all_gather((w_query, w_key, w_value), "shard", axis=0, tiled=True)
    d_inputs = (
        along_last(d_query_low, pieces[0])
        + along_last(d_key_low, pieces[1])
        + along_last(d_value_low, pieces[2])
    )
    input_grad = d_resid + d_inputs
    qkv_term = along_first(inputs, jnp.concatenate([d_query_low, d_key_low, d_value_low], axis=1))
    out_term = along_first(mixed_low, d_branch_low)
    gain_term = jnp.stack([d_query_gain, d_key_gain, d_attn_gain, d_mlp_gain], axis=1)
    attn_sums = reduce_three(qkv_term, out_term, gain_term)
    gate_sum, up_sum, down_sum, qkv_sum, out_sum, gain_sum = (
        lax.psum(ffn_sums[0].astype(jnp.bfloat16), "grp").astype(jnp.float32),
        lax.psum(ffn_sums[1].astype(jnp.bfloat16), "grp").astype(jnp.float32),
        lax.psum(ffn_sums[2].astype(jnp.bfloat16), "grp").astype(jnp.float32),
        lax.psum(attn_sums[0].astype(jnp.bfloat16), "grp").astype(jnp.float32),
        lax.psum(attn_sums[1].astype(jnp.bfloat16), "grp").astype(jnp.float32),
        lax.psum(attn_sums[2].astype(jnp.bfloat16), "grp").astype(jnp.float32),
    )
    return (
        output,
        input_grad,
        qkv_sum[:, :feature_width],
        qkv_sum[:, feature_width : 2 * feature_width],
        qkv_sum[:, 2 * feature_width :],
        out_sum,
        gain_sum[:, 0],
        gain_sum[:, 1],
        gain_sum[:, 2],
        gate_sum,
        up_sum,
        down_sum,
        gain_sum[:, 3],
    )


LINE = 4
SQUARE = 4
X, Y, Z, FAR = 1, 2, 4, 8
ROWS = 128
BLOCKS = 16
WINDOW = 1152
SHARE = 256
SCALING = 1.0 / math.sqrt(HEAD)
SQUARES = [[SQUARE * z + r for r in range(SQUARE)] for z in range(LINE)]


def swap(value, bit):
    return lax.ppermute(value, "shard", [(source, source ^ bit) for source in range(BLOCKS)])


def swap_core(value):
    return lax.ppermute(value, "grp", [(0, 1), (1, 0)])


def along(bit):
    return lambda value: swap(value, bit)


def line_place():
    return lax.axis_index("shard") // SQUARE


def square_place():
    return lax.axis_index("shard") % SQUARE


def line_move(pairs):
    pairs = [(SQUARE * z + r, SQUARE * to + r) for z, to in pairs for r in range(SQUARE)]
    return lambda value: lax.ppermute(value, "shard", pairs)


RIGHT, LEFT = ((0, 1), (1, 2), (2, 3)), ((3, 2), (2, 1), (1, 0))


def line_turn(distance):
    pairs = [(s, (s + SQUARE * distance) % BLOCKS) for s in range(BLOCKS)]
    return lambda value: lax.ppermute(value, "shard", pairs)


def hold(values, *later):
    return lax.optimization_barrier((values, later))[0]


def together(*values):
    return lax.optimization_barrier(values)


def run(*tracks):
    live, results = {}, {}

    def advance(name, generator, came):
        try:
            live[name] = (generator, generator.send(came))
        except StopIteration as end:
            live.pop(name, None)
            results[name] = end.value

    for name, generator in enumerate(tracks):
        advance(name, generator, None)
    while live:
        requests = [request for _, asked in live.values() for request in asked]
        given = lax.optimization_barrier(tuple(value for value, _ in requests))
        came = [move(value) for value, (_, move) in zip(given, requests)]
        came = list(lax.optimization_barrier(tuple(came)))
        for name, (generator, asked) in list(live.items()):
            mine, came = came[: len(asked)], came[len(asked) :]
            advance(name, generator, mine)
    return [results[name] for name in range(len(tracks))]


def alone(track):
    return run(track)[0]


def gather_first(value):
    right, left = yield [(value, line_move(RIGHT)), (value, line_move(LEFT))]
    return value, right, left


def gather_second(value, right, left):
    place = line_place()
    further = jnp.where(place == 1, right, left)
    rights, lefts, further = yield [
        (right, line_move(RIGHT[1:])),
        (left, line_move(LEFT[1:])),
        (further, line_move(((1, 3), (2, 0)))),
    ]
    rows, width = value.shape
    shape = jax.ShapeDtypeStruct((LINE * rows, width), value.dtype)
    arrays = [value, right, left, rights, lefts, further]
    return whole_call(gather_kernel, [shape], [place.astype(jnp.int32).reshape(1)], arrays)


def gather_kernel(place_ref, own_ref, right_ref, left_ref, rights_ref, lefts_ref, further_ref, out_ref):
    place, rows = place_ref[0], own_ref.shape[0]

    def put(slot, condition, ref):
        @pl.when(condition)
        def _():
            out_ref[slot * rows : (slot + 1) * rows, :] = ref[...]

    out_ref[:rows, :] = own_ref[...]
    put(1, place >= 1, right_ref)
    put(1, place == 0, further_ref)
    put(2, place >= 2, rights_ref)
    put(2, place < 2, lefts_ref)
    put(3, place == 3, further_ref)
    put(3, place < 3, left_ref)


def gather_line(value):
    came = yield from gather_first(value)
    return (yield from gather_second(*came))


def join_kernel(own_ref, other_ref, out_ref):
    rows = own_ref.shape[0]
    out_ref[:rows, :] = own_ref[...]
    out_ref[rows:, :] = other_ref[...]


def both_cores(own):
    shape = jax.ShapeDtypeStruct((2 * own.shape[0], own.shape[1]), own.dtype)
    return whole_call(join_kernel, [shape], [], [own, swap_core(own)])


def scatter_first(total):
    parts = total.reshape(LINE, -1, total.shape[-1])
    further = jnp.where(line_place() == 0, parts[1], parts[3])
    return (
        yield [
            (parts[2], line_move(RIGHT[:2])),
            (parts[2], line_move(LEFT[:2])),
            (further, line_move(((0, 2), (3, 1)))),
        ]
    )


def scatter_second(total, right, left, further):
    parts = total.reshape(LINE, -1, total.shape[-1])
    place, nothing = line_place(), jnp.zeros((), total.dtype)
    right, left = yield [
        (add_low(parts[3], right, jnp.where(place == 2, further, nothing)), line_move(RIGHT)),
        (add_low(parts[1], left, jnp.where(place == 1, further, nothing)), line_move(LEFT)),
    ]
    return add_wide(parts[0], right, left)


def scatter_line(total):
    came = yield from scatter_first(total)
    return (yield from scatter_second(total, *came))


def add_wide(*values):
    return sum(value.astype(jnp.float32) for value in values)


def add_low(*values):
    return add_wide(*values).astype(jnp.bfloat16)


def turn_line(block):
    place = line_place()
    came = yield [
        (lax.dynamic_index_in_dim(block, (place + k) % LINE, 0, keepdims=False), line_turn(k))
        for k in range(1, LINE)
    ]
    own = lax.dynamic_index_in_dim(block, place, 0, keepdims=False)
    return jnp.stack([own, *came])


def to_slots(value):
    place = line_place()
    return jnp.stack(
        [lax.dynamic_index_in_dim(value, (place - k) % LINE, 0, keepdims=False) for k in range(LINE)]
    )


def in_two(value):
    return jnp.split(value, 2, axis=-1)


def square_first(value):
    first, second = in_two(value)
    return swap(first, X), swap(second, Y)


def square_track(value):
    came = yield [(part, along(bit)) for part, bit in zip(in_two(value), (X, Y))]
    return tuple(came)


def second_kernel(own_ref, first_ref, second_ref, to_first_ref, to_second_ref):
    half = own_ref.shape[-1] // 2
    to_first_ref[0] = own_ref[..., :half]
    to_first_ref[1] = first_ref[...]
    to_second_ref[0] = own_ref[..., half:]
    to_second_ref[1] = second_ref[...]


def second_parts(value, came):
    shape = jax.ShapeDtypeStruct((2,) + came[0].shape, value.dtype)
    return whole_call(second_kernel, [shape] * 2, [], [value, *came])


def square_second(value, came):
    first, second = second_parts(value, came)
    return swap(first, Y), swap(second, X)


def second_track(value, came):
    first, second = second_parts(value, came)
    later = yield [(first, along(Y)), (second, along(X))]
    return tuple(later)


def square_kernel(index_ref, own_ref, first_ref, second_ref, firsts_ref, seconds_ref, out_ref):
    half, count = own_ref.shape[-1] // 2, own_ref.shape[0]
    firsts = (own_ref, first_ref, firsts_ref.at[0], firsts_ref.at[1])
    seconds = (own_ref, seconds_ref.at[0], second_ref, seconds_ref.at[1])
    for corner in range(SQUARE):
        for number in range(count):
            target = index_ref[corner * count + number]
            out_ref[target, :, :half] = firsts[corner][number, :, :half]
            lanes = slice(half, None) if corner == 0 else slice(None)
            out_ref[target, :, half:] = seconds[corner][number, :, lanes]


def square_join(index, value, came, later):
    count, rows, width = value.shape
    shape = jax.ShapeDtypeStruct((SQUARE * count, rows, width), value.dtype)
    return whole_call(square_kernel, [shape], [index], [value, *came, *later])


def split_kernel(index_ref, grad_ref, kept_first, sent_first, kept_second, sent_second):
    half, count = grad_ref.shape[-1] // 2, kept_first.shape[1]
    firsts = ((kept_first, 0), (kept_first, 1), (sent_first, 0), (sent_first, 1))
    seconds = ((kept_second, 0), (sent_second, 0), (kept_second, 1), (sent_second, 1))
    for corner in range(SQUARE):
        for number in range(count):
            block = grad_ref[index_ref[corner * count + number]]
            for (target, place), lanes in (
                (firsts[corner], slice(0, half)),
                (seconds[corner], slice(half, 2 * half)),
            ):
                target[place, number] = block[:, lanes]


def sum_split(index, grad):
    blocks, rows, width = grad.shape
    shape = jax.ShapeDtypeStruct((2, blocks // SQUARE, rows, width // 2), grad.dtype)
    return whole_call(split_kernel, [shape] * 4, [index], [grad])


def sum_first(split):
    return swap(split[1], Y), swap(split[3], X)


def low_sum(first, second):
    return (first.astype(jnp.float32) + second.astype(jnp.float32)).astype(jnp.bfloat16)


def add_kernel(kept_first, came_first, kept_second, came_second, *targets):
    for number, (kept, came) in enumerate(((kept_first, came_first), (kept_second, came_second))):
        for place in range(2):
            for block in range(kept.shape[1]):
                targets[2 * number + place][block] = low_sum(kept[place, block], came[place, block])


def sum_second(split, came):
    shape = jax.ShapeDtypeStruct(came[0].shape[1:], jnp.bfloat16)
    arrays = [split[0], came[0], split[2], came[1]]
    first, to_first, second, to_second = whole_call(add_kernel, [shape] * 4, [], arrays)
    return (first, second), (swap(to_first, X), swap(to_second, Y))


def end_kernel(first_ref, came_first, second_ref, came_second, out_ref):
    half = first_ref.shape[-1]
    for block in range(out_ref.shape[0]):
        out_ref[block, :, :half] = low_sum(first_ref[block], came_first[block])
        out_ref[block, :, half:] = low_sum(second_ref[block], came_second[block])


def sum_end(kept, came):
    count, rows, half = kept[0].shape
    shape = jax.ShapeDtypeStruct((count, rows, 2 * half), jnp.bfloat16)
    return whole_call(end_kernel, [shape], [], [kept[0], came[0], kept[1], came[1]])


def in_vmem(count, scalars=1):
    return [pl.BlockSpec(memory_space=pltpu.SMEM)] * scalars + [
        pl.BlockSpec(memory_space=pltpu.VMEM)
    ] * count


def whole_call(kernel, shapes, scalars, arrays, scratch=(), megabytes=40, cost=None):
    specs = [pl.BlockSpec(memory_space=pltpu.VMEM)] * len(shapes)
    single = len(shapes) == 1
    size = sum(array.size * array.dtype.itemsize for array in arrays)
    return pl.pallas_call(
        kernel,
        out_shape=shapes[0] if single else shapes,
        in_specs=in_vmem(len(arrays), len(scalars)),
        out_specs=specs[0] if single else specs,
        scratch_shapes=list(scratch),
        compiler_params=pltpu.CompilerParams(vmem_limit_bytes=megabytes * 2**20),
        cost_estimate=cost or pl.CostEstimate(flops=0, bytes_accessed=2 * size, transcendentals=0),
    )(*scalars, *arrays)


def column_start(columns, parts, place, part, core):
    return pl.multiple_of(place * (columns // LINE) + part * 2 * SHARE + core * SHARE, SHARE)


def pick_kernel(parts, core_ref, *refs):
    *weight_refs, block_ref = refs
    columns = weight_refs[0].shape[1]
    for place in range(LINE):
        for number, weight_ref in enumerate(weight_refs):
            for part in range(parts):
                start = column_start(columns, parts, place, part, core_ref[0])
                lane = (number * parts + part) * SHARE
                block_ref[place, :ROWS, lane : lane + SHARE] = weight_ref[:, pl.ds(start, SHARE)]


def pick_more_kernel(parts, core_ref, *refs):
    *weight_refs, more_ref, block_ref = refs
    pick_kernel(parts, core_ref, *weight_refs, block_ref)
    for place in range(LINE):
        for lane in range(0, block_ref.shape[2], HEAD):
            block_ref[place, ROWS:, lane : lane + HEAD] = more_ref[...]


def spread_kernel(parts, core_ref, mine_ref, came_ref, place_ref, *grad_refs):
    columns = grad_refs[0].shape[1]
    for slot in range(LINE):
        for number, grad_ref in enumerate(grad_refs):
            for part in range(parts):
                lane = (number * parts + part) * SHARE
                for source, core in ((mine_ref, core_ref[0]), (came_ref, 1 - core_ref[0])):
                    start = column_start(columns, parts, place_ref[slot], part, core)
                    grad_ref[:, pl.ds(start, SHARE)] = source[slot, :, lane : lane + SHARE].astype(
                        jnp.float32
                    )


def spread_scalars_kernel(parts, core_ref, place_ref, mine_ref, came_ref, *grad_refs):
    spread_kernel(parts, core_ref, mine_ref, came_ref, place_ref, *grad_refs)


def pick_columns(core_ref, weights, parts, more=None):
    rows, columns = weights[0].shape
    extra = [] if more is None else [more]
    rows += sum(array.shape[0] for array in extra)
    shape = jax.ShapeDtypeStruct((LINE, rows, len(weights) * columns // 8), jnp.bfloat16)
    kernel = functools.partial(pick_more_kernel if extra else pick_kernel, parts)
    return whole_call(kernel, [shape], [core_ref], [*weights, *extra])


def spread_columns(core_ref, place_ref, mine, came, count, parts):
    shape = jax.ShapeDtypeStruct((mine.shape[1], 8 * mine.shape[2] // count), jnp.float32)
    kernel = functools.partial(spread_scalars_kernel, parts)
    return whole_call(kernel, [shape] * count, [core_ref, place_ref], [mine, came])


def head_lanes(head):
    return slice(head * HEAD, (head + 1) * HEAD)


def halo_slots(place):
    return lax.rem(place + 2, LINE), lax.rem(place + 1, LINE)


def pack_kernel(core_ref, place_ref, q_ref, k_ref, v_ref, out_ref):
    for group in range(2):
        part = core_ref[0] if group == 0 else 1 - core_ref[0]
        for head in range(2):
            lanes, target = head_lanes(head), 2 * group + head
            for slot in range(LINE):
                for number, ref in enumerate((q_ref, k_ref, v_ref)):
                    out_ref[target, LINE * number + slot] = ref[part, slot, :, lanes]
            for number, slot in enumerate(halo_slots(place_ref[0])):
                out_ref[target, 12 + number] = k_ref[core_ref[0], slot, :, lanes]
                out_ref[target, 14 + number] = v_ref[core_ref[0], slot, :, lanes]


def unpack_kernel(core_ref, came_ref, out_ref):
    for group in range(2):
        part = core_ref[0] if group == 0 else 1 - core_ref[0]
        for head in range(2):
            for slot in range(LINE):
                out_ref[part, slot, :, head_lanes(head)] = came_ref[2 * group + head, slot]


def pack_grad_kernel(core_ref, grad_ref, out_ref):
    for group in range(2):
        part = core_ref[0] if group == 0 else 1 - core_ref[0]
        for head in range(2):
            for slot in range(LINE):
                out_ref[2 * group + head, slot] = grad_ref[part, slot, :, head_lanes(head)]


def unpack_grad_kernel(core_ref, place_ref, came_ref, dq_ref, dk_ref, dv_ref):
    for group in range(2):
        part = core_ref[0] if group == 0 else 1 - core_ref[0]
        for head in range(2):
            for slot in range(LINE):
                for number, ref in enumerate((dq_ref, dk_ref, dv_ref)):
                    ref[part, slot, :, head_lanes(head)] = came_ref[
                        2 * group + head, LINE * number + slot
                    ].astype(jnp.float32)
    for head in range(2):
        for number, slot in enumerate(halo_slots(place_ref[0])):
            dk_ref[core_ref[0], slot, :, head_lanes(head)] += came_ref[2 + head, 12 + number].astype(
                jnp.float32
            )
            dv_ref[core_ref[0], slot, :, head_lanes(head)] += came_ref[2 + head, 14 + number].astype(
                jnp.float32
            )


def visible_of(place):
    row = lax.broadcasted_iota(jnp.int32, (ROWS, WINDOW), 0)
    column = lax.broadcasted_iota(jnp.int32, (ROWS, WINDOW), 1)
    distance = row - column + (WINDOW - ROWS)
    return (distance >= 0) & (distance <= place)


def dot_last(left, right):
    return lax.dot_general(
        left, right, (((1,), (1,)), ((), ())), preferred_element_type=jnp.float32
    )


def stream_row(place, source, slot):
    block = lax.rem(place - slot + LINE, LINE) * SQUARE + source
    return block, pl.multiple_of(block * ROWS, ROWS)


def rows_at(start):
    return pl.ds(pl.multiple_of(start, ROWS), ROWS)


def fill(place, message_ref, keys, values):
    for source in range(SQUARE):
        for slot in range(LINE):
            _, start = stream_row(place, source, slot)
            keys[rows_at(start + DOC_LEN), :] = message_ref[source, LINE + slot]
            values[rows_at(start + DOC_LEN), :] = message_ref[source, 2 * LINE + slot]
        for number in range(2):
            start = (number * SQUARE + source) * ROWS
            keys[start : start + ROWS, :] = message_ref[source, 12 + number]
            values[start : start + ROWS, :] = message_ref[source, 14 + number]


def attend_kernel(place_ref, message_ref, pos_ref, o_ref, lse_ref, keys, values):
    place = place_ref[0]
    fill(place, message_ref, keys, values)

    def step(number, carry):
        source, slot = number // LINE, number % LINE
        block, start = stream_row(place, source, slot)
        rows = pl.ds(start, WINDOW)
        scores = dot_last(message_ref[source, slot], keys[rows, :]) * SCALING
        masked = jnp.where(visible_of(pos_ref[block]), scores, -jnp.inf)
        top = jnp.max(masked, axis=-1, keepdims=True)
        expo = jnp.exp(masked - top)
        total = jnp.sum(expo, axis=-1, keepdims=True)
        probs = (expo / total).astype(jnp.bfloat16)
        mixed = jnp.dot(probs, values[rows, :], preferred_element_type=jnp.float32)
        o_ref[source, slot] = mixed.astype(jnp.bfloat16)
        lse_ref[number] = top + jnp.log(total)
        return carry

    lax.fori_loop(0, BLOCKS, step, 0)


def attend_back_kernel(
    place_ref, message_ref, pos_ref, lse_ref, do_ref, out_ref, keys, values, d_keys, d_values
):
    place = place_ref[0]
    fill(place, message_ref, keys, values)
    d_keys[...] = jnp.zeros_like(d_keys)
    d_values[...] = jnp.zeros_like(d_values)

    def step(number, carry):
        source, slot = number // LINE, number % LINE
        block, start = stream_row(place, source, slot)
        rows = pl.ds(start, WINDOW)
        query, grad = message_ref[source, slot], do_ref[source, slot]
        key, value = keys[rows, :], values[rows, :]
        scores = dot_last(query, key) * SCALING
        probs = jnp.where(visible_of(pos_ref[block]), jnp.exp(scores - lse_ref[number]), 0.0)
        d_probs = dot_last(grad, value)
        inner = jnp.sum(probs * d_probs, axis=-1, keepdims=True)
        d_scores = (probs * (d_probs - inner) * SCALING).astype(jnp.bfloat16)
        d_query = jnp.dot(d_scores, key, preferred_element_type=jnp.float32)
        out_ref[source, slot] = d_query.astype(jnp.bfloat16)
        d_keys[rows, :] += along_first(d_scores, query)
        d_values[rows, :] += along_first(probs.astype(jnp.bfloat16), grad)
        return carry

    lax.fori_loop(0, BLOCKS, step, 0)
    for source in range(SQUARE):
        for slot in range(LINE):
            _, start = stream_row(place, source, slot)
            out_ref[source, LINE + slot] = d_keys[rows_at(start + DOC_LEN), :].astype(jnp.bfloat16)
            out_ref[source, 2 * LINE + slot] = d_values[rows_at(start + DOC_LEN), :].astype(jnp.bfloat16)
        for number in range(2):
            start = (number * SQUARE + source) * ROWS
            out_ref[source, 12 + number] = d_keys[start : start + ROWS, :].astype(jnp.bfloat16)
            out_ref[source, 14 + number] = d_values[start : start + ROWS, :].astype(jnp.bfloat16)


KEPT = [pltpu.VMEM((3 * DOC_LEN, HEAD), jnp.bfloat16)] * 2
SUMMED = [pltpu.VMEM((3 * DOC_LEN, HEAD), jnp.float32)] * 2


def attend(place_ref, message, positions):
    shapes = [
        jax.ShapeDtypeStruct((SQUARE, LINE, ROWS, HEAD), jnp.bfloat16),
        jax.ShapeDtypeStruct((BLOCKS, ROWS, 1), jnp.float32),
    ]
    return whole_call(attend_kernel, shapes, [place_ref], [message, positions], KEPT)


def attend_back(place_ref, message, positions, lse, grad):
    shape = jax.ShapeDtypeStruct(message.shape, jnp.bfloat16)
    arrays = [message, positions, lse, grad]
    return whole_call(attend_back_kernel, [shape], [place_ref], arrays, KEPT + SUMMED)


def turn_square(message):
    return lax.all_to_all(message, "shard", 0, 0, tiled=True, axis_index_groups=SQUARES)


def local_line(
    inputs,
    positions,
    cotangent,
    w_query,
    w_key,
    w_value,
    w_out,
    query_gain,
    key_gain,
    attn_gain,
    w_gate,
    w_up,
    w_down,
    mlp_gain,
):
    bf16, f32 = jnp.bfloat16, jnp.float32
    width = inputs.shape[1]
    core_index = lax.axis_index("grp")
    shard_index = lax.axis_index("shard")
    core = core_index == 1
    place, corner = line_place(), square_place()
    core_ref = core_index.astype(jnp.int32).reshape(1)
    place_ref = place.astype(jnp.int32).reshape(1)
    slots = jnp.arange(LINE, dtype=jnp.int32)
    slot_places = (place - slots) % LINE
    hidden = w_down.shape[0] * 2
    tokens = 2 * LINE * ROWS
    part_tokens = tokens // 2
    heads = 2 * HEAD
    from_slots = (slot_places[None, :] * SQUARE + (corner ^ slots)[:, None]).reshape(-1)
    from_order = (slots[None, :] * SQUARE + (corner ^ slots)[:, None]).reshape(-1)
    from_corner = corner ^ slots

    def region(function, *given):
        shapes = jax.eval_shape(function, *given)
        empty = lambda *given: jax.tree.map(lambda leaf: jnp.zeros(leaf.shape, leaf.dtype), shapes)
        return lax.cond(positions[0] >= 0, function, empty, *given)

    def across_cores(left, right, product):
        other = product(left[part_tokens:], right).astype(bf16)
        own = product(left[:part_tokens], right)
        return add_low(own, swap_core(other))

    def dot(left, right):
        return jnp.dot(left, right, preferred_element_type=f32)

    small = jnp.concatenate(
        [
            jnp.stack([query_gain, key_gain, attn_gain, mlp_gain]),
            jnp.stack([positions // 32, positions % 32]).astype(bf16),
            jnp.zeros((10, ROWS), bf16),
        ]
    )
    down_own = lax.dynamic_index_in_dim(w_down.reshape(2, 1, hidden // SQUARE, width), core_index, 0, keepdims=False)
    out_own = w_out[None]
    head_block, out_came, down_came = run(
        turn_line(pick_columns(core_ref, (w_query, w_key, w_value), 1, small)),
        square_track(out_own),
        square_track(down_own),
    )
    x_came, head_came = run(gather_first(inputs), square_track(head_block))
    x_own, head_later = run(gather_second(*x_came), second_track(head_block, head_came))
    out_own, down_own = hold((out_own, down_own), x_own)
    out_later = square_second(out_own, out_came)
    down_later = square_second(down_own, down_came)
    x_all = both_cores(x_own)
    head_block = square_join(from_slots, head_block, head_came, head_later)
    qkv_w = head_block[:, :ROWS].reshape(width, 3 * heads)
    gains = head_block[:, ROWS : ROWS + 4, :HEAD].astype(f32)
    first_head = place * SQUARE + core_index * 2
    head_gain = lax.dynamic_slice_in_dim(gains, first_head, 2, 0)[:, :2].transpose(1, 0, 2).reshape(2, heads)
    gains = gains.transpose(1, 0, 2).reshape(4, width)
    stream = head_block[:, ROWS + 4 : ROWS + 6, :HEAD].astype(jnp.int32)
    stream = stream[:, 0] * 32 + stream[:, 1]
    stream_other = swap_core(stream)
    query_places = jnp.where((corner >= 2) == core, stream, stream_other).reshape(BLOCKS, ROWS, 1)
    held = [
        to_slots(lax.dynamic_index_in_dim(part.reshape(LINE, SQUARE, ROWS), corner, 1, keepdims=False))
        for part in (stream, stream_other)
    ]
    middle = HEAD // 2
    frequency = jnp.power(500000.0, -2.0 * jnp.arange(middle).astype(f32) / HEAD)
    angles = jnp.stack(held).astype(f32).reshape(tokens, 1) * frequency[None, :]
    cosines, sines = together(jnp.cos(angles), jnp.sin(angles))
    cosines = jnp.concatenate([cosines] * 4, axis=1)
    sines = jnp.concatenate([-sines, sines] * 2, axis=1)

    def halves_swapped(values):
        return jnp.concatenate(
            [jnp.roll(values[:, head_lanes(head)], middle, axis=1) for head in range(2)], axis=1
        )

    def rotated(values):
        return values * cosines + halves_swapped(values) * sines

    def rotated_back(values):
        return values * cosines - halves_swapped(values) * sines

    def row_sums(first, second):
        sums = jnp.stack([jnp.sum(first, axis=-1), jnp.sum(second, axis=-1)])
        return to_slots(sums.reshape(2, 2, LINE, ROWS).transpose(2, 0, 1, 3))

    def sums_track(value):
        for bit in (Z, FAR):
            (came,) = yield [(value, along(bit))]
            value = value + came
        (came,) = yield [(value, swap_core)]
        return value + jnp.flip(came, 2)

    def row_means(sums):
        return to_slots(sums).transpose(1, 2, 0, 3).reshape(2, tokens, 1) / width

    raw = dot(x_all, qkv_w)
    q_raw, k_raw, v_raw = raw[:, :heads], raw[:, heads : 2 * heads], raw[:, 2 * heads :]
    sums = region(lambda sums: alone(sums_track(sums)), row_sums(q_raw * q_raw, k_raw * k_raw))
    sums, out_later, down_later = together(sums, out_later, down_later)
    down_w = square_join(from_corner, down_own, down_came, down_later).reshape(-1, width)
    out_w = square_join(from_corner, out_own, out_came, out_later)
    out_w = lax.dynamic_slice_in_dim(out_w, core_index * 2, 2, 0).reshape(heads, width)

    hidden_block = hold(pick_columns(core_ref, (w_gate, w_up), SQUARE), sums)
    line_came = [
        line_turn(k)(lax.dynamic_index_in_dim(hidden_block, (place + k) % LINE, 0, keepdims=False))
        for k in range(1, LINE)
    ]
    means = row_means(sums)
    q_scale, k_scale = lax.rsqrt(means[0] + 1e-06), lax.rsqrt(means[1] + 1e-06)
    shape = (2, LINE, ROWS, heads)
    query = rotated(q_raw * q_scale * head_gain[0]).astype(bf16).reshape(shape)
    key = rotated(k_raw * k_scale * head_gain[1]).astype(bf16).reshape(shape)
    value = v_raw.astype(bf16).reshape(shape)
    message_shape = jax.ShapeDtypeStruct((SQUARE, 16, ROWS, HEAD), bf16)
    heads_shape = jax.ShapeDtypeStruct((SQUARE, LINE, ROWS, HEAD), bf16)
    tokens_shape = jax.ShapeDtypeStruct(shape, bf16)

    def attended(query, key, value):
        message = turn_square(
            whole_call(pack_kernel, [message_shape], [core_ref, place_ref], [query, key, value])
        )
        mixed, lse = attend(place_ref, message, query_places)
        mixed = whole_call(unpack_kernel, [tokens_shape], [core_ref], [turn_square(mixed)])
        return message, lse, mixed.reshape(tokens, heads)

    message, lse, mixed = region(attended, query, key, value)
    mixed, line_came = together(mixed, line_came)
    hidden_own = jnp.stack(
        [lax.dynamic_index_in_dim(hidden_block, place, 0, keepdims=False), *line_came]
    )
    hidden_came = square_first(hidden_own)
    branch = region(lambda mixed: alone(scatter_line(across_cores(mixed, out_w, dot))), mixed)
    branch, hidden_came = together(branch, hidden_came)
    hidden_later = square_second(hidden_own, hidden_came)

    def state_of(branch):
        branch_scale = lax.rsqrt(jnp.mean(branch * branch, axis=-1, keepdims=True) + 1e-06)
        hidden_state = inputs.astype(f32) + branch * branch_scale * gains[2]
        state = both_cores(alone(gather_line(hidden_state.astype(bf16))))
        return branch_scale, hidden_state, state

    branch_scale, hidden_state, state = region(state_of, branch)
    state, hidden_later = together(state, hidden_later)
    hidden_w = square_join(from_slots, hidden_own, hidden_came, hidden_later).reshape(width, -1)

    both = dot(state, hidden_w)
    gate, up = in_two(both)
    active = (jax.nn.silu(gate) * up).astype(bf16)
    mlp = alone(scatter_line(across_cores(active, down_w, dot)))
    mlp_scale = lax.rsqrt(jnp.mean(mlp * mlp, axis=-1, keepdims=True) + 1e-06)
    cot = cotangent.astype(f32)
    scaled = cot * gains[3]
    d_mlp = mlp_scale * scaled - mlp * mlp_scale**3 * jnp.mean(mlp * scaled, axis=-1, keepdims=True)
    d_mlp = both_cores(alone(gather_line(d_mlp.astype(bf16))))
    output = (hidden_state + mlp * mlp_scale * gains[3]).astype(bf16)
    mlp_gain_part = jnp.sum(cot * mlp * mlp_scale, axis=0)

    d_active = along_last(d_mlp, down_w)
    sigma = jax.nn.sigmoid(gate)
    d_gate = (d_active * up * sigma * (1.0 + gate * (1.0 - sigma))).astype(bf16)
    d_up = (d_active * gate * sigma).astype(bf16)
    d_both = jnp.concatenate([d_gate, d_up], axis=1)

    total = across_cores(d_both, hidden_w, along_last)
    hidden_split = sum_split(
        from_order, along_first(state, d_both).astype(bf16).reshape(BLOCKS, ROWS, -1)
    )
    down_split = sum_split(
        from_corner, along_first(active, d_mlp).astype(bf16).reshape(SQUARE, -1, width)
    )
    split = [
        jnp.concatenate([first, second.reshape(2, -1, ROWS, second.shape[-1])], axis=1)
        for first, second in zip(hidden_split, down_split)
    ]
    total, split = together(total, split)
    grads_came = sum_first(split)
    d_resid = region(lambda total: cot + alone(scatter_line(total)), total)
    def d_branch_begun(d_resid):
        scaled = d_resid * gains[2]
        d_branch = branch_scale * scaled - branch * branch_scale**3 * jnp.mean(
            branch * scaled, axis=-1, keepdims=True
        )
        attn_gain_part = jnp.sum(d_resid * branch * branch_scale, axis=0)
        return alone(gather_first(d_branch.astype(bf16))), jnp.stack([attn_gain_part, mlp_gain_part])

    def d_branch_of(*came):
        d_branch = both_cores(alone(gather_second(*came)))
        return d_branch, along_last(d_branch, out_w).astype(bf16)

    d_branch, norms = region(d_branch_begun, d_resid)
    d_branch, grads_came = together(d_branch, grads_came)
    grads_kept, grads_came = sum_second(split, grads_came)
    d_branch, d_mixed = region(d_branch_of, *d_branch)
    d_mixed, grads_came = together(d_mixed, grads_came)
    grads = sum_end(grads_kept, grads_came)
    hidden_grad, down_grad = grads[:LINE], grads[LINE:].reshape(-1, width)
    line_came = [
        line_turn(k)(lax.dynamic_index_in_dim(hidden_grad, (place + k) % LINE, 0, keepdims=False))
        for k in range(1, LINE)
    ]

    def attended_back(d_mixed, message, lse, d_branch, mixed):
        grad = whole_call(pack_grad_kernel, [heads_shape], [core_ref], [d_mixed.reshape(shape)])
        grads = attend_back(place_ref, message, query_places, lse, turn_square(grad))
        grads = turn_square(grads)
        wide = jax.ShapeDtypeStruct(shape, f32)
        out_grad = along_first(mixed, d_branch).reshape(1, 2, ROWS, width)
        out_grad = jnp.where(core == jnp.arange(2).reshape(2, 1, 1, 1), out_grad, 0.0).astype(bf16)
        return (
            whole_call(unpack_grad_kernel, [wide] * 3, [core_ref, place_ref], [grads]),
            sum_split(from_corner, out_grad.reshape(SQUARE, ROWS, width)),
        )

    (d_query, d_key, d_value), out_split = region(attended_back, d_mixed, message, lse, d_branch, mixed)
    d_query, line_came = together(d_query, line_came)
    hidden_grad = jnp.stack(
        [lax.dynamic_index_in_dim(hidden_grad, place, 0, keepdims=False), *line_came]
    )
    hidden_other = swap_core(hidden_grad)
    down_other = swap_core(down_grad)
    out_came = sum_first(out_split)
    d_query = rotated_back(d_query.reshape(tokens, heads))
    d_key = rotated_back(d_key.reshape(tokens, heads))
    d_value = d_value.reshape(tokens, heads).astype(bf16)
    query_gain_part = jnp.sum(d_query * q_raw * q_scale, axis=0)
    key_gain_part = jnp.sum(d_key * k_raw * k_scale, axis=0)
    d_query = d_query * head_gain[0]
    d_key = d_key * head_gain[1]

    def head_gains(value):
        for move in (along(X), along(Y), swap_core):
            (came,) = yield [(value, move)]
            value = value + came
        return value

    def all_norms(value):
        for move in (along(Z), along(FAR), swap_core, along(X), along(Y)):
            (came,) = yield [(value, move)]
            value = value + came
        return value

    head_part = jnp.stack([query_gain_part, key_gain_part]).reshape(2, 1, 2, HEAD)
    head_part = jnp.where(core == jnp.arange(2).reshape(1, 2, 1, 1), head_part, 0.0)
    sums, head_grads, norms = region(
        lambda *given: run(sums_track(given[0]), head_gains(given[1]), all_norms(given[2])),
        row_sums(d_query * q_raw, d_key * k_raw),
        head_part,
        norms,
    )
    sums, out_came = together(sums, out_came)
    out_kept, out_came = sum_second(out_split, out_came)
    head_grads = lax.dynamic_index_in_dim(head_grads.reshape(2, SQUARE, HEAD), corner, 1, keepdims=False)
    norms = lax.dynamic_index_in_dim(norms.reshape(2, BLOCKS, ROWS), shard_index, 1, keepdims=False)
    means = row_means(sums)
    d_query = (d_query * q_scale - q_raw * q_scale**3 * means[0]).astype(bf16)
    d_key = (d_key * k_scale - k_raw * k_scale**3 * means[1]).astype(bf16)
    d_qkv = jnp.concatenate([d_query, d_key, d_value], axis=1)
    total = across_cores(d_qkv, qkv_w, along_last)
    qkv_split = sum_split(
        from_order, along_first(x_all, d_qkv).astype(bf16).reshape(BLOCKS, ROWS, -1)
    )
    total, qkv_split = together(total, qkv_split)
    qkv_came = sum_first(qkv_split)

    def inputs_begun(total, hidden_grad, hidden_other):
        hidden_grads = spread_columns(core_ref, slot_places, hidden_grad, hidden_other, 2, SQUARE)
        return alone(scatter_first(total)), hidden_grads

    carried, (gate_grad, up_grad) = region(inputs_begun, total, hidden_grad, hidden_other)
    total, carried, qkv_came, out_came = together(total, carried, qkv_came, out_came)
    qkv_kept, qkv_came = sum_second(qkv_split, qkv_came)
    out_grad = sum_end(out_kept, out_came)[0]
    out_other = swap_core(out_grad)
    input_grad = region(
        lambda total, carried: d_resid + alone(scatter_second(total, *carried)), total, carried
    )
    input_grad, qkv_came = together(input_grad, qkv_came)
    qkv_grad = alone(turn_line(sum_end(qkv_kept, qkv_came)))
    query_grad, key_grad, value_grad = spread_columns(
        core_ref, slot_places, qkv_grad, swap_core(qkv_grad), 3, 1
    )
    down_grad = jnp.concatenate(
        [jnp.where(core, down_other, down_grad), jnp.where(core, down_grad, down_other)]
    )
    return (
        output,
        input_grad,
        query_grad,
        key_grad,
        value_grad,
        out_grad.astype(f32) + out_other.astype(f32),
        head_grads[0],
        head_grads[1],
        norms[0],
        gate_grad,
        up_grad,
        down_grad.astype(f32),
        norms[1],
    )


def solution(mesh):
    on_line = mesh.shape["grp"] == 2 and mesh.shape["shard"] == 16
    placed = (
        P(("grp", "shard"), None),
        P(("grp", "shard")),
        P(("grp", "shard"), None),
        P("shard", None),
        P("shard", None),
        P("shard", None),
        P("shard", None),
        P("shard"),
        P("shard"),
        P("shard"),
        P("shard", None),
        P("shard", None),
        P("shard", None),
        P("shard"),
    )
    return jax.shard_map(
        local_line if on_line else local_general,
        mesh=mesh,
        in_specs=placed,
        out_specs=(
            P(("grp", "shard"), None),
            P(("grp", "shard"), None),
            P("shard", None),
            P("shard", None),
            P("shard", None),
            P("shard", None),
            P("shard"),
            P("shard"),
            P("shard"),
            P("shard", None),
            P("shard", None),
            P("shard", None),
            P("shard"),
        ),
        check_vma=False,
    )
```

```python
import functools
import math

import jax
import jax.numpy as jnp
from jax import lax
from jax.experimental import pallas as pl
from jax.experimental.pallas import tpu as pltpu
from jax.sharding import PartitionSpec as P

HEADS = 16
HEAD = 128
DOC_LEN = 1024


def from_behind(value, axis, steps):
    count = lax.axis_size(axis)
    leading, last = (max(0, -steps), min(count, count - steps))
    return lax.ppermute(value, axis, [(source, source + steps) for source in range(leading, last)])


def norm_rows(values, scales):
    return values * lax.rsqrt(jnp.mean(values * values, axis=-1, keepdims=True) + 1e-06) * scales


def rotate(values, cosines, sines):
    row_count = values.shape[0]
    middle = HEAD // 2
    shaped = values.reshape(row_count, HEADS, HEAD)
    first_half = shaped[..., :middle]
    second_half = shaped[..., middle:]
    turned = jnp.concatenate(
        [first_half * cosines - second_half * sines, second_half * cosines + first_half * sines],
        axis=-1,
    )
    return turned.reshape(row_count, HEADS * HEAD)


def activate(gate_in, up_in):
    return jax.nn.silu(gate_in) * up_in


def along_last(left, right):
    return lax.dot_general(
        left, right, (((1,), (1,)), ((), ())), preferred_element_type=jnp.float32
    )


def along_first(left, right):
    return lax.dot_general(
        left, right, (((0,), (0,)), ((), ())), preferred_element_type=jnp.float32
    )


def reduce_three(first_term, second_term, third_term):
    return (
        lax.psum_scatter(first_term, "shard", scatter_dimension=0, tiled=True),
        lax.psum_scatter(second_term, "shard", scatter_dimension=0, tiled=True),
        lax.psum_scatter(third_term, "shard", scatter_dimension=0, tiled=True),
    )


def local_general(
    inputs,
    positions,
    cotangent,
    w_query,
    w_key,
    w_value,
    w_out,
    query_gain,
    key_gain,
    attn_gain,
    w_gate,
    w_up,
    w_down,
    mlp_gain,
):
    row_count, feature_width = inputs.shape
    reach_back = (DOC_LEN - 2) // row_count + 1
    span_rows = min(row_count, 512)
    key_rows = span_rows + reach_back * row_count
    scaling = 1.0 / math.sqrt(HEAD)
    middle = HEAD // 2
    frequency = jnp.power(500000.0, -2.0 * jnp.arange(middle).astype(jnp.float32) / HEAD)
    angles = positions.astype(jnp.float32)[:, None] * frequency[None, :]
    cosines = jnp.cos(angles)[:, None, :]
    sines = jnp.sin(angles)[:, None, :]
    pieces = (
        lax.all_gather(w_query, "shard", axis=0, tiled=True),
        lax.all_gather(w_key, "shard", axis=0, tiled=True),
        lax.all_gather(w_value, "shard", axis=0, tiled=True),
        lax.all_gather(w_out, "shard", axis=0, tiled=True),
        lax.all_gather(query_gain, "shard", axis=0, tiled=True),
        lax.all_gather(key_gain, "shard", axis=0, tiled=True),
        lax.all_gather(attn_gain, "shard", axis=0, tiled=True),
        lax.all_gather(mlp_gain, "shard", axis=0, tiled=True),
    )
    columns_in = inputs
    acc_query = jnp.dot(columns_in, pieces[0], preferred_element_type=jnp.float32)
    acc_key = jnp.dot(columns_in, pieces[1], preferred_element_type=jnp.float32)
    acc_value = jnp.dot(columns_in, pieces[2], preferred_element_type=jnp.float32)
    out_full = pieces[3]
    gain_block = jnp.stack([pieces[4], pieces[5], pieces[6], pieces[7]]).astype(jnp.float32)
    gain_table = gain_block
    q_raw, k_raw, v_raw, out_full, gain_table = (
        acc_query,
        acc_key,
        acc_value,
        out_full,
        gain_table,
    )

    def prepare(query_in, key_in, query_scale, key_scale):
        return (
            rotate(norm_rows(query_in, query_scale), cosines, sines),
            rotate(norm_rows(key_in, key_scale), cosines, sines),
        )

    rotated, prepare_pull = jax.vjp(prepare, q_raw, k_raw, gain_table[0], gain_table[1])
    query_low = rotated[0].astype(jnp.bfloat16)
    key_value = jnp.stack([rotated[1].astype(jnp.bfloat16), v_raw.astype(jnp.bfloat16)])
    earlier = [
        from_behind(key_value, ("grp", "shard"), distance_back)
        for distance_back in range(reach_back, 0, -1)
    ]
    key_window = jnp.concatenate(earlier + [key_value], axis=1)
    distance = (
        jnp.arange(span_rows)[:, None] + reach_back * row_count - jnp.arange(key_rows)[None, :]
    )

    def block_scores(block_start):
        query_block = query_low.reshape(span_rows, HEADS, HEAD)
        key_block = key_window[0, block_start : block_start + key_rows].reshape(
            key_rows, HEADS, HEAD
        )
        value_block = key_window[1, block_start : block_start + key_rows].reshape(
            key_rows, HEADS, HEAD
        )
        visible = (distance >= 0) & (distance <= positions[:, None])
        scores = (
            jnp.einsum("qhd,khd->hqk", query_block, key_block, preferred_element_type=jnp.float32)
            * scaling
        )
        return (query_block, key_block, value_block, visible, scores)

    block_start = 0
    query_block, key_block, value_block, visible, scores = block_scores(block_start)
    masked = jnp.where(visible[None], scores, -jnp.inf)
    top_score = jnp.max(masked, axis=-1, keepdims=True)
    expo = jnp.exp(masked - top_score)
    totals = jnp.sum(expo, axis=-1, keepdims=True)
    probs_low = (expo / totals).astype(jnp.bfloat16)
    lse_parts = [top_score + jnp.log(totals)]
    mixed = jnp.einsum("hqk,khd->qhd", probs_low, value_block, preferred_element_type=jnp.float32)
    mixed_parts = mixed.reshape(span_rows, feature_width)
    mixed_low = mixed_parts.astype(jnp.bfloat16)
    branch = jnp.dot(mixed_low, out_full, preferred_element_type=jnp.float32)
    branch_normed, attn_pull = jax.vjp(norm_rows, branch, gain_table[2])
    hidden_state = inputs.astype(jnp.float32) + branch_normed
    state_low = hidden_state.astype(jnp.bfloat16)
    pieces = (
        lax.all_gather(w_gate, "shard", axis=0, tiled=True),
        lax.all_gather(w_up, "shard", axis=0, tiled=True),
    )
    columns_in = state_low
    gate_val = jnp.dot(columns_in, pieces[0], preferred_element_type=jnp.float32)
    up_val = jnp.dot(columns_in, pieces[1], preferred_element_type=jnp.float32)
    activated, act_pull = jax.vjp(activate, gate_val, up_val)
    activated_low = activated.astype(jnp.bfloat16)
    columns_in = activated_low
    mlp_out = jnp.dot(
        columns_in,
        lax.all_gather(w_down, "shard", axis=0, tiled=True),
        preferred_element_type=jnp.float32,
    )
    mlp_normed, mlp_pull = jax.vjp(norm_rows, mlp_out, gain_table[3])
    output = (hidden_state + mlp_normed).astype(jnp.bfloat16)
    cot_float = cotangent.astype(jnp.float32)
    d_mlp, d_mlp_gain = mlp_pull(cot_float)
    d_mlp_low = d_mlp.astype(jnp.bfloat16)
    d_hidden = along_last(d_mlp_low, lax.all_gather(w_down, "shard", axis=0, tiled=True))
    d_gate, d_up = act_pull(d_hidden)
    d_gate_low = d_gate.astype(jnp.bfloat16)
    d_up_low = d_up.astype(jnp.bfloat16)
    pieces = lax.all_gather((w_gate, w_up), "shard", axis=0, tiled=True)
    d_state = along_last(d_gate_low, pieces[0]) + along_last(d_up_low, pieces[1])
    d_resid = cot_float + d_state
    gate_term = along_first(state_low, d_gate_low)
    up_term = along_first(state_low, d_up_low)
    down_term = along_first(activated_low, d_mlp_low)
    ffn_sums = reduce_three(gate_term, up_term, down_term)
    d_branch, d_attn_gain = attn_pull(d_resid)
    d_branch_low = d_branch.astype(jnp.bfloat16)
    d_mixed_low = along_last(
        d_branch_low, lax.all_gather(w_out, "shard", axis=0, tiled=True)
    ).astype(jnp.bfloat16)
    dq_parts = []
    grad_window = jnp.zeros((2, (reach_back + 1) * row_count, feature_width), jnp.float32)
    for block_number, block_start in enumerate(range(0, row_count, span_rows)):
        query_block, key_block, value_block, visible, scores = block_scores(block_start)
        probs = jnp.where(visible[None], jnp.exp(scores - lse_parts[block_number]), 0.0)
        grad_block = d_mixed_low.reshape(span_rows, HEADS, HEAD)
        d_probs = jnp.einsum(
            "qhd,khd->hqk", grad_block, value_block, preferred_element_type=jnp.float32
        )
        inner = jnp.sum(probs * d_probs, axis=-1, keepdims=True)
        d_scores = (probs * (d_probs - inner) * scaling).astype(jnp.bfloat16)
        dq_block = jnp.einsum(
            "hqk,khd->qhd", d_scores, key_block, preferred_element_type=jnp.float32
        )
        dq_parts.append(dq_block.reshape(span_rows, feature_width))
        d_keys = jnp.einsum(
            "hqk,qhd->khd", d_scores, query_block, preferred_element_type=jnp.float32
        ).reshape(key_rows, feature_width)
        d_values = jnp.einsum(
            "hqk,qhd->khd",
            probs.astype(jnp.bfloat16),
            grad_block,
            preferred_element_type=jnp.float32,
        ).reshape(key_rows, feature_width)
        grad_window = grad_window.at[:, block_start : block_start + key_rows].add(
            jnp.stack([d_keys, d_values])
        )
    own_grads = grad_window[:, reach_back * row_count :]
    for distance_back in range(1, reach_back + 1):
        lower_row = (reach_back - distance_back) * row_count
        own_grads = own_grads + from_behind(
            grad_window[:, lower_row : lower_row + row_count].astype(jnp.bfloat16),
            ("grp", "shard"),
            -distance_back,
        ).astype(jnp.float32)
    d_query_raw, d_key_raw, d_query_gain, d_key_gain = prepare_pull((dq_parts[0], own_grads[0]))
    d_query_low = d_query_raw.astype(jnp.bfloat16)
    d_key_low = d_key_raw.astype(jnp.bfloat16)
    d_value_low = own_grads[1].astype(jnp.bfloat16)
    pieces = lax.all_gather((w_query, w_key, w_value), "shard", axis=0, tiled=True)
    d_inputs = (
        along_last(d_query_low, pieces[0])
        + along_last(d_key_low, pieces[1])
        + along_last(d_value_low, pieces[2])
    )
    input_grad = d_resid + d_inputs
    qkv_term = along_first(inputs, jnp.concatenate([d_query_low, d_key_low, d_value_low], axis=1))
    out_term = along_first(mixed_low, d_branch_low)
    gain_term = jnp.stack([d_query_gain, d_key_gain, d_attn_gain, d_mlp_gain], axis=1)
    attn_sums = reduce_three(qkv_term, out_term, gain_term)
    gate_sum, up_sum, down_sum, qkv_sum, out_sum, gain_sum = (
        lax.psum(ffn_sums[0].astype(jnp.bfloat16), "grp").astype(jnp.float32),
        lax.psum(ffn_sums[1].astype(jnp.bfloat16), "grp").astype(jnp.float32),
        lax.psum(ffn_sums[2].astype(jnp.bfloat16), "grp").astype(jnp.float32),
        lax.psum(attn_sums[0].astype(jnp.bfloat16), "grp").astype(jnp.float32),
        lax.psum(attn_sums[1].astype(jnp.bfloat16), "grp").astype(jnp.float32),
        lax.psum(attn_sums[2].astype(jnp.bfloat16), "grp").astype(jnp.float32),
    )
    return (
        output,
        input_grad,
        qkv_sum[:, :feature_width],
        qkv_sum[:, feature_width : 2 * feature_width],
        qkv_sum[:, 2 * feature_width :],
        out_sum,
        gain_sum[:, 0],
        gain_sum[:, 1],
        gain_sum[:, 2],
        gate_sum,
        up_sum,
        down_sum,
        gain_sum[:, 3],
    )


LINE = 4
SQUARE = 4
X, Y, Z, FAR = 1, 2, 4, 8
ROWS = 128
BLOCKS = 16
WINDOW = 1152
SHARE = 256
SCALING = 1.0 / math.sqrt(HEAD)
SQUARES = [[SQUARE * z + r for r in range(SQUARE)] for z in range(LINE)]


def swap(value, bit):
    return lax.ppermute(value, "shard", [(source, source ^ bit) for source in range(BLOCKS)])


def swap_core(value):
    return lax.ppermute(value, "grp", [(0, 1), (1, 0)])


def along(bit):
    return lambda value: swap(value, bit)


def line_place():
    return lax.axis_index("shard") // SQUARE


def square_place():
    return lax.axis_index("shard") % SQUARE


def line_move(pairs):
    pairs = [(SQUARE * z + r, SQUARE * to + r) for z, to in pairs for r in range(SQUARE)]
    return lambda value: lax.ppermute(value, "shard", pairs)


RIGHT, LEFT = ((0, 1), (1, 2), (2, 3)), ((3, 2), (2, 1), (1, 0))


def line_turn(distance):
    pairs = [(s, (s + SQUARE * distance) % BLOCKS) for s in range(BLOCKS)]
    return lambda value: lax.ppermute(value, "shard", pairs)


def hold(values, *later):
    return lax.optimization_barrier((values, later))[0]


def together(*values):
    return lax.optimization_barrier(values)


def run(*tracks):
    live, results = {}, {}

    def advance(name, generator, came):
        try:
            live[name] = (generator, generator.send(came))
        except StopIteration as end:
            live.pop(name, None)
            results[name] = end.value

    for name, generator in enumerate(tracks):
        advance(name, generator, None)
    while live:
        requests = [request for _, asked in live.values() for request in asked]
        given = lax.optimization_barrier(tuple(value for value, _ in requests))
        came = [move(value) for value, (_, move) in zip(given, requests)]
        came = list(lax.optimization_barrier(tuple(came)))
        for name, (generator, asked) in list(live.items()):
            mine, came = came[: len(asked)], came[len(asked) :]
            advance(name, generator, mine)
    return [results[name] for name in range(len(tracks))]


def one(value, move):
    (came,) = yield [(value, move)]
    return came


def alone(track):
    return run(track)[0]


def gather_first(value):
    right, left = yield [(value, line_move(RIGHT)), (value, line_move(LEFT))]
    return value, right, left


def gather_second(value, right, left):
    place = line_place()
    further = jnp.where(place == 1, right, left)
    rights, lefts, further = yield [
        (right, line_move(RIGHT[1:])),
        (left, line_move(LEFT[1:])),
        (further, line_move(((1, 3), (2, 0)))),
    ]
    rows, width = value.shape
    shape = jax.ShapeDtypeStruct((LINE * rows, width), value.dtype)
    arrays = [value, right, left, rights, lefts, further]
    return whole_call(gather_kernel, [shape], [place.astype(jnp.int32).reshape(1)], arrays)


def gather_kernel(place_ref, own_ref, right_ref, left_ref, rights_ref, lefts_ref, further_ref, out_ref):
    place, rows = place_ref[0], own_ref.shape[0]

    def put(slot, condition, ref):
        @pl.when(condition)
        def _():
            out_ref[slot * rows : (slot + 1) * rows, :] = ref[...]

    out_ref[:rows, :] = own_ref[...]
    put(1, place >= 1, right_ref)
    put(1, place == 0, further_ref)
    put(2, place >= 2, rights_ref)
    put(2, place < 2, lefts_ref)
    put(3, place == 3, further_ref)
    put(3, place < 3, left_ref)


def gather_line(value):
    came = yield from gather_first(value)
    return (yield from gather_second(*came))


def join_kernel(own_ref, other_ref, out_ref):
    rows = own_ref.shape[0]
    out_ref[:rows, :] = own_ref[...]
    out_ref[rows:, :] = other_ref[...]


def both_cores(own):
    shape = jax.ShapeDtypeStruct((2 * own.shape[0], own.shape[1]), own.dtype)
    return whole_call(join_kernel, [shape], [], [own, swap_core(own)])


def scatter_first(total):
    parts = total.reshape(LINE, -1, total.shape[-1])
    further = jnp.where(line_place() == 0, parts[1], parts[3])
    return (
        yield [
            (parts[2], line_move(RIGHT[:2])),
            (parts[2], line_move(LEFT[:2])),
            (further, line_move(((0, 2), (3, 1)))),
        ]
    )


def scatter_second(total, right, left, further):
    parts = total.reshape(LINE, -1, total.shape[-1])
    place, nothing = line_place(), jnp.zeros((), total.dtype)
    right, left = yield [
        (add_low(parts[3], right, jnp.where(place == 2, further, nothing)), line_move(RIGHT)),
        (add_low(parts[1], left, jnp.where(place == 1, further, nothing)), line_move(LEFT)),
    ]
    return add_wide(parts[0], right, left)


def scatter_line(total):
    came = yield from scatter_first(total)
    return (yield from scatter_second(total, *came))


def add_wide(*values):
    return sum(value.astype(jnp.float32) for value in values)


def add_low(*values):
    return add_wide(*values).astype(jnp.bfloat16)


def turn_line(block):
    place = line_place()
    came = yield [
        (lax.dynamic_index_in_dim(block, (place + k) % LINE, 0, keepdims=False), line_turn(k))
        for k in range(1, LINE)
    ]
    own = lax.dynamic_index_in_dim(block, place, 0, keepdims=False)
    return jnp.stack([own, *came])


def to_slots(value):
    place = line_place()
    return jnp.stack(
        [lax.dynamic_index_in_dim(value, (place - k) % LINE, 0, keepdims=False) for k in range(LINE)]
    )


def in_two(value):
    return jnp.split(value, 2, axis=-1)


def square_first(value):
    first, second = in_two(value)
    return swap(first, X), swap(second, Y)


def square_track(value):
    came = yield [(part, along(bit)) for part, bit in zip(in_two(value), (X, Y))]
    return tuple(came)


def second_kernel(own_ref, first_ref, second_ref, to_first_ref, to_second_ref):
    half = own_ref.shape[-1] // 2
    to_first_ref[0] = own_ref[..., :half]
    to_first_ref[1] = first_ref[...]
    to_second_ref[0] = own_ref[..., half:]
    to_second_ref[1] = second_ref[...]


def second_parts(value, came):
    shape = jax.ShapeDtypeStruct((2,) + came[0].shape, value.dtype)
    return whole_call(second_kernel, [shape] * 2, [], [value, *came])


def square_second(value, came):
    first, second = second_parts(value, came)
    return swap(first, Y), swap(second, X)


def second_track(value, came):
    first, second = second_parts(value, came)
    later = yield [(first, along(Y)), (second, along(X))]
    return tuple(later)


def square_kernel(index_ref, own_ref, first_ref, second_ref, firsts_ref, seconds_ref, out_ref):
    half, count = own_ref.shape[-1] // 2, own_ref.shape[0]
    firsts = (own_ref, first_ref, firsts_ref.at[0], firsts_ref.at[1])
    seconds = (own_ref, seconds_ref.at[0], second_ref, seconds_ref.at[1])
    for corner in range(SQUARE):
        for number in range(count):
            target = index_ref[corner * count + number]
            out_ref[target, :, :half] = firsts[corner][number, :, :half]
            lanes = slice(half, None) if corner == 0 else slice(None)
            out_ref[target, :, half:] = seconds[corner][number, :, lanes]


def square_join(index, value, came, later):
    count, rows, width = value.shape
    shape = jax.ShapeDtypeStruct((SQUARE * count, rows, width), value.dtype)
    return whole_call(square_kernel, [shape], [index], [value, *came, *later])


def split_kernel(index_ref, grad_ref, kept_first, sent_first, kept_second, sent_second):
    half, count = grad_ref.shape[-1] // 2, kept_first.shape[1]
    firsts = ((kept_first, 0), (kept_first, 1), (sent_first, 0), (sent_first, 1))
    seconds = ((kept_second, 0), (sent_second, 0), (kept_second, 1), (sent_second, 1))
    for corner in range(SQUARE):
        for number in range(count):
            block = grad_ref[index_ref[corner * count + number]]
            for (target, place), lanes in (
                (firsts[corner], slice(0, half)),
                (seconds[corner], slice(half, 2 * half)),
            ):
                target[place, number] = block[:, lanes]


def sum_split(index, grad):
    blocks, rows, width = grad.shape
    shape = jax.ShapeDtypeStruct((2, blocks // SQUARE, rows, width // 2), grad.dtype)
    return whole_call(split_kernel, [shape] * 4, [index], [grad])


def sum_first(split):
    return swap(split[1], Y), swap(split[3], X)


def low_sum(first, second):
    return (first.astype(jnp.float32) + second.astype(jnp.float32)).astype(jnp.bfloat16)


def add_kernel(kept_first, came_first, kept_second, came_second, *targets):
    for number, (kept, came) in enumerate(((kept_first, came_first), (kept_second, came_second))):
        for place in range(2):
            for block in range(kept.shape[1]):
                targets[2 * number + place][block] = low_sum(kept[place, block], came[place, block])


def sum_later(split, came):
    shape = jax.ShapeDtypeStruct(came[0].shape[1:], jnp.bfloat16)
    arrays = [split[0], came[0], split[2], came[1]]
    first, to_first, second, to_second = whole_call(add_kernel, [shape] * 4, [], arrays)
    return (first, second), (to_first, to_second)


def sum_second(split, came):
    kept, sent = sum_later(split, came)
    return kept, (swap(sent[0], X), swap(sent[1], Y))


def end_kernel(first_ref, came_first, second_ref, came_second, out_ref):
    half = first_ref.shape[-1]
    for block in range(out_ref.shape[0]):
        out_ref[block, :, :half] = low_sum(first_ref[block], came_first[block])
        out_ref[block, :, half:] = low_sum(second_ref[block], came_second[block])


def sum_end(kept, came):
    count, rows, half = kept[0].shape
    shape = jax.ShapeDtypeStruct((count, rows, 2 * half), jnp.bfloat16)
    return whole_call(end_kernel, [shape], [], [kept[0], came[0], kept[1], came[1]])


def in_vmem(count, scalars=1):
    return [pl.BlockSpec(memory_space=pltpu.SMEM)] * scalars + [
        pl.BlockSpec(memory_space=pltpu.VMEM)
    ] * count


def whole_call(kernel, shapes, scalars, arrays, scratch=(), megabytes=40, cost=None):
    specs = [pl.BlockSpec(memory_space=pltpu.VMEM)] * len(shapes)
    single = len(shapes) == 1
    size = sum(array.size * array.dtype.itemsize for array in arrays)
    return pl.pallas_call(
        kernel,
        out_shape=shapes[0] if single else shapes,
        in_specs=in_vmem(len(arrays), len(scalars)),
        out_specs=specs[0] if single else specs,
        scratch_shapes=list(scratch),
        compiler_params=pltpu.CompilerParams(vmem_limit_bytes=megabytes * 2**20),
        cost_estimate=cost or pl.CostEstimate(flops=0, bytes_accessed=2 * size, transcendentals=0),
    )(*scalars, *arrays)


def column_start(columns, parts, place, part, core):
    return pl.multiple_of(place * (columns // LINE) + part * 2 * SHARE + core * SHARE, SHARE)


def pick_kernel(parts, core_ref, *refs):
    *weight_refs, block_ref = refs
    columns = weight_refs[0].shape[1]
    for place in range(LINE):
        for number, weight_ref in enumerate(weight_refs):
            for part in range(parts):
                start = column_start(columns, parts, place, part, core_ref[0])
                lane = (number * parts + part) * SHARE
                block_ref[place, :ROWS, lane : lane + SHARE] = weight_ref[:, pl.ds(start, SHARE)]


def pick_more_kernel(parts, core_ref, *refs):
    *weight_refs, more_ref, block_ref = refs
    pick_kernel(parts, core_ref, *weight_refs, block_ref)
    for place in range(LINE):
        for lane in range(0, block_ref.shape[2], HEAD):
            block_ref[place, ROWS:, lane : lane + HEAD] = more_ref[...]


def spread_kernel(parts, core_ref, mine_ref, came_ref, place_ref, *grad_refs):
    columns = grad_refs[0].shape[1]
    for slot in range(LINE):
        for number, grad_ref in enumerate(grad_refs):
            for part in range(parts):
                lane = (number * parts + part) * SHARE
                for source, core in ((mine_ref, core_ref[0]), (came_ref, 1 - core_ref[0])):
                    start = column_start(columns, parts, place_ref[slot], part, core)
                    grad_ref[:, pl.ds(start, SHARE)] = source[slot, :, lane : lane + SHARE].astype(
                        jnp.float32
                    )


def spread_scalars_kernel(parts, core_ref, place_ref, mine_ref, came_ref, *grad_refs):
    spread_kernel(parts, core_ref, mine_ref, came_ref, place_ref, *grad_refs)


def pick_columns(core_ref, weights, parts, more=None):
    rows, columns = weights[0].shape
    extra = [] if more is None else [more]
    rows += sum(array.shape[0] for array in extra)
    shape = jax.ShapeDtypeStruct((LINE, rows, len(weights) * columns // 8), jnp.bfloat16)
    kernel = functools.partial(pick_more_kernel if extra else pick_kernel, parts)
    return whole_call(kernel, [shape], [core_ref], [*weights, *extra])


def spread_columns(core_ref, place_ref, mine, came, count, parts):
    shape = jax.ShapeDtypeStruct((mine.shape[1], 8 * mine.shape[2] // count), jnp.float32)
    kernel = functools.partial(spread_scalars_kernel, parts)
    return whole_call(kernel, [shape] * count, [core_ref, place_ref], [mine, came])


def head_lanes(head):
    return slice(head * HEAD, (head + 1) * HEAD)


def halo_slots(place):
    return lax.rem(place + 2, LINE), lax.rem(place + 1, LINE)


def rotated(value, cosines, sines):
    return value * cosines + pltpu.roll(value, HEAD // 2, 1) * sines


def rotated_back(value, cosines, sines):
    return value * cosines - pltpu.roll(value, HEAD // 2, 1) * sines


def part_of(group, core):
    return core if group == 0 else 1 - core


def pack_kernel(core_ref, place_ref, raw_ref, scale_ref, gain_ref, cos_ref, sin_ref, out_ref):
    for group in range(2):
        part = part_of(group, core_ref[0])
        for head in range(2):
            target = 2 * group + head
            for slot in range(LINE):
                for number in range(2):
                    lanes = slice((2 * number + head) * HEAD, (2 * number + head + 1) * HEAD)
                    value = raw_ref[part, slot, :, lanes] * scale_ref[number, part, slot]
                    value = value * gain_ref[number : number + 1, head_lanes(head)]
                    value = rotated(value, cos_ref[part, slot], sin_ref[part, slot])
                    out_ref[target, LINE * number + slot] = value.astype(jnp.bfloat16)
                lanes = slice((4 + head) * HEAD, (5 + head) * HEAD)
                out_ref[target, 2 * LINE + slot] = raw_ref[part, slot, :, lanes].astype(jnp.bfloat16)
    for target in range(SQUARE):
        for number, slot in enumerate(halo_slots(place_ref[0])):
            out_ref[target, 12 + number] = out_ref[target % 2, LINE + slot]
            out_ref[target, 14 + number] = out_ref[target % 2, 2 * LINE + slot]


def unpack_kernel(core_ref, came_ref, out_ref):
    for group in range(2):
        part = core_ref[0] if group == 0 else 1 - core_ref[0]
        for head in range(2):
            for slot in range(LINE):
                out_ref[part, slot, :, head_lanes(head)] = came_ref[2 * group + head, slot]


def pack_grad_kernel(core_ref, grad_ref, out_ref):
    for group in range(2):
        part = core_ref[0] if group == 0 else 1 - core_ref[0]
        for head in range(2):
            for slot in range(LINE):
                out_ref[2 * group + head, slot] = grad_ref[part, slot, :, head_lanes(head)]


def unpack_grad_kernel(
    core_ref,
    place_ref,
    came_ref,
    raw_ref,
    scale_ref,
    gain_ref,
    cos_ref,
    sin_ref,
    grad_ref,
    value_ref,
    sums_ref,
    gain_grad_ref,
    d_key,
    d_value,
):
    for group in range(2):
        part = part_of(group, core_ref[0])
        for head in range(2):
            for slot in range(LINE):
                for number, ref in ((1, d_key), (2, d_value)):
                    ref[part, slot, :, head_lanes(head)] = came_ref[
                        2 * group + head, LINE * number + slot
                    ].astype(jnp.float32)
    for head in range(2):
        for number, slot in enumerate(halo_slots(place_ref[0])):
            for first, ref in ((12, d_key), (14, d_value)):
                ref[core_ref[0], slot, :, head_lanes(head)] += came_ref[2 + head, first + number].astype(
                    jnp.float32
                )
    totals = [[jnp.zeros((1, HEAD), jnp.float32) for _ in range(2)] for _ in range(2)]
    for group in range(2):
        part = part_of(group, core_ref[0])
        for slot in range(LINE):
            sums = [jnp.zeros((ROWS, 1), jnp.float32) for _ in range(2)]
            for head in range(2):
                lanes = head_lanes(head)
                d_query = came_ref[2 * group + head, slot].astype(jnp.float32)
                for number, grad in ((0, d_query), (1, d_key[part, slot, :, lanes])):
                    grad = rotated_back(grad, cos_ref[part, slot], sin_ref[part, slot])
                    raw_lanes = slice((2 * number + head) * HEAD, (2 * number + head + 1) * HEAD)
                    raw = raw_ref[part, slot, :, raw_lanes]
                    totals[number][head] += jnp.sum(
                        grad * raw * scale_ref[number, part, slot], axis=0, keepdims=True
                    )
                    grad = grad * gain_ref[number : number + 1, lanes]
                    sums[number] += jnp.sum(grad * raw, axis=1, keepdims=True)
                    grad_ref[number, part, slot, :, lanes] = grad
            for number in range(2):
                sums_ref[number, part, slot] = sums[number]
    for number in range(2):
        for head in range(2):
            gain_grad_ref[number : number + 1, head_lanes(head)] = totals[number][head]
    value_ref[...] = d_value[...].astype(jnp.bfloat16)


def norm_grad_kernel(grad_ref, value_ref, raw_ref, scale_ref, mean_ref, out_ref):
    for part in range(2):
        for slot in range(LINE):
            for number in range(2):
                lanes = slice(2 * number * HEAD, 2 * (number + 1) * HEAD)
                scale = scale_ref[number, part, slot]
                grad = grad_ref[number, part, slot] * scale - raw_ref[part, slot, :, lanes] * (
                    scale * scale * scale * mean_ref[number, part, slot]
                )
                out_ref[part, slot, :, lanes] = grad.astype(jnp.bfloat16)
            out_ref[part, slot, :, 4 * HEAD :] = value_ref[part, slot]


def visible_of(place):
    row = lax.broadcasted_iota(jnp.int32, (ROWS, WINDOW), 0)
    column = lax.broadcasted_iota(jnp.int32, (ROWS, WINDOW), 1)
    distance = row - column + (WINDOW - ROWS)
    return (distance >= 0) & (distance <= place)


def dot_last(left, right):
    return lax.dot_general(
        left, right, (((1,), (1,)), ((), ())), preferred_element_type=jnp.float32
    )


def stream_row(place, source, slot):
    block = lax.rem(place - slot + LINE, LINE) * SQUARE + source
    return block, pl.multiple_of(block * ROWS, ROWS)


def rows_at(start):
    return pl.ds(pl.multiple_of(start, ROWS), ROWS)


def fill(place, message_ref, keys, values):
    for source in range(SQUARE):
        for slot in range(LINE):
            _, start = stream_row(place, source, slot)
            keys[rows_at(start + DOC_LEN), :] = message_ref[source, LINE + slot]
            values[rows_at(start + DOC_LEN), :] = message_ref[source, 2 * LINE + slot]
        for number in range(2):
            start = (number * SQUARE + source) * ROWS
            keys[start : start + ROWS, :] = message_ref[source, 12 + number]
            values[start : start + ROWS, :] = message_ref[source, 14 + number]


def attend_kernel(place_ref, message_ref, pos_ref, o_ref, lse_ref, keys, values):
    place = place_ref[0]
    fill(place, message_ref, keys, values)

    def step(number, carry):
        source, slot = number // LINE, number % LINE
        block, start = stream_row(place, source, slot)
        rows = pl.ds(start, WINDOW)
        scores = dot_last(message_ref[source, slot], keys[rows, :]) * SCALING
        masked = jnp.where(visible_of(pos_ref[block]), scores, -jnp.inf)
        top = jnp.max(masked, axis=-1, keepdims=True)
        expo = jnp.exp(masked - top)
        total = jnp.sum(expo, axis=-1, keepdims=True)
        probs = (expo / total).astype(jnp.bfloat16)
        mixed = jnp.dot(probs, values[rows, :], preferred_element_type=jnp.float32)
        o_ref[source, slot] = mixed.astype(jnp.bfloat16)
        lse_ref[number] = top + jnp.log(total)
        return carry

    lax.fori_loop(0, BLOCKS, step, 0)


def attend_back_kernel(
    place_ref, message_ref, pos_ref, lse_ref, do_ref, out_ref, keys, values, d_keys, d_values
):
    place = place_ref[0]
    fill(place, message_ref, keys, values)
    d_keys[...] = jnp.zeros_like(d_keys)
    d_values[...] = jnp.zeros_like(d_values)

    def step(number, carry):
        source, slot = number // LINE, number % LINE
        block, start = stream_row(place, source, slot)
        rows = pl.ds(start, WINDOW)
        query, grad = message_ref[source, slot], do_ref[source, slot]
        key, value = keys[rows, :], values[rows, :]
        scores = dot_last(query, key) * SCALING
        probs = jnp.where(visible_of(pos_ref[block]), jnp.exp(scores - lse_ref[number]), 0.0)
        d_probs = dot_last(grad, value)
        inner = jnp.sum(probs * d_probs, axis=-1, keepdims=True)
        d_scores = (probs * (d_probs - inner) * SCALING).astype(jnp.bfloat16)
        d_query = jnp.dot(d_scores, key, preferred_element_type=jnp.float32)
        out_ref[source, slot] = d_query.astype(jnp.bfloat16)
        d_keys[rows, :] += along_first(d_scores, query)
        d_values[rows, :] += along_first(probs.astype(jnp.bfloat16), grad)
        return carry

    lax.fori_loop(0, BLOCKS, step, 0)
    for source in range(SQUARE):
        for slot in range(LINE):
            _, start = stream_row(place, source, slot)
            out_ref[source, LINE + slot] = d_keys[rows_at(start + DOC_LEN), :].astype(jnp.bfloat16)
            out_ref[source, 2 * LINE + slot] = d_values[rows_at(start + DOC_LEN), :].astype(jnp.bfloat16)
        for number in range(2):
            start = (number * SQUARE + source) * ROWS
            out_ref[source, 12 + number] = d_keys[start : start + ROWS, :].astype(jnp.bfloat16)
            out_ref[source, 14 + number] = d_values[start : start + ROWS, :].astype(jnp.bfloat16)


KEPT = [pltpu.VMEM((3 * DOC_LEN, HEAD), jnp.bfloat16)] * 2
SUMMED = [pltpu.VMEM((3 * DOC_LEN, HEAD), jnp.float32)] * 2


def attend(place_ref, message, positions):
    shapes = [
        jax.ShapeDtypeStruct((SQUARE, LINE, ROWS, HEAD), jnp.bfloat16),
        jax.ShapeDtypeStruct((BLOCKS, ROWS, 1), jnp.float32),
    ]
    return whole_call(attend_kernel, shapes, [place_ref], [message, positions], KEPT)


def attend_back(place_ref, message, positions, lse, grad):
    shape = jax.ShapeDtypeStruct(message.shape, jnp.bfloat16)
    arrays = [message, positions, lse, grad]
    return whole_call(attend_back_kernel, [shape], [place_ref], arrays, KEPT + SUMMED)


def turn_square(message):
    return lax.all_to_all(message, "shard", 0, 0, tiled=True, axis_index_groups=SQUARES)


def turned_kernel(place_ref, block_ref, *refs):
    came_refs, (whole_ref, first_ref, second_ref) = refs[: LINE - 1], refs[LINE - 1 :]
    half = whole_ref.shape[-1] // 2
    own_ref = block_ref.at[place_ref[0]]
    for slot, ref in enumerate((own_ref, *came_refs)):
        whole_ref[slot] = ref[...]
        first_ref[slot] = ref[:, :half]
        second_ref[slot] = ref[:, half:]


def turned_line(place_ref, block, came):
    half = jax.ShapeDtypeStruct(block.shape[:-1] + (block.shape[-1] // 2,), block.dtype)
    whole = jax.ShapeDtypeStruct(block.shape, block.dtype)
    whole, *parts = whole_call(turned_kernel, [whole, half, half], [place_ref], [block, *came])
    return whole, parts


def local_line(
    inputs,
    positions,
    cotangent,
    w_query,
    w_key,
    w_value,
    w_out,
    query_gain,
    key_gain,
    attn_gain,
    w_gate,
    w_up,
    w_down,
    mlp_gain,
):
    bf16, f32 = jnp.bfloat16, jnp.float32
    width = inputs.shape[1]
    core_index = lax.axis_index("grp")
    shard_index = lax.axis_index("shard")
    core = core_index == 1
    place, corner = line_place(), square_place()
    core_ref = core_index.astype(jnp.int32).reshape(1)
    place_ref = place.astype(jnp.int32).reshape(1)
    slots = jnp.arange(LINE, dtype=jnp.int32)
    slot_places = (place - slots) % LINE
    hidden = w_down.shape[0] * 2
    tokens = 2 * LINE * ROWS
    part_tokens = tokens // 2
    heads = 2 * HEAD
    from_slots = (slot_places[None, :] * SQUARE + (corner ^ slots)[:, None]).reshape(-1)
    from_order = (slots[None, :] * SQUARE + (corner ^ slots)[:, None]).reshape(-1)
    from_corner = corner ^ slots

    def region(function, *given):
        shapes = jax.eval_shape(function, *given)
        empty = lambda *given: jax.tree.map(lambda leaf: jnp.zeros(leaf.shape, leaf.dtype), shapes)
        return lax.cond(positions[0] >= 0, function, empty, *given)

    def across_cores(left, right, product):
        other = product(left[part_tokens:], right).astype(bf16)
        own = product(left[:part_tokens], right)
        return add_low(own, swap_core(other))

    def dot(left, right):
        return jnp.dot(left, right, preferred_element_type=f32)

    small = jnp.concatenate(
        [
            jnp.stack([query_gain, key_gain, attn_gain, mlp_gain]),
            jnp.stack([positions // 32, positions % 32]).astype(bf16),
            jnp.zeros((10, ROWS), bf16),
        ]
    )
    down_own = lax.dynamic_index_in_dim(w_down.reshape(2, 1, hidden // SQUARE, width), core_index, 0, keepdims=False)
    out_own = w_out[None]
    head_block, out_came, down_came = run(
        turn_line(pick_columns(core_ref, (w_query, w_key, w_value), 1, small)),
        square_track(out_own),
        square_track(down_own),
    )
    x_came, head_came = run(gather_first(inputs), square_track(head_block))
    x_own, head_later = run(gather_second(*x_came), second_track(head_block, head_came))
    out_own, down_own = hold((out_own, down_own), x_own)
    out_later = square_second(out_own, out_came)
    down_later = square_second(down_own, down_came)
    x_all = both_cores(x_own)
    head_block = square_join(from_slots, head_block, head_came, head_later)
    qkv_w = head_block[:, :ROWS].reshape(width, 3 * heads)
    gains = head_block[:, ROWS : ROWS + 4, :HEAD].astype(f32)
    first_head = place * SQUARE + core_index * 2
    head_gain = lax.dynamic_slice_in_dim(gains, first_head, 2, 0)[:, :2].transpose(1, 0, 2).reshape(2, heads)
    gains = gains.transpose(1, 0, 2).reshape(4, width)
    stream = head_block[:, ROWS + 4 : ROWS + 6, :HEAD].astype(jnp.int32)
    stream = stream[:, 0] * 32 + stream[:, 1]
    stream_other = swap_core(stream)
    query_places = jnp.where((corner >= 2) == core, stream, stream_other).reshape(BLOCKS, ROWS, 1)
    held = [
        to_slots(lax.dynamic_index_in_dim(part.reshape(LINE, SQUARE, ROWS), corner, 1, keepdims=False))
        for part in (stream, stream_other)
    ]
    middle = HEAD // 2
    frequency = jnp.power(500000.0, -2.0 * (jnp.arange(HEAD) % middle).astype(f32) / HEAD)
    angles = jnp.stack(held).astype(f32)[..., None] * frequency
    sign = jnp.where(jnp.arange(HEAD) < middle, -1.0, 1.0)
    cosines, sines = together(jnp.cos(angles), jnp.sin(angles) * sign)

    def sums_track(value):
        for bit in (Z, FAR):
            (came,) = yield [(value, along(bit))]
            value = value + came
        (came,) = yield [(value, swap_core)]
        return value + jnp.flip(came, 2)

    def row_means(sums):
        sums = to_slots(sums.transpose(2, 0, 1, 3))

        def finish(sums):
            return to_slots(sums).transpose(1, 2, 0, 3)[..., None] / width

        return sums, finish

    raw = dot(x_all, qkv_w)
    raw = raw.reshape(2, LINE, ROWS, 3 * heads)
    squares = raw[..., : 2 * heads] * raw[..., : 2 * heads]
    sums = jnp.stack([jnp.sum(squares[..., :heads], axis=-1), jnp.sum(squares[..., heads:], axis=-1)])
    sums, finish = row_means(sums)
    sums = region(lambda sums: alone(sums_track(sums)), sums)
    sums, out_later = together(sums, out_later)
    scales = lax.rsqrt(finish(sums) + 1e-06)
    out_w = square_join(from_corner, out_own, out_came, out_later)
    out_w = lax.dynamic_slice_in_dim(out_w, core_index * 2, 2, 0).reshape(heads, width)

    hidden_block = hold(pick_columns(core_ref, (w_gate, w_up), SQUARE), sums)
    line_came = [
        line_turn(k)(lax.dynamic_index_in_dim(hidden_block, (place + k) % LINE, 0, keepdims=False))
        for k in range(1, LINE)
    ]
    shape = (2, LINE, ROWS, heads)
    message_shape = jax.ShapeDtypeStruct((SQUARE, 16, ROWS, HEAD), bf16)
    heads_shape = jax.ShapeDtypeStruct((SQUARE, LINE, ROWS, HEAD), bf16)
    tokens_shape = jax.ShapeDtypeStruct(shape, bf16)

    tables = [head_gain, cosines, sines]

    def attended(raw, scales, *tables):
        message = whole_call(
            pack_kernel, [message_shape], [core_ref, place_ref], [raw, scales, *tables]
        )
        message = turn_square(message)
        mixed, lse = attend(place_ref, message, query_places)
        mixed = whole_call(unpack_kernel, [tokens_shape], [core_ref], [turn_square(mixed)])
        return message, lse, mixed.reshape(tokens, heads)

    message, lse, mixed = region(attended, raw, scales, *tables)
    mixed, line_came, down_later = together(mixed, line_came, down_later)
    hidden_own, parts = turned_line(place_ref, hidden_block, line_came)
    hidden_came = swap(parts[0], X), swap(parts[1], Y)

    def branch_of(mixed, out_w, *down):
        down_w = square_join(from_corner, down[0], down[1:3], down[3:]).reshape(-1, width)
        return alone(scatter_line(across_cores(mixed, out_w, dot))), down_w

    branch, down_w = region(branch_of, mixed, out_w, down_own, *down_came, *down_later)
    branch, hidden_came = together(branch, hidden_came)
    hidden_later = square_second(hidden_own, hidden_came)

    def state_of(branch):
        branch_scale = lax.rsqrt(jnp.mean(branch * branch, axis=-1, keepdims=True) + 1e-06)
        hidden_state = inputs.astype(f32) + branch * branch_scale * gains[2]
        state = both_cores(alone(gather_line(hidden_state.astype(bf16))))
        return branch_scale, hidden_state, state

    branch_scale, hidden_state, state = region(state_of, branch)
    state, hidden_later = together(state, hidden_later)
    hidden_w = square_join(from_slots, hidden_own, hidden_came, hidden_later).reshape(width, -1)

    both = dot(state, hidden_w)
    gate, up = in_two(both)
    active = (jax.nn.silu(gate) * up).astype(bf16)
    mlp = alone(scatter_line(across_cores(active, down_w, dot)))
    mlp_scale = lax.rsqrt(jnp.mean(mlp * mlp, axis=-1, keepdims=True) + 1e-06)
    cot = cotangent.astype(f32)
    scaled = cot * gains[3]
    d_mlp = mlp_scale * scaled - mlp * mlp_scale**3 * jnp.mean(mlp * scaled, axis=-1, keepdims=True)
    d_mlp = both_cores(alone(gather_line(d_mlp.astype(bf16))))
    output = (hidden_state + mlp * mlp_scale * gains[3]).astype(bf16)
    mlp_gain_part = jnp.sum(cot * mlp * mlp_scale, axis=0)

    d_active = along_last(d_mlp, down_w)
    sigma = jax.nn.sigmoid(gate)
    d_gate = (d_active * up * sigma * (1.0 + gate * (1.0 - sigma))).astype(bf16)
    d_up = (d_active * gate * sigma).astype(bf16)
    d_both = jnp.concatenate([d_gate, d_up], axis=1)

    total = across_cores(d_both, hidden_w, along_last)

    def d_state_begun(total, state, d_both, active, d_mlp):
        carried = alone(scatter_first(total))
        hidden_grad = along_first(state, d_both).astype(bf16).reshape(BLOCKS, ROWS, -1)
        down_grad = along_first(active, d_mlp).astype(bf16).reshape(SQUARE, -1, width)
        return carried, sum_split(from_order, hidden_grad), sum_split(from_corner, down_grad)

    carried, hidden_split, down_split = region(d_state_begun, total, state, d_both, active, d_mlp)
    hidden_came = sum_first(hidden_split)

    def d_branch_begun(total, *carried):
        d_resid = cot + alone(scatter_second(total, *carried))
        scaled = d_resid * gains[2]
        d_branch = branch_scale * scaled - branch * branch_scale**3 * jnp.mean(
            branch * scaled, axis=-1, keepdims=True
        )
        attn_gain_part = jnp.sum(d_resid * branch * branch_scale, axis=0)
        norms = jnp.stack([attn_gain_part, mlp_gain_part])
        return d_resid, alone(gather_first(d_branch.astype(bf16))), norms

    def d_branch_of(*came):
        d_branch = both_cores(alone(gather_second(*came)))
        return d_branch, along_last(d_branch, out_w).astype(bf16)

    d_resid, d_branch, norms = region(d_branch_begun, total, *carried)
    d_branch, hidden_came = together(d_branch, hidden_came)
    hidden_kept, hidden_came = sum_second(hidden_split, hidden_came)
    d_branch, d_mixed = region(d_branch_of, *d_branch)
    d_mixed, hidden_came = together(d_mixed, hidden_came)
    hidden_grad = sum_end(hidden_kept, hidden_came)
    down_came = sum_first(hold(down_split, hidden_came))
    line_came = [
        line_turn(k)(lax.dynamic_index_in_dim(hidden_grad, (place + k) % LINE, 0, keepdims=False))
        for k in range(1, LINE)
    ]

    def attended_back(d_mixed, message, lse, d_branch, mixed, raw, scales, *tables):
        grad = whole_call(pack_grad_kernel, [heads_shape], [core_ref], [d_mixed.reshape(shape)])
        grads = attend_back(place_ref, message, query_places, lse, turn_square(grad))
        grads = turn_square(grads)
        out_grad = along_first(mixed, d_branch).reshape(1, 2, ROWS, width)
        out_grad = jnp.where(core == jnp.arange(2).reshape(2, 1, 1, 1), out_grad, 0.0).astype(bf16)
        shapes = [
            jax.ShapeDtypeStruct((2,) + shape, f32),
            tokens_shape,
            jax.ShapeDtypeStruct((2, 2, LINE, ROWS, 1), f32),
            jax.ShapeDtypeStruct((2, heads), f32),
        ]
        return (
            whole_call(
                unpack_grad_kernel,
                shapes,
                [core_ref, place_ref],
                [grads, raw, scales, *tables],
                [pltpu.VMEM(shape, f32)] * 2,
            ),
            sum_split(from_corner, out_grad.reshape(SQUARE, ROWS, width)),
        )

    (d_head, d_value, sums, head_part), out_split = region(
        attended_back, d_mixed, message, lse, d_branch, mixed, raw, scales, *tables
    )
    d_head, sums, line_came, down_came = together(d_head, sums, line_came, down_came)
    hidden_grad, _ = turned_line(place_ref, hidden_grad, line_came)
    hidden_other = swap_core(hidden_grad)
    out_came = sum_first(out_split)

    def head_gains(value):
        for move in (along(X), along(Y), swap_core):
            (came,) = yield [(value, move)]
            value = value + came
        return value

    def all_norms(value):
        for move in (along(Z), along(FAR), swap_core):
            (came,) = yield [(value, move)]
            value = value + came
        return value

    def norms_over(bit, value):
        (came,) = yield [(value, along(bit))]
        return value + came

    head_part = head_part.reshape(2, 1, 2, HEAD)
    head_part = jnp.where(core == jnp.arange(2).reshape(1, 2, 1, 1), head_part, 0.0)
    sums, finish = row_means(sums.reshape(2, 2, LINE, ROWS))
    sums, head_grads, norms = region(
        lambda *given: run(sums_track(given[0]), head_gains(given[1]), all_norms(given[2])),
        sums,
        head_part,
        norms,
    )
    sums, out_came = together(sums, out_came)
    head_grads = lax.dynamic_index_in_dim(head_grads.reshape(2, SQUARE, HEAD), corner, 1, keepdims=False)
    qkv_shape = jax.ShapeDtypeStruct(raw.shape, bf16)
    d_qkv = whole_call(norm_grad_kernel, [qkv_shape], [], [d_head, d_value, raw, scales, finish(sums)])
    d_qkv = d_qkv.reshape(tokens, -1)
    total = across_cores(d_qkv, qkv_w, along_last)
    qkv_split = sum_split(
        from_order, along_first(x_all, d_qkv).astype(bf16).reshape(BLOCKS, ROWS, -1)
    )

    def first_track(split):
        return (yield [(split[1], along(Y)), (split[3], along(X))])

    def later_track(split, came):
        kept, (first, second) = sum_later(split, came)
        came = yield [(first, along(X)), (second, along(Y))]
        return sum_end(kept, came)

    def inputs_begun(total, split, hidden_grad, hidden_other):
        hidden_grads = spread_columns(core_ref, slot_places, hidden_grad, hidden_other, 2, SQUARE)
        return run(scatter_first(total), first_track(split)), hidden_grads

    (carried, qkv_came), (gate_grad, up_grad) = region(
        inputs_begun, total, qkv_split, hidden_grad, hidden_other
    )
    total, out_came = together(total, out_came)
    d_inputs, qkv_grad, norms = region(
        lambda total, carried, split, came, norms: run(
            scatter_second(total, *carried), later_track(split, came), norms_over(X, norms)
        ),
        total,
        carried,
        qkv_split,
        qkv_came,
        norms,
    )
    input_grad = d_resid + d_inputs
    qkv_grad, out_grad, down_grad = run(
        turn_line(qkv_grad), later_track(out_split, out_came), later_track(down_split, down_came)
    )
    out_grad, down_grad = out_grad[0], down_grad[0]
    qkv_other, out_other, down_other, norms = run(
        one(qkv_grad, swap_core),
        one(out_grad, swap_core),
        one(down_grad, swap_core),
        norms_over(Y, norms),
    )
    norms = lax.dynamic_index_in_dim(norms.reshape(2, BLOCKS, ROWS), shard_index, 1, keepdims=False)
    query_grad, key_grad, value_grad = spread_columns(core_ref, slot_places, qkv_grad, qkv_other, 3, 1)
    down_grad = jnp.concatenate(
        [jnp.where(core, down_other, down_grad), jnp.where(core, down_grad, down_other)]
    )
    return (
        output,
        input_grad,
        query_grad,
        key_grad,
        value_grad,
        out_grad.astype(f32) + out_other.astype(f32),
        head_grads[0],
        head_grads[1],
        norms[0],
        gate_grad,
        up_grad,
        down_grad.astype(f32),
        norms[1],
    )


def solution(mesh):
    on_line = mesh.shape["grp"] == 2 and mesh.shape["shard"] == 16
    placed = (
        P(("grp", "shard"), None),
        P(("grp", "shard")),
        P(("grp", "shard"), None),
        P("shard", None),
        P("shard", None),
        P("shard", None),
        P("shard", None),
        P("shard"),
        P("shard"),
        P("shard"),
        P("shard", None),
        P("shard", None),
        P("shard", None),
        P("shard"),
    )
    return jax.shard_map(
        local_line if on_line else local_general,
        mesh=mesh,
        in_specs=placed,
        out_specs=(
            P(("grp", "shard"), None),
            P(("grp", "shard"), None),
            P("shard", None),
            P("shard", None),
            P("shard", None),
            P("shard", None),
            P("shard"),
            P("shard"),
            P("shard"),
            P("shard", None),
            P("shard", None),
            P("shard", None),
            P("shard"),
        ),
        check_vma=False,
    )
```

```python
import functools
import math

import jax
import jax.numpy as jnp
from jax import lax
from jax.experimental import pallas as pl
from jax.experimental.layout import Layout, with_layout_constraint
from jax.experimental.pallas import tpu as pltpu
from jax.sharding import PartitionSpec as P

HEADS = 16
HEAD = 128
DOC_LEN = 1024


def from_behind(value, axis, steps):
    count = lax.axis_size(axis)
    leading, last = (max(0, -steps), min(count, count - steps))
    return lax.ppermute(value, axis, [(source, source + steps) for source in range(leading, last)])


def norm_rows(values, scales):
    return values * lax.rsqrt(jnp.mean(values * values, axis=-1, keepdims=True) + 1e-06) * scales


def rotate(values, cosines, sines):
    row_count = values.shape[0]
    middle = HEAD // 2
    shaped = values.reshape(row_count, HEADS, HEAD)
    first_half = shaped[..., :middle]
    second_half = shaped[..., middle:]
    turned = jnp.concatenate(
        [first_half * cosines - second_half * sines, second_half * cosines + first_half * sines],
        axis=-1,
    )
    return turned.reshape(row_count, HEADS * HEAD)


def activate(gate_in, up_in):
    return jax.nn.silu(gate_in) * up_in


def along_last(left, right):
    return lax.dot_general(
        left, right, (((1,), (1,)), ((), ())), preferred_element_type=jnp.float32
    )


def along_first(left, right):
    return lax.dot_general(
        left, right, (((0,), (0,)), ((), ())), preferred_element_type=jnp.float32
    )


def reduce_three(first_term, second_term, third_term):
    return (
        lax.psum_scatter(first_term, "shard", scatter_dimension=0, tiled=True),
        lax.psum_scatter(second_term, "shard", scatter_dimension=0, tiled=True),
        lax.psum_scatter(third_term, "shard", scatter_dimension=0, tiled=True),
    )


def local_general(
    inputs,
    positions,
    cotangent,
    w_query,
    w_key,
    w_value,
    w_out,
    query_gain,
    key_gain,
    attn_gain,
    w_gate,
    w_up,
    w_down,
    mlp_gain,
):
    row_count, feature_width = inputs.shape
    reach_back = (DOC_LEN - 2) // row_count + 1
    span_rows = min(row_count, 512)
    key_rows = span_rows + reach_back * row_count
    scaling = 1.0 / math.sqrt(HEAD)
    middle = HEAD // 2
    frequency = jnp.power(500000.0, -2.0 * jnp.arange(middle).astype(jnp.float32) / HEAD)
    angles = positions.astype(jnp.float32)[:, None] * frequency[None, :]
    cosines = jnp.cos(angles)[:, None, :]
    sines = jnp.sin(angles)[:, None, :]
    pieces = (
        lax.all_gather(w_query, "shard", axis=0, tiled=True),
        lax.all_gather(w_key, "shard", axis=0, tiled=True),
        lax.all_gather(w_value, "shard", axis=0, tiled=True),
        lax.all_gather(w_out, "shard", axis=0, tiled=True),
        lax.all_gather(query_gain, "shard", axis=0, tiled=True),
        lax.all_gather(key_gain, "shard", axis=0, tiled=True),
        lax.all_gather(attn_gain, "shard", axis=0, tiled=True),
        lax.all_gather(mlp_gain, "shard", axis=0, tiled=True),
    )
    columns_in = inputs
    acc_query = jnp.dot(columns_in, pieces[0], preferred_element_type=jnp.float32)
    acc_key = jnp.dot(columns_in, pieces[1], preferred_element_type=jnp.float32)
    acc_value = jnp.dot(columns_in, pieces[2], preferred_element_type=jnp.float32)
    out_full = pieces[3]
    gain_block = jnp.stack([pieces[4], pieces[5], pieces[6], pieces[7]]).astype(jnp.float32)
    gain_table = gain_block
    q_raw, k_raw, v_raw, out_full, gain_table = (
        acc_query,
        acc_key,
        acc_value,
        out_full,
        gain_table,
    )

    def prepare(query_in, key_in, query_scale, key_scale):
        return (
            rotate(norm_rows(query_in, query_scale), cosines, sines),
            rotate(norm_rows(key_in, key_scale), cosines, sines),
        )

    rotated, prepare_pull = jax.vjp(prepare, q_raw, k_raw, gain_table[0], gain_table[1])
    query_low = rotated[0].astype(jnp.bfloat16)
    key_value = jnp.stack([rotated[1].astype(jnp.bfloat16), v_raw.astype(jnp.bfloat16)])
    earlier = [
        from_behind(key_value, ("grp", "shard"), distance_back)
        for distance_back in range(reach_back, 0, -1)
    ]
    key_window = jnp.concatenate(earlier + [key_value], axis=1)
    distance = (
        jnp.arange(span_rows)[:, None] + reach_back * row_count - jnp.arange(key_rows)[None, :]
    )

    def block_scores(block_start):
        query_block = query_low.reshape(span_rows, HEADS, HEAD)
        key_block = key_window[0, block_start : block_start + key_rows].reshape(
            key_rows, HEADS, HEAD
        )
        value_block = key_window[1, block_start : block_start + key_rows].reshape(
            key_rows, HEADS, HEAD
        )
        visible = (distance >= 0) & (distance <= positions[:, None])
        scores = (
            jnp.einsum("qhd,khd->hqk", query_block, key_block, preferred_element_type=jnp.float32)
            * scaling
        )
        return (query_block, key_block, value_block, visible, scores)

    block_start = 0
    query_block, key_block, value_block, visible, scores = block_scores(block_start)
    masked = jnp.where(visible[None], scores, -jnp.inf)
    top_score = jnp.max(masked, axis=-1, keepdims=True)
    expo = jnp.exp(masked - top_score)
    totals = jnp.sum(expo, axis=-1, keepdims=True)
    probs_low = (expo / totals).astype(jnp.bfloat16)
    lse_parts = [top_score + jnp.log(totals)]
    mixed = jnp.einsum("hqk,khd->qhd", probs_low, value_block, preferred_element_type=jnp.float32)
    mixed_parts = mixed.reshape(span_rows, feature_width)
    mixed_low = mixed_parts.astype(jnp.bfloat16)
    branch = jnp.dot(mixed_low, out_full, preferred_element_type=jnp.float32)
    branch_normed, attn_pull = jax.vjp(norm_rows, branch, gain_table[2])
    hidden_state = inputs.astype(jnp.float32) + branch_normed
    state_low = hidden_state.astype(jnp.bfloat16)
    pieces = (
        lax.all_gather(w_gate, "shard", axis=0, tiled=True),
        lax.all_gather(w_up, "shard", axis=0, tiled=True),
    )
    columns_in = state_low
    gate_val = jnp.dot(columns_in, pieces[0], preferred_element_type=jnp.float32)
    up_val = jnp.dot(columns_in, pieces[1], preferred_element_type=jnp.float32)
    activated, act_pull = jax.vjp(activate, gate_val, up_val)
    activated_low = activated.astype(jnp.bfloat16)
    columns_in = activated_low
    mlp_out = jnp.dot(
        columns_in,
        lax.all_gather(w_down, "shard", axis=0, tiled=True),
        preferred_element_type=jnp.float32,
    )
    mlp_normed, mlp_pull = jax.vjp(norm_rows, mlp_out, gain_table[3])
    output = (hidden_state + mlp_normed).astype(jnp.bfloat16)
    cot_float = cotangent.astype(jnp.float32)
    d_mlp, d_mlp_gain = mlp_pull(cot_float)
    d_mlp_low = d_mlp.astype(jnp.bfloat16)
    d_hidden = along_last(d_mlp_low, lax.all_gather(w_down, "shard", axis=0, tiled=True))
    d_gate, d_up = act_pull(d_hidden)
    d_gate_low = d_gate.astype(jnp.bfloat16)
    d_up_low = d_up.astype(jnp.bfloat16)
    pieces = lax.all_gather((w_gate, w_up), "shard", axis=0, tiled=True)
    d_state = along_last(d_gate_low, pieces[0]) + along_last(d_up_low, pieces[1])
    d_resid = cot_float + d_state
    gate_term = along_first(state_low, d_gate_low)
    up_term = along_first(state_low, d_up_low)
    down_term = along_first(activated_low, d_mlp_low)
    ffn_sums = reduce_three(gate_term, up_term, down_term)
    d_branch, d_attn_gain = attn_pull(d_resid)
    d_branch_low = d_branch.astype(jnp.bfloat16)
    d_mixed_low = along_last(
        d_branch_low, lax.all_gather(w_out, "shard", axis=0, tiled=True)
    ).astype(jnp.bfloat16)
    dq_parts = []
    grad_window = jnp.zeros((2, (reach_back + 1) * row_count, feature_width), jnp.float32)
    for block_number, block_start in enumerate(range(0, row_count, span_rows)):
        query_block, key_block, value_block, visible, scores = block_scores(block_start)
        probs = jnp.where(visible[None], jnp.exp(scores - lse_parts[block_number]), 0.0)
        grad_block = d_mixed_low.reshape(span_rows, HEADS, HEAD)
        d_probs = jnp.einsum(
            "qhd,khd->hqk", grad_block, value_block, preferred_element_type=jnp.float32
        )
        inner = jnp.sum(probs * d_probs, axis=-1, keepdims=True)
        d_scores = (probs * (d_probs - inner) * scaling).astype(jnp.bfloat16)
        dq_block = jnp.einsum(
            "hqk,khd->qhd", d_scores, key_block, preferred_element_type=jnp.float32
        )
        dq_parts.append(dq_block.reshape(span_rows, feature_width))
        d_keys = jnp.einsum(
            "hqk,qhd->khd", d_scores, query_block, preferred_element_type=jnp.float32
        ).reshape(key_rows, feature_width)
        d_values = jnp.einsum(
            "hqk,qhd->khd",
            probs.astype(jnp.bfloat16),
            grad_block,
            preferred_element_type=jnp.float32,
        ).reshape(key_rows, feature_width)
        grad_window = grad_window.at[:, block_start : block_start + key_rows].add(
            jnp.stack([d_keys, d_values])
        )
    own_grads = grad_window[:, reach_back * row_count :]
    for distance_back in range(1, reach_back + 1):
        lower_row = (reach_back - distance_back) * row_count
        own_grads = own_grads + from_behind(
            grad_window[:, lower_row : lower_row + row_count].astype(jnp.bfloat16),
            ("grp", "shard"),
            -distance_back,
        ).astype(jnp.float32)
    d_query_raw, d_key_raw, d_query_gain, d_key_gain = prepare_pull((dq_parts[0], own_grads[0]))
    d_query_low = d_query_raw.astype(jnp.bfloat16)
    d_key_low = d_key_raw.astype(jnp.bfloat16)
    d_value_low = own_grads[1].astype(jnp.bfloat16)
    pieces = lax.all_gather((w_query, w_key, w_value), "shard", axis=0, tiled=True)
    d_inputs = (
        along_last(d_query_low, pieces[0])
        + along_last(d_key_low, pieces[1])
        + along_last(d_value_low, pieces[2])
    )
    input_grad = d_resid + d_inputs
    qkv_term = along_first(inputs, jnp.concatenate([d_query_low, d_key_low, d_value_low], axis=1))
    out_term = along_first(mixed_low, d_branch_low)
    gain_term = jnp.stack([d_query_gain, d_key_gain, d_attn_gain, d_mlp_gain], axis=1)
    attn_sums = reduce_three(qkv_term, out_term, gain_term)
    gate_sum, up_sum, down_sum, qkv_sum, out_sum, gain_sum = (
        lax.psum(ffn_sums[0].astype(jnp.bfloat16), "grp").astype(jnp.float32),
        lax.psum(ffn_sums[1].astype(jnp.bfloat16), "grp").astype(jnp.float32),
        lax.psum(ffn_sums[2].astype(jnp.bfloat16), "grp").astype(jnp.float32),
        lax.psum(attn_sums[0].astype(jnp.bfloat16), "grp").astype(jnp.float32),
        lax.psum(attn_sums[1].astype(jnp.bfloat16), "grp").astype(jnp.float32),
        lax.psum(attn_sums[2].astype(jnp.bfloat16), "grp").astype(jnp.float32),
    )
    return (
        output,
        input_grad,
        qkv_sum[:, :feature_width],
        qkv_sum[:, feature_width : 2 * feature_width],
        qkv_sum[:, 2 * feature_width :],
        out_sum,
        gain_sum[:, 0],
        gain_sum[:, 1],
        gain_sum[:, 2],
        gate_sum,
        up_sum,
        down_sum,
        gain_sum[:, 3],
    )


LINE = 4
SQUARE = 4
X, Y, Z, FAR = 1, 2, 4, 8
ROWS = 128
BLOCKS = 16
QUERIES = 2 * ROWS
WINDOW = DOC_LEN + QUERIES
SHARE = 256
SCALING = 1.0 / math.sqrt(HEAD)
LINES = [[SQUARE * z + r for z in range(LINE)] for r in range(SQUARE)]
SQUARES = [[SQUARE * z + r for r in range(SQUARE)] for z in range(LINE)]


def swap(value, bit):
    return lax.ppermute(value, "shard", [(source, source ^ bit) for source in range(BLOCKS)])


def swap_core(value):
    return lax.ppermute(value, "grp", [(0, 1), (1, 0)])


def along(bit):
    return lambda value: swap(value, bit)


def line_place():
    return lax.axis_index("shard") // SQUARE


def square_place():
    return lax.axis_index("shard") % SQUARE


def line_move(pairs):
    pairs = [(SQUARE * z + r, SQUARE * to + r) for z, to in pairs for r in range(SQUARE)]
    return lambda value: lax.ppermute(value, "shard", pairs)


RIGHT, LEFT = ((0, 1), (1, 2), (2, 3)), ((3, 2), (2, 1), (1, 0))


def line_step(distance):
    pairs = [(s, (s + SQUARE * distance) % BLOCKS) for s in range(BLOCKS)]
    return lambda value: lax.ppermute(value, "shard", pairs)


def hold(values, *later):
    return lax.optimization_barrier((values, later))[0]


def together(*values):
    return lax.optimization_barrier(values)


def run(*tracks):
    live, results = {}, {}

    def advance(name, generator, came):
        try:
            live[name] = (generator, generator.send(came))
        except StopIteration as end:
            live.pop(name, None)
            results[name] = end.value

    for name, generator in enumerate(tracks):
        advance(name, generator, None)
    while live:
        requests = [request for _, asked in live.values() for request in asked]
        given = lax.optimization_barrier(tuple(value for value, _ in requests))
        came = [move(value) for value, (_, move) in zip(given, requests)]
        came = list(lax.optimization_barrier(tuple(came)))
        for name, (generator, asked) in list(live.items()):
            mine, came = came[: len(asked)], came[len(asked) :]
            advance(name, generator, mine)
    return [results[name] for name in range(len(tracks))]


def one(value, move):
    (came,) = yield [(value, move)]
    return came


def alone(track):
    return run(track)[0]


def gather_first(value):
    right, left = yield [(value, line_move(RIGHT)), (value, line_move(LEFT))]
    return value, right, left


def gather_second(value, right, left):
    place = line_place()
    further = jnp.where(place == 1, right, left)
    rights, lefts, further = yield [
        (right, line_move(RIGHT[1:])),
        (left, line_move(LEFT[1:])),
        (further, line_move(((1, 3), (2, 0)))),
    ]
    rows, width = value.shape
    shape = jax.ShapeDtypeStruct((LINE * rows, width), value.dtype)
    arrays = [value, right, left, rights, lefts, further]
    return whole_call(gather_kernel, [shape], [place.astype(jnp.int32).reshape(1)], arrays)


def gather_kernel(place_ref, own_ref, right_ref, left_ref, rights_ref, lefts_ref, further_ref, out_ref):
    place, rows = place_ref[0], own_ref.shape[0]

    def put(slot, condition, ref):
        @pl.when(condition)
        def _():
            out_ref[slot * rows : (slot + 1) * rows, :] = ref[...]

    out_ref[:rows, :] = own_ref[...]
    put(1, place >= 1, right_ref)
    put(1, place == 0, further_ref)
    put(2, place >= 2, rights_ref)
    put(2, place < 2, lefts_ref)
    put(3, place == 3, further_ref)
    put(3, place < 3, left_ref)


def gather_line(value):
    came = yield from gather_first(value)
    return (yield from gather_second(*came))


def join_kernel(own_ref, other_ref, out_ref):
    rows = own_ref.shape[0]
    out_ref[:rows, :] = own_ref[...]
    out_ref[rows:, :] = other_ref[...]


def join(own, other):
    shape = jax.ShapeDtypeStruct((2 * own.shape[0], own.shape[1]), own.dtype)
    return whole_call(join_kernel, [shape], [], [own, other])


def both_cores(own):
    return join(own, swap_core(own))


def scatter_first(total):
    parts = total.reshape(LINE, -1, total.shape[-1])
    further = jnp.where(line_place() == 0, parts[1], parts[3])
    return (
        yield [
            (parts[2], line_move(RIGHT[:2])),
            (parts[2], line_move(LEFT[:2])),
            (further, line_move(((0, 2), (3, 1)))),
        ]
    )


def scatter_second(total, right, left, further):
    parts = total.reshape(LINE, -1, total.shape[-1])
    place, nothing = line_place(), jnp.zeros((), total.dtype)
    right, left = yield [
        (add_low(parts[3], right, jnp.where(place == 2, further, nothing)), line_move(RIGHT)),
        (add_low(parts[1], left, jnp.where(place == 1, further, nothing)), line_move(LEFT)),
    ]
    return add_wide(parts[0], right, left)


def scatter_line(total):
    came = yield from scatter_first(total)
    return (yield from scatter_second(total, *came))


def add_wide(*values):
    return sum(value.astype(jnp.float32) for value in values)


def add_low(*values):
    return add_wide(*values).astype(jnp.bfloat16)


def turn_line(block):
    return lax.all_to_all(block, "shard", 0, 0, tiled=True, axis_index_groups=LINES)


def to_slots(value):
    place = line_place()
    return jnp.stack(
        [lax.dynamic_index_in_dim(value, (place - k) % LINE, 0, keepdims=False) for k in range(LINE)]
    )


def in_two(value):
    return jnp.split(value, 2, axis=-1)


def square_first(value):
    first, second = in_two(value)
    return swap(first, X), swap(second, Y)


def square_track(value):
    came = yield [(part, along(bit)) for part, bit in zip(in_two(value), (X, Y))]
    return tuple(came)


def second_kernel(own_ref, first_ref, second_ref, to_first_ref, to_second_ref):
    half = own_ref.shape[-1] // 2
    to_first_ref[0] = own_ref[..., :half]
    to_first_ref[1] = first_ref[...]
    to_second_ref[0] = own_ref[..., half:]
    to_second_ref[1] = second_ref[...]


def second_parts(value, came):
    shape = jax.ShapeDtypeStruct((2,) + came[0].shape, value.dtype)
    return whole_call(second_kernel, [shape] * 2, [], [value, *came])


def square_second(value, came):
    first, second = second_parts(value, came)
    return swap(first, Y), swap(second, X)


def second_track(value, came):
    first, second = second_parts(value, came)
    later = yield [(first, along(Y)), (second, along(X))]
    return tuple(later)


def square_kernel(index_ref, own_ref, first_ref, second_ref, firsts_ref, seconds_ref, out_ref):
    half, count = own_ref.shape[-1] // 2, own_ref.shape[0]
    firsts = (own_ref, first_ref, firsts_ref.at[0], firsts_ref.at[1])
    seconds = (own_ref, seconds_ref.at[0], second_ref, seconds_ref.at[1])
    for corner in range(SQUARE):
        for number in range(count):
            target = index_ref[corner * count + number]
            out_ref[target, :, :half] = firsts[corner][number, :, :half]
            lanes = slice(half, None) if corner == 0 else slice(None)
            out_ref[target, :, half:] = seconds[corner][number, :, lanes]


def square_join(index, value, came, later):
    count, rows, width = value.shape
    shape = jax.ShapeDtypeStruct((SQUARE * count, rows, width), value.dtype)
    return whole_call(square_kernel, [shape], [index], [value, *came, *later])


def split_kernel(index_ref, *refs):
    *grad_refs, kept_first, sent_first, kept_second, sent_second = refs
    half, count = kept_first.shape[-1], kept_first.shape[1]
    firsts = ((kept_first, 0), (kept_first, 1), (sent_first, 0), (sent_first, 1))
    seconds = ((kept_second, 0), (sent_second, 0), (kept_second, 1), (sent_second, 1))
    for corner in range(SQUARE):
        for number in range(count):
            row = 0
            for grad_ref in grad_refs:
                block = grad_ref[index_ref[corner * count + number]]
                rows = slice(row, row + block.shape[0])
                row += block.shape[0]
                (target, place), (other, other_place) = firsts[corner], seconds[corner]
                target[place, number, rows, :] = block[:, :half]
                other[other_place, number, rows, :] = block[:, half:]


def sum_split(index, *grads):
    rows = sum(grad.shape[1] for grad in grads)
    shape = (2, grads[0].shape[0] // SQUARE, rows, grads[0].shape[2] // 2)
    shape = jax.ShapeDtypeStruct(shape, grads[0].dtype)
    return whole_call(split_kernel, [shape] * 4, [index], list(grads))


def sum_first(split):
    return swap(split[1], Y), swap(split[3], X)


def low_sum(first, second):
    return (first.astype(jnp.float32) + second.astype(jnp.float32)).astype(jnp.bfloat16)


def add_kernel(kept_first, came_first, kept_second, came_second, *targets):
    for number, (kept, came) in enumerate(((kept_first, came_first), (kept_second, came_second))):
        for place in range(2):
            for block in range(kept.shape[1]):
                targets[2 * number + place][block] = low_sum(kept[place, block], came[place, block])


def sum_later(split, came):
    shape = jax.ShapeDtypeStruct(came[0].shape[1:], jnp.bfloat16)
    arrays = [split[0], came[0], split[2], came[1]]
    first, to_first, second, to_second = whole_call(add_kernel, [shape] * 4, [], arrays)
    return (first, second), (to_first, to_second)


def sum_second(split, came):
    kept, sent = sum_later(split, came)
    return kept, (swap(sent[0], X), swap(sent[1], Y))


def end_kernel(first_ref, came_first, second_ref, came_second, out_ref):
    half = first_ref.shape[-1]
    for block in range(out_ref.shape[0]):
        out_ref[block, :, :half] = low_sum(first_ref[block], came_first[block])
        out_ref[block, :, half:] = low_sum(second_ref[block], came_second[block])


def sum_end(kept, came):
    count, rows, half = kept[0].shape
    shape = jax.ShapeDtypeStruct((count, rows, 2 * half), jnp.bfloat16)
    return whole_call(end_kernel, [shape], [], [kept[0], came[0], kept[1], came[1]])


def in_vmem(count, scalars=1):
    return [pl.BlockSpec(memory_space=pltpu.SMEM)] * scalars + [
        pl.BlockSpec(memory_space=pltpu.VMEM)
    ] * count


def whole_call(kernel, shapes, scalars, arrays, scratch=(), megabytes=40, cost=None):
    specs = [pl.BlockSpec(memory_space=pltpu.VMEM)] * len(shapes)
    single = len(shapes) == 1
    size = sum(array.size * array.dtype.itemsize for array in arrays)
    return pl.pallas_call(
        kernel,
        out_shape=shapes[0] if single else shapes,
        in_specs=in_vmem(len(arrays), len(scalars)),
        out_specs=specs[0] if single else specs,
        scratch_shapes=list(scratch),
        compiler_params=pltpu.CompilerParams(vmem_limit_bytes=megabytes * 2**20),
        cost_estimate=cost or pl.CostEstimate(flops=0, bytes_accessed=2 * size, transcendentals=0),
    )(*scalars, *arrays)


def column_start(columns, parts, place, part, core):
    return pl.multiple_of(place * (columns // LINE) + part * 2 * SHARE + core * SHARE, SHARE)


def pick_kernel(parts, core_ref, *refs):
    *weight_refs, block_ref = refs
    columns = weight_refs[0].shape[1]
    for place in range(LINE):
        for number, weight_ref in enumerate(weight_refs):
            for part in range(parts):
                start = column_start(columns, parts, place, part, core_ref[0])
                lane = (number * parts + part) * SHARE
                block_ref[place, :ROWS, lane : lane + SHARE] = weight_ref[:, pl.ds(start, SHARE)]


def pick_more_kernel(parts, core_ref, *refs):
    *weight_refs, more_ref, block_ref = refs
    pick_kernel(parts, core_ref, *weight_refs, block_ref)
    for place in range(LINE):
        for lane in range(0, block_ref.shape[2], HEAD):
            block_ref[place, ROWS:, lane : lane + HEAD] = more_ref[...]


def spread_kernel(parts, core_ref, mine_ref, came_ref, place_ref, *grad_refs):
    columns = grad_refs[0].shape[1]
    for slot in range(LINE):
        for number, grad_ref in enumerate(grad_refs):
            for part in range(parts):
                lane = (number * parts + part) * SHARE
                for source, core in ((mine_ref, core_ref[0]), (came_ref, 1 - core_ref[0])):
                    start = column_start(columns, parts, place_ref[slot], part, core)
                    grad_ref[:, pl.ds(start, SHARE)] = source[slot, :, lane : lane + SHARE].astype(
                        jnp.float32
                    )


def spread_scalars_kernel(parts, core_ref, place_ref, mine_ref, came_ref, *grad_refs):
    spread_kernel(parts, core_ref, mine_ref, came_ref, place_ref, *grad_refs)


def pick_columns(core_ref, weights, parts, more=None):
    rows, columns = weights[0].shape
    extra = [] if more is None else [more]
    rows += sum(array.shape[0] for array in extra)
    shape = jax.ShapeDtypeStruct((LINE, rows, len(weights) * columns // 8), jnp.bfloat16)
    kernel = functools.partial(pick_more_kernel if extra else pick_kernel, parts)
    return whole_call(kernel, [shape], [core_ref], [*weights, *extra])


def spread_columns(core_ref, place_ref, mine, came, count, parts):
    shape = jax.ShapeDtypeStruct((mine.shape[1], 8 * mine.shape[2] // count), jnp.float32)
    kernel = functools.partial(spread_scalars_kernel, parts)
    return whole_call(kernel, [shape] * count, [core_ref, place_ref], [mine, came])


def gated_grad_kernel(grad_ref, both_ref, out_ref):
    width = grad_ref.shape[1]
    gate, up, grad = both_ref[:, :width], both_ref[:, width:], grad_ref[...]
    sigma = 1.0 / (1.0 + jnp.exp(-gate))
    out_ref[:, :width] = (grad * up * sigma * (1.0 + gate * (1.0 - sigma))).astype(jnp.bfloat16)
    out_ref[:, width:] = (grad * gate * sigma).astype(jnp.bfloat16)


def gated_grad(grad, both):
    rows, width = grad.shape
    narrow, wide = (pl.BlockSpec((ROWS, w), lambda i: (i, 0)) for w in (width, 2 * width))
    return pl.pallas_call(
        gated_grad_kernel,
        out_shape=jax.ShapeDtypeStruct(both.shape, jnp.bfloat16),
        grid=(rows // ROWS,),
        in_specs=[narrow, wide],
        out_specs=wide,
        compiler_params=pltpu.CompilerParams(vmem_limit_bytes=32 * 2**20),
        cost_estimate=pl.CostEstimate(
            flops=20 * grad.size, bytes_accessed=16 * grad.size, transcendentals=grad.size
        ),
    )(grad, both)


def head_lanes(head):
    return slice(head * HEAD, (head + 1) * HEAD)


def halo_slots(place):
    return lax.rem(place + 2, LINE), lax.rem(place + 1, LINE)


def rotated(value, cosines, sines):
    return value * cosines + pltpu.roll(value, HEAD // 2, 1) * sines


def rotated_back(value, cosines, sines):
    return value * cosines - pltpu.roll(value, HEAD // 2, 1) * sines


def part_of(group, core):
    return core if group == 0 else 1 - core


def pack_kernel(core_ref, place_ref, raw_ref, scale_ref, gain_ref, cos_ref, sin_ref, out_ref):
    for group in range(2):
        part = part_of(group, core_ref[0])
        for head in range(2):
            target = 2 * group + head
            for slot in range(LINE):
                for number in range(2):
                    lanes = slice((2 * number + head) * HEAD, (2 * number + head + 1) * HEAD)
                    value = raw_ref[part, slot, :, lanes] * scale_ref[number, part, slot]
                    value = value * gain_ref[number : number + 1, head_lanes(head)]
                    value = rotated(value, cos_ref[part, slot], sin_ref[part, slot])
                    out_ref[target, LINE * number + slot] = value.astype(jnp.bfloat16)
                lanes = slice((4 + head) * HEAD, (5 + head) * HEAD)
                out_ref[target, 2 * LINE + slot] = raw_ref[part, slot, :, lanes].astype(jnp.bfloat16)
    for target in range(SQUARE):
        for number, slot in enumerate(halo_slots(place_ref[0])):
            out_ref[target, 12 + number] = out_ref[target % 2, LINE + slot]
            out_ref[target, 14 + number] = out_ref[target % 2, 2 * LINE + slot]


def unpack_kernel(core_ref, came_ref, out_ref):
    for group in range(2):
        part = core_ref[0] if group == 0 else 1 - core_ref[0]
        for head in range(2):
            for slot in range(LINE):
                out_ref[part, slot, :, head_lanes(head)] = came_ref[2 * group + head, slot]


def pack_grad_kernel(core_ref, grad_ref, out_ref):
    for group in range(2):
        part = core_ref[0] if group == 0 else 1 - core_ref[0]
        for head in range(2):
            for slot in range(LINE):
                out_ref[2 * group + head, slot] = grad_ref[part, slot, :, head_lanes(head)]


def unpack_grad_kernel(
    core_ref,
    place_ref,
    came_ref,
    raw_ref,
    scale_ref,
    gain_ref,
    cos_ref,
    sin_ref,
    grad_ref,
    value_ref,
    sums_ref,
    gain_grad_ref,
    d_key,
    d_value,
):
    for group in range(2):
        part = part_of(group, core_ref[0])
        for head in range(2):
            for slot in range(LINE):
                for number, ref in ((1, d_key), (2, d_value)):
                    ref[part, slot, :, head_lanes(head)] = came_ref[
                        2 * group + head, LINE * number + slot
                    ].astype(jnp.float32)
    for head in range(2):
        for number, slot in enumerate(halo_slots(place_ref[0])):
            for first, ref in ((12, d_key), (14, d_value)):
                ref[core_ref[0], slot, :, head_lanes(head)] += came_ref[2 + head, first + number].astype(
                    jnp.float32
                )
    totals = [[jnp.zeros((1, HEAD), jnp.float32) for _ in range(2)] for _ in range(2)]
    for group in range(2):
        part = part_of(group, core_ref[0])
        for slot in range(LINE):
            sums = [jnp.zeros((ROWS, 1), jnp.float32) for _ in range(2)]
            for head in range(2):
                lanes = head_lanes(head)
                d_query = came_ref[2 * group + head, slot].astype(jnp.float32)
                for number, grad in ((0, d_query), (1, d_key[part, slot, :, lanes])):
                    grad = rotated_back(grad, cos_ref[part, slot], sin_ref[part, slot])
                    raw_lanes = slice((2 * number + head) * HEAD, (2 * number + head + 1) * HEAD)
                    raw = raw_ref[part, slot, :, raw_lanes]
                    totals[number][head] += jnp.sum(
                        grad * raw * scale_ref[number, part, slot], axis=0, keepdims=True
                    )
                    grad = grad * gain_ref[number : number + 1, lanes]
                    sums[number] += jnp.sum(grad * raw, axis=1, keepdims=True)
                    grad_ref[number, part, slot, :, lanes] = grad
            for number in range(2):
                sums_ref[number, part, slot] = sums[number]
    for number in range(2):
        for head in range(2):
            gain_grad_ref[number : number + 1, head_lanes(head)] = totals[number][head]
    value_ref[...] = d_value[...].astype(jnp.bfloat16)


def norm_grad_kernel(grad_ref, value_ref, raw_ref, scale_ref, mean_ref, out_ref):
    for part in range(2):
        for slot in range(LINE):
            for number in range(2):
                lanes = slice(2 * number * HEAD, 2 * (number + 1) * HEAD)
                scale = scale_ref[number, part, slot]
                grad = grad_ref[number, part, slot] * scale - raw_ref[part, slot, :, lanes] * (
                    scale * scale * scale * mean_ref[number, part, slot]
                )
                out_ref[part, slot, :, lanes] = grad.astype(jnp.bfloat16)
            out_ref[part, slot, :, 4 * HEAD :] = value_ref[part, slot]


def visible_of(place):
    row = lax.broadcasted_iota(jnp.int32, (QUERIES, WINDOW), 0)
    column = lax.broadcasted_iota(jnp.int32, (QUERIES, WINDOW), 1)
    distance = row - column + DOC_LEN
    return (distance >= 0) & (distance <= place)


def dot_last(left, right):
    return lax.dot_general(
        left, right, (((1,), (1,)), ((), ())), preferred_element_type=jnp.float32
    )


def stream_row(place, source, slot):
    block = lax.rem(place - slot + LINE, LINE) * SQUARE + source
    return block, pl.multiple_of(block * ROWS, ROWS)


def rows_at(start):
    return pl.ds(pl.multiple_of(start, ROWS), ROWS)


def fill(place, message_ref, keys, values):
    for source in range(SQUARE):
        for slot in range(LINE):
            _, start = stream_row(place, source, slot)
            keys[rows_at(start + DOC_LEN), :] = message_ref[source, LINE + slot]
            values[rows_at(start + DOC_LEN), :] = message_ref[source, 2 * LINE + slot]
        for number in range(2):
            start = (number * SQUARE + source) * ROWS
            keys[start : start + ROWS, :] = message_ref[source, 12 + number]
            values[start : start + ROWS, :] = message_ref[source, 14 + number]


def attend_kernel(place_ref, message_ref, pos_ref, o_ref, lse_ref, keys, values):
    place = place_ref[0]
    fill(place, message_ref, keys, values)

    def step(number, carry):
        sources, slot = pl.ds(2 * (number // LINE), 2), number % LINE
        block, start = stream_row(place, 2 * (number // LINE), slot)
        rows = pl.ds(start, WINDOW)
        query = message_ref[sources, slot].reshape(QUERIES, HEAD)
        scores = dot_last(query, keys[rows, :]) * SCALING
        seen = pos_ref[pl.ds(block, 2)].reshape(QUERIES, 1)
        masked = jnp.where(visible_of(seen), scores, -jnp.inf)
        top = jnp.max(masked, axis=-1, keepdims=True)
        expo = jnp.exp(masked - top)
        total = jnp.sum(expo, axis=-1, keepdims=True)
        probs = (expo / total).astype(jnp.bfloat16)
        mixed = jnp.dot(probs, values[rows, :], preferred_element_type=jnp.float32)
        o_ref[sources, slot] = mixed.astype(jnp.bfloat16).reshape(2, ROWS, HEAD)
        lse_ref[pl.ds(2 * number, 2)] = (top + jnp.log(total)).reshape(2, ROWS, 1)
        return carry

    lax.fori_loop(0, BLOCKS // 2, step, 0)


def attend_back_kernel(
    place_ref, message_ref, pos_ref, lse_ref, do_ref, out_ref, keys, values, d_keys, d_values
):
    place = place_ref[0]
    fill(place, message_ref, keys, values)
    d_keys[...] = jnp.zeros_like(d_keys)
    d_values[...] = jnp.zeros_like(d_values)

    def step(number, carry):
        sources, slot = pl.ds(2 * (number // LINE), 2), number % LINE
        block, start = stream_row(place, 2 * (number // LINE), slot)
        rows = pl.ds(start, WINDOW)
        query = message_ref[sources, slot].reshape(QUERIES, HEAD)
        grad = do_ref[sources, slot].reshape(QUERIES, HEAD)
        key, value = keys[rows, :], values[rows, :]
        scores = dot_last(query, key) * SCALING
        seen = pos_ref[pl.ds(block, 2)].reshape(QUERIES, 1)
        lse = lse_ref[pl.ds(2 * number, 2)].reshape(QUERIES, 1)
        probs = jnp.where(visible_of(seen), jnp.exp(scores - lse), 0.0)
        d_probs = dot_last(grad, value)
        inner = jnp.sum(probs * d_probs, axis=-1, keepdims=True)
        d_scores = (probs * (d_probs - inner) * SCALING).astype(jnp.bfloat16)
        d_query = jnp.dot(d_scores, key, preferred_element_type=jnp.float32)
        out_ref[sources, slot] = d_query.astype(jnp.bfloat16).reshape(2, ROWS, HEAD)
        d_keys[rows, :] += along_first(d_scores, query)
        d_values[rows, :] += along_first(probs.astype(jnp.bfloat16), grad)
        return carry

    lax.fori_loop(0, BLOCKS // 2, step, 0)
    for source in range(SQUARE):
        for slot in range(LINE):
            _, start = stream_row(place, source, slot)
            out_ref[source, LINE + slot] = d_keys[rows_at(start + DOC_LEN), :].astype(jnp.bfloat16)
            out_ref[source, 2 * LINE + slot] = d_values[rows_at(start + DOC_LEN), :].astype(jnp.bfloat16)
        for number in range(2):
            start = (number * SQUARE + source) * ROWS
            out_ref[source, 12 + number] = d_keys[start : start + ROWS, :].astype(jnp.bfloat16)
            out_ref[source, 14 + number] = d_values[start : start + ROWS, :].astype(jnp.bfloat16)


KEPT = [pltpu.VMEM((3 * DOC_LEN, HEAD), jnp.bfloat16)] * 2
SUMMED = [pltpu.VMEM((3 * DOC_LEN, HEAD), jnp.float32)] * 2


def attend(place_ref, message, positions):
    shapes = [
        jax.ShapeDtypeStruct((SQUARE, LINE, ROWS, HEAD), jnp.bfloat16),
        jax.ShapeDtypeStruct((BLOCKS, ROWS, 1), jnp.float32),
    ]
    return whole_call(attend_kernel, shapes, [place_ref], [message, positions], KEPT)


def attend_back(place_ref, message, positions, lse, grad):
    shape = jax.ShapeDtypeStruct(message.shape, jnp.bfloat16)
    arrays = [message, positions, lse, grad]
    return whole_call(attend_back_kernel, [shape], [place_ref], arrays, KEPT + SUMMED)


def turn_square(message):
    return lax.all_to_all(message, "shard", 0, 0, tiled=True, axis_index_groups=SQUARES)


def turned_kernel(place_ref, block_ref, *refs):
    came_refs, (whole_ref, first_ref, second_ref) = refs[: LINE - 1], refs[LINE - 1 :]
    half = whole_ref.shape[-1] // 2
    own_ref = block_ref.at[place_ref[0]]
    for slot, ref in enumerate((own_ref, *came_refs)):
        whole_ref[slot] = ref[...]
        first_ref[slot] = ref[:, :half]
        second_ref[slot] = ref[:, half:]


def turned_line(place_ref, block, came):
    half = jax.ShapeDtypeStruct(block.shape[:-1] + (block.shape[-1] // 2,), block.dtype)
    whole = jax.ShapeDtypeStruct(block.shape, block.dtype)
    whole, *parts = whole_call(turned_kernel, [whole, half, half], [place_ref], [block, *came])
    return whole, parts


def local_line(
    inputs,
    positions,
    cotangent,
    w_query,
    w_key,
    w_value,
    w_out,
    query_gain,
    key_gain,
    attn_gain,
    w_gate,
    w_up,
    w_down,
    mlp_gain,
):
    bf16, f32 = jnp.bfloat16, jnp.float32
    width = inputs.shape[1]
    core_index = lax.axis_index("grp")
    shard_index = lax.axis_index("shard")
    core = core_index == 1
    place, corner = line_place(), square_place()
    core_ref = core_index.astype(jnp.int32).reshape(1)
    place_ref = place.astype(jnp.int32).reshape(1)
    slots = jnp.arange(LINE, dtype=jnp.int32)
    slot_places = (place - slots) % LINE
    hidden = w_down.shape[0] * 2
    tokens = 2 * LINE * ROWS
    part_tokens = tokens // 2
    heads = 2 * HEAD
    from_slots = (slot_places[None, :] * SQUARE + (corner ^ slots)[:, None]).reshape(-1)
    from_order = (slots[None, :] * SQUARE + (corner ^ slots)[:, None]).reshape(-1)
    from_corner = corner ^ slots

    def region(function, *given):
        shapes = jax.eval_shape(function, *given)
        empty = lambda *given: jax.tree.map(lambda leaf: jnp.zeros(leaf.shape, leaf.dtype), shapes)
        return lax.cond(positions[0] >= 0, function, empty, *given)

    def across_cores(left, right, product):
        other = swap_core(product(left[1], right).astype(bf16))
        own = together(product(left[0], right).astype(bf16))[0]
        return add_low(own, other)

    def parts_of(value):
        return value[:part_tokens], value[part_tokens:]

    def dot(left, right):
        return jnp.dot(left, right, preferred_element_type=f32)

    small = jnp.concatenate(
        [
            jnp.stack([query_gain, key_gain, attn_gain, mlp_gain]),
            jnp.stack([positions // 32, positions % 32]).astype(bf16),
            jnp.zeros((10, ROWS), bf16),
        ]
    )
    down_own = lax.dynamic_index_in_dim(w_down.reshape(2, 1, hidden // SQUARE, width), core_index, 0, keepdims=False)
    rows_own = jnp.concatenate([w_out[None], down_own], axis=1)
    head_block, rows_came = run(
        one(pick_columns(core_ref, (w_query, w_key, w_value), 1, small), turn_line),
        square_track(rows_own),
    )
    x_came, head_came = run(gather_first(inputs), square_track(head_block))
    x_own, head_later, rows_parts = run(
        gather_second(*x_came),
        second_track(head_block, head_came),
        one((rows_own, rows_came), lambda given: second_parts(*given)),
    )
    rows_later = swap(rows_parts[0], Y), swap(rows_parts[1], X)
    head_block = square_join(from_order, head_block, head_came, head_later)
    qkv_w = head_block[:, :ROWS].reshape(width, 3 * heads)
    gains = head_block[:, ROWS : ROWS + 4, :HEAD].astype(f32)
    first_head = place * SQUARE + core_index * 2
    head_gain = lax.dynamic_slice_in_dim(gains, first_head, 2, 0)[:, :2].transpose(1, 0, 2).reshape(2, heads)
    gains = gains.transpose(1, 0, 2).reshape(4, width)
    stream = head_block[:, ROWS + 4 : ROWS + 6, :HEAD].astype(jnp.int32)
    stream = stream[:, 0] * 32 + stream[:, 1]
    stream_other = swap_core(stream)
    query_places = jnp.where((corner >= 2) == core, stream, stream_other).reshape(BLOCKS, ROWS, 1)
    held = [
        to_slots(lax.dynamic_index_in_dim(part.reshape(LINE, SQUARE, ROWS), corner, 1, keepdims=False))
        for part in (stream, stream_other)
    ]
    middle = HEAD // 2
    frequency = jnp.power(500000.0, -2.0 * (jnp.arange(HEAD) % middle).astype(f32) / HEAD)
    def sums_track(value):
        for bit in (Z, FAR):
            (came,) = yield [(value, along(bit))]
            value = value + came
        (came,) = yield [(value, swap_core)]
        return value + jnp.flip(came, 2)

    def row_sums(sums):
        return to_slots(sums.transpose(2, 0, 1, 3))

    def row_means(sums):
        return to_slots(sums).transpose(1, 2, 0, 3)[..., None] / width

    def projected(x_own, qkv_w, *held):
        x_other = swap_core(x_own)
        raw = jnp.stack([dot(x_own, qkv_w), dot(x_other, qkv_w)]).reshape(2, LINE, ROWS, 3 * heads)
        squares = raw[..., : 2 * heads] * raw[..., : 2 * heads]
        sums = jnp.stack([jnp.sum(squares[..., :heads], axis=-1), jnp.sum(squares[..., heads:], axis=-1)])
        angles = jnp.stack(held).astype(f32)[..., None] * frequency
        sign = jnp.where(jnp.arange(HEAD) < middle, -1.0, 1.0)
        return x_other, raw, alone(sums_track(row_sums(sums))), jnp.cos(angles), jnp.sin(angles) * sign

    x_other, raw, sums, cosines, sines = region(projected, x_own, qkv_w, *held)
    raw, rows_later = together(raw, rows_later)
    scales = lax.rsqrt(row_means(sums) + 1e-06)

    hidden_block = hold(pick_columns(core_ref, (w_gate, w_up), SQUARE), sums)
    line_came = [
        line_step(k)(lax.dynamic_index_in_dim(hidden_block, (place + k) % LINE, 0, keepdims=False))
        for k in range(1, LINE)
    ]
    shape = (2, LINE, ROWS, heads)
    message_shape = jax.ShapeDtypeStruct((SQUARE, 16, ROWS, HEAD), bf16)
    heads_shape = jax.ShapeDtypeStruct((SQUARE, LINE, ROWS, HEAD), bf16)
    tokens_shape = jax.ShapeDtypeStruct(shape, bf16)

    tables = [head_gain, cosines, sines]

    def attended(raw, scales, *tables):
        message = whole_call(
            pack_kernel, [message_shape], [core_ref, place_ref], [raw, scales, *tables]
        )
        message = turn_square(message)
        mixed, lse = attend(place_ref, message, query_places)
        mixed = whole_call(unpack_kernel, [tokens_shape], [core_ref], [turn_square(mixed)])
        rows_w = square_join(from_corner, rows_own, rows_came, rows_later)
        return message, lse, mixed.reshape(tokens, heads), rows_w

    message, lse, mixed, rows_w = region(attended, raw, scales, *tables)
    mixed, line_came = together(mixed, line_came)
    out_w = lax.dynamic_slice(rows_w, (core_index * 2, 0, 0), (2, ROWS, width)).reshape(heads, width)
    hidden_own, parts = turned_line(place_ref, hidden_block, line_came)
    hidden_came = swap(parts[0], X), swap(parts[1], Y)

    branch = across_cores(parts_of(mixed), out_w, dot)
    branch, down_w = region(
        lambda total, rows: (alone(scatter_line(total)), rows[:, ROWS:].reshape(-1, width)), branch, rows_w
    )
    branch, hidden_came = together(branch, hidden_came)
    hidden_later = square_second(hidden_own, hidden_came)

    def state_of(branch):
        branch_scale = lax.rsqrt(jnp.mean(branch * branch, axis=-1, keepdims=True) + 1e-06)
        hidden_state = inputs.astype(f32) + branch * branch_scale * gains[2]
        state = alone(gather_line(hidden_state.astype(bf16)))
        return branch_scale, hidden_state, state

    branch_scale, hidden_state, state = region(state_of, branch)
    state, hidden_later = together(state, hidden_later)
    hidden_w = square_join(from_slots, hidden_own, hidden_came, hidden_later).reshape(width, -1)

    state = (state, swap_core(state))
    both = [dot(part, hidden_w) for part in state]
    active = [(jax.nn.silu(in_two(part)[0]) * in_two(part)[1]).astype(bf16) for part in both]
    mlp, (state, both, active) = run(
        scatter_line(across_cores(active, down_w, dot)),
        one((state, both, active), lambda pairs: [join(*pair) for pair in pairs]),
    )
    mlp_scale = lax.rsqrt(jnp.mean(mlp * mlp, axis=-1, keepdims=True) + 1e-06)
    cot = cotangent.astype(f32)
    scaled = cot * gains[3]
    d_mlp = mlp_scale * scaled - mlp * mlp_scale**3 * jnp.mean(mlp * scaled, axis=-1, keepdims=True)
    d_mlp = both_cores(alone(gather_line(d_mlp.astype(bf16))))
    output = (hidden_state + mlp * mlp_scale * gains[3]).astype(bf16)
    mlp_gain_part = jnp.sum(cot * mlp * mlp_scale, axis=0)

    d_both = gated_grad(along_last(d_mlp, down_w), both)

    total = across_cores(parts_of(d_both), hidden_w, along_last)

    def d_state_begun(total, state, d_both):
        carried = alone(scatter_first(total))
        hidden_grad = along_first(state, d_both).astype(bf16).reshape(BLOCKS, ROWS, -1)
        return carried, sum_split(from_order, hidden_grad)

    carried, hidden_split = region(d_state_begun, total, state, d_both)
    hidden_came = sum_first(hidden_split)

    def d_branch_begun(total, carried, active, d_mlp):
        d_resid = cotangent.astype(f32) + alone(scatter_second(total, *carried))
        scaled = d_resid * gains[2]
        d_branch = branch_scale * scaled - branch * branch_scale**3 * jnp.mean(
            branch * scaled, axis=-1, keepdims=True
        )
        attn_gain_part = jnp.sum(d_resid * branch * branch_scale, axis=0)
        norms = jnp.stack([attn_gain_part, mlp_gain_part])
        down_grad = along_first(active, d_mlp).astype(bf16).reshape(SQUARE, -1, width)
        return d_resid, alone(gather_first(d_branch.astype(bf16))), norms, down_grad

    def d_branch_of(d_branch):
        d_branch = (d_branch, swap_core(d_branch))
        return d_branch, jnp.stack([along_last(part, out_w).astype(bf16) for part in d_branch])

    d_resid, d_branch, norms, down_grad = region(d_branch_begun, total, carried, active, d_mlp)
    d_branch, hidden_came = together(d_branch, hidden_came)
    hidden_kept, hidden_came = sum_second(hidden_split, hidden_came)
    d_branch, d_mixed = region(d_branch_of, alone(gather_second(*d_branch)))
    d_mixed, hidden_came = together(d_mixed, hidden_came)
    hidden_grad = sum_end(hidden_kept, hidden_came)
    line_came = [
        line_step(k)(lax.dynamic_index_in_dim(hidden_grad, (place + k) % LINE, 0, keepdims=False))
        for k in range(1, LINE)
    ]

    def attended_back(d_mixed, message, lse, d_branch, mixed, down_grad, raw, scales, *tables):
        grad = whole_call(pack_grad_kernel, [heads_shape], [core_ref], [d_mixed.reshape(shape)])
        grads = attend_back(place_ref, message, query_places, lse, turn_square(grad))
        grads = turn_square(grads)
        out_grad = sum(along_first(*pair) for pair in zip(parts_of(mixed), d_branch))
        out_grad = out_grad.reshape(1, 2, ROWS, width)
        out_grad = jnp.where(core == jnp.arange(2).reshape(2, 1, 1, 1), out_grad, 0.0).astype(bf16)
        shapes = [
            jax.ShapeDtypeStruct((2,) + shape, f32),
            tokens_shape,
            jax.ShapeDtypeStruct((2, 2, LINE, ROWS, 1), f32),
            jax.ShapeDtypeStruct((2, heads), f32),
        ]
        return (
            whole_call(
                unpack_grad_kernel,
                shapes,
                [core_ref, place_ref],
                [grads, raw, scales, *tables],
                [pltpu.VMEM(shape, f32)] * 2,
            ),
            sum_split(from_corner, out_grad.reshape(SQUARE, ROWS, width), down_grad),
        )

    (d_head, d_value, sums, head_part), rows_split = region(
        attended_back, d_mixed, message, lse, d_branch, mixed, down_grad, raw, scales, *tables
    )
    d_head, sums, line_came = together(d_head, sums, line_came)
    hidden_grad, _ = turned_line(place_ref, hidden_grad, line_came)
    hidden_other = swap_core(hidden_grad)
    rows_grads_came = sum_first(rows_split)

    head_part = head_part.reshape(2, 1, 2, HEAD)
    head_part = jnp.where(core == jnp.arange(2).reshape(1, 2, 1, 1), head_part, 0.0)

    def gain_sums(norms, heads):
        for bit in (Z, FAR):
            (came,) = yield [(norms, along(bit))]
            norms = norms + came
        both = jnp.concatenate([norms.reshape(-1, ROWS), heads.reshape(-1, ROWS)])
        (came,) = yield [(both, swap_core)]
        return both + came

    def gains_over(bit, value):
        (came,) = yield [(value, along(bit))]
        return value + came

    def d_qkv_of(sums, head_part, norms, d_head, d_value, raw, scales, *x_parts):
        sums, gain_grads, x_all = run(
            sums_track(row_sums(sums.reshape(2, 2, LINE, ROWS))),
            gain_sums(norms, head_part),
            one(x_parts, lambda parts: join(*parts)),
        )
        qkv_shape = jax.ShapeDtypeStruct(raw.shape, bf16)
        arrays = [d_head, d_value, raw, scales, row_means(sums)]
        d_qkv = whole_call(norm_grad_kernel, [qkv_shape], [], arrays).reshape(tokens, -1)
        total = across_cores(parts_of(d_qkv), qkv_w, along_last)
        qkv_grad = along_first(x_all, d_qkv).astype(bf16)
        qkv_grad = with_layout_constraint(qkv_grad, Layout(major_to_minor=(0, 1)))
        return total, sum_split(from_order, qkv_grad.reshape(BLOCKS, ROWS, -1)), gain_grads

    total, qkv_split, gain_grads = region(
        d_qkv_of, sums, head_part, norms, d_head, d_value, raw, scales, x_own, x_other
    )
    total, rows_grads_came = together(total, rows_grads_came)
    def first_track(split):
        return (yield [(split[1], along(Y)), (split[3], along(X))])

    def later_track(split, came):
        kept, (first, second) = sum_later(split, came)
        came = yield [(first, along(X)), (second, along(Y))]
        return sum_end(kept, came)

    def inputs_begun(total, split, hidden_grad, hidden_other):
        hidden_grads = spread_columns(core_ref, slot_places, hidden_grad, hidden_other, 2, SQUARE)
        return run(scatter_first(total), first_track(split)), hidden_grads

    (carried, qkv_came), (gate_grad, up_grad) = region(
        inputs_begun, total, qkv_split, hidden_grad, hidden_other
    )
    def inputs_ended(total, *carried):
        return d_resid + (yield from scatter_second(total, *carried))

    input_grad, qkv_grad, gain_grads = region(
        lambda total, carried, split, came, norms: run(
            inputs_ended(total, *carried), later_track(split, came), gains_over(X, norms)
        ),
        total,
        carried,
        qkv_split,
        qkv_came,
        gain_grads,
    )
    qkv_grad, rows_grad = run(one(qkv_grad, turn_line), later_track(rows_split, rows_grads_came))
    qkv_other, rows_other, gain_grads = run(
        one(qkv_grad, swap_core), one(rows_grad[0], swap_core), gains_over(Y, gain_grads)
    )
    out_grad, down_grad = rows_grad[0, :ROWS], rows_grad[0, ROWS:]
    out_other, down_other = rows_other[:ROWS], rows_other[ROWS:]
    norms, head_grads = (
        lax.dynamic_index_in_dim(part.reshape(2, -1, ROWS), number, 1, keepdims=False)
        for part, number in ((gain_grads[: 2 * BLOCKS], shard_index), (gain_grads[2 * BLOCKS :], corner))
    )
    query_grad, key_grad, value_grad = spread_columns(core_ref, slots, qkv_grad, qkv_other, 3, 1)
    down_grad = jnp.concatenate(
        [jnp.where(core, down_other, down_grad), jnp.where(core, down_grad, down_other)]
    )
    return (
        output,
        input_grad,
        query_grad,
        key_grad,
        value_grad,
        out_grad.astype(f32) + out_other.astype(f32),
        head_grads[0],
        head_grads[1],
        norms[0],
        gate_grad,
        up_grad,
        down_grad.astype(f32),
        norms[1],
    )


def solution(mesh):
    on_line = mesh.shape["grp"] == 2 and mesh.shape["shard"] == 16
    placed = (
        P(("grp", "shard"), None),
        P(("grp", "shard")),
        P(("grp", "shard"), None),
        P("shard", None),
        P("shard", None),
        P("shard", None),
        P("shard", None),
        P("shard"),
        P("shard"),
        P("shard"),
        P("shard", None),
        P("shard", None),
        P("shard", None),
        P("shard"),
    )
    return jax.shard_map(
        local_line if on_line else local_general,
        mesh=mesh,
        in_specs=placed,
        out_specs=(
            P(("grp", "shard"), None),
            P(("grp", "shard"), None),
            P("shard", None),
            P("shard", None),
            P("shard", None),
            P("shard", None),
            P("shard"),
            P("shard"),
            P("shard"),
            P("shard", None),
            P("shard", None),
            P("shard", None),
            P("shard"),
        ),
        check_vma=False,
    )
```

```python
import functools
import math

import jax
import jax.numpy as jnp
from jax import lax
from jax.experimental import pallas as pl
from jax.experimental.layout import Layout, with_layout_constraint
from jax.experimental.pallas import tpu as pltpu
from jax.sharding import PartitionSpec as P

HEADS = 16
HEAD = 128
DOC_LEN = 1024


def from_behind(value, axis, steps):
    count = lax.axis_size(axis)
    leading, last = (max(0, -steps), min(count, count - steps))
    return lax.ppermute(value, axis, [(source, source + steps) for source in range(leading, last)])


def norm_rows(values, scales):
    return values * lax.rsqrt(jnp.mean(values * values, axis=-1, keepdims=True) + 1e-06) * scales


def rotate(values, cosines, sines):
    row_count = values.shape[0]
    middle = HEAD // 2
    shaped = values.reshape(row_count, HEADS, HEAD)
    first_half = shaped[..., :middle]
    second_half = shaped[..., middle:]
    turned = jnp.concatenate(
        [first_half * cosines - second_half * sines, second_half * cosines + first_half * sines],
        axis=-1,
    )
    return turned.reshape(row_count, HEADS * HEAD)


def activate(gate_in, up_in):
    return jax.nn.silu(gate_in) * up_in


def along_last(left, right):
    return lax.dot_general(
        left, right, (((1,), (1,)), ((), ())), preferred_element_type=jnp.float32
    )


def along_first(left, right):
    return lax.dot_general(
        left, right, (((0,), (0,)), ((), ())), preferred_element_type=jnp.float32
    )


def reduce_three(first_term, second_term, third_term):
    return (
        lax.psum_scatter(first_term, "shard", scatter_dimension=0, tiled=True),
        lax.psum_scatter(second_term, "shard", scatter_dimension=0, tiled=True),
        lax.psum_scatter(third_term, "shard", scatter_dimension=0, tiled=True),
    )


def local_general(
    inputs,
    positions,
    cotangent,
    w_query,
    w_key,
    w_value,
    w_out,
    query_gain,
    key_gain,
    attn_gain,
    w_gate,
    w_up,
    w_down,
    mlp_gain,
):
    row_count, feature_width = inputs.shape
    reach_back = (DOC_LEN - 2) // row_count + 1
    span_rows = min(row_count, 512)
    key_rows = span_rows + reach_back * row_count
    scaling = 1.0 / math.sqrt(HEAD)
    middle = HEAD // 2
    frequency = jnp.power(500000.0, -2.0 * jnp.arange(middle).astype(jnp.float32) / HEAD)
    angles = positions.astype(jnp.float32)[:, None] * frequency[None, :]
    cosines = jnp.cos(angles)[:, None, :]
    sines = jnp.sin(angles)[:, None, :]
    pieces = (
        lax.all_gather(w_query, "shard", axis=0, tiled=True),
        lax.all_gather(w_key, "shard", axis=0, tiled=True),
        lax.all_gather(w_value, "shard", axis=0, tiled=True),
        lax.all_gather(w_out, "shard", axis=0, tiled=True),
        lax.all_gather(query_gain, "shard", axis=0, tiled=True),
        lax.all_gather(key_gain, "shard", axis=0, tiled=True),
        lax.all_gather(attn_gain, "shard", axis=0, tiled=True),
        lax.all_gather(mlp_gain, "shard", axis=0, tiled=True),
    )
    columns_in = inputs
    acc_query = jnp.dot(columns_in, pieces[0], preferred_element_type=jnp.float32)
    acc_key = jnp.dot(columns_in, pieces[1], preferred_element_type=jnp.float32)
    acc_value = jnp.dot(columns_in, pieces[2], preferred_element_type=jnp.float32)
    out_full = pieces[3]
    gain_block = jnp.stack([pieces[4], pieces[5], pieces[6], pieces[7]]).astype(jnp.float32)
    gain_table = gain_block
    q_raw, k_raw, v_raw, out_full, gain_table = (
        acc_query,
        acc_key,
        acc_value,
        out_full,
        gain_table,
    )

    def prepare(query_in, key_in, query_scale, key_scale):
        return (
            rotate(norm_rows(query_in, query_scale), cosines, sines),
            rotate(norm_rows(key_in, key_scale), cosines, sines),
        )

    rotated, prepare_pull = jax.vjp(prepare, q_raw, k_raw, gain_table[0], gain_table[1])
    query_low = rotated[0].astype(jnp.bfloat16)
    key_value = jnp.stack([rotated[1].astype(jnp.bfloat16), v_raw.astype(jnp.bfloat16)])
    earlier = [
        from_behind(key_value, ("grp", "shard"), distance_back)
        for distance_back in range(reach_back, 0, -1)
    ]
    key_window = jnp.concatenate(earlier + [key_value], axis=1)
    distance = (
        jnp.arange(span_rows)[:, None] + reach_back * row_count - jnp.arange(key_rows)[None, :]
    )

    def block_scores(block_start):
        query_block = query_low.reshape(span_rows, HEADS, HEAD)
        key_block = key_window[0, block_start : block_start + key_rows].reshape(
            key_rows, HEADS, HEAD
        )
        value_block = key_window[1, block_start : block_start + key_rows].reshape(
            key_rows, HEADS, HEAD
        )
        visible = (distance >= 0) & (distance <= positions[:, None])
        scores = (
            jnp.einsum("qhd,khd->hqk", query_block, key_block, preferred_element_type=jnp.float32)
            * scaling
        )
        return (query_block, key_block, value_block, visible, scores)

    block_start = 0
    query_block, key_block, value_block, visible, scores = block_scores(block_start)
    masked = jnp.where(visible[None], scores, -jnp.inf)
    top_score = jnp.max(masked, axis=-1, keepdims=True)
    expo = jnp.exp(masked - top_score)
    totals = jnp.sum(expo, axis=-1, keepdims=True)
    probs_low = (expo / totals).astype(jnp.bfloat16)
    lse_parts = [top_score + jnp.log(totals)]
    mixed = jnp.einsum("hqk,khd->qhd", probs_low, value_block, preferred_element_type=jnp.float32)
    mixed_parts = mixed.reshape(span_rows, feature_width)
    mixed_low = mixed_parts.astype(jnp.bfloat16)
    branch = jnp.dot(mixed_low, out_full, preferred_element_type=jnp.float32)
    branch_normed, attn_pull = jax.vjp(norm_rows, branch, gain_table[2])
    hidden_state = inputs.astype(jnp.float32) + branch_normed
    state_low = hidden_state.astype(jnp.bfloat16)
    pieces = (
        lax.all_gather(w_gate, "shard", axis=0, tiled=True),
        lax.all_gather(w_up, "shard", axis=0, tiled=True),
    )
    columns_in = state_low
    gate_val = jnp.dot(columns_in, pieces[0], preferred_element_type=jnp.float32)
    up_val = jnp.dot(columns_in, pieces[1], preferred_element_type=jnp.float32)
    activated, act_pull = jax.vjp(activate, gate_val, up_val)
    activated_low = activated.astype(jnp.bfloat16)
    columns_in = activated_low
    mlp_out = jnp.dot(
        columns_in,
        lax.all_gather(w_down, "shard", axis=0, tiled=True),
        preferred_element_type=jnp.float32,
    )
    mlp_normed, mlp_pull = jax.vjp(norm_rows, mlp_out, gain_table[3])
    output = (hidden_state + mlp_normed).astype(jnp.bfloat16)
    cot_float = cotangent.astype(jnp.float32)
    d_mlp, d_mlp_gain = mlp_pull(cot_float)
    d_mlp_low = d_mlp.astype(jnp.bfloat16)
    d_hidden = along_last(d_mlp_low, lax.all_gather(w_down, "shard", axis=0, tiled=True))
    d_gate, d_up = act_pull(d_hidden)
    d_gate_low = d_gate.astype(jnp.bfloat16)
    d_up_low = d_up.astype(jnp.bfloat16)
    pieces = lax.all_gather((w_gate, w_up), "shard", axis=0, tiled=True)
    d_state = along_last(d_gate_low, pieces[0]) + along_last(d_up_low, pieces[1])
    d_resid = cot_float + d_state
    gate_term = along_first(state_low, d_gate_low)
    up_term = along_first(state_low, d_up_low)
    down_term = along_first(activated_low, d_mlp_low)
    ffn_sums = reduce_three(gate_term, up_term, down_term)
    d_branch, d_attn_gain = attn_pull(d_resid)
    d_branch_low = d_branch.astype(jnp.bfloat16)
    d_mixed_low = along_last(
        d_branch_low, lax.all_gather(w_out, "shard", axis=0, tiled=True)
    ).astype(jnp.bfloat16)
    dq_parts = []
    grad_window = jnp.zeros((2, (reach_back + 1) * row_count, feature_width), jnp.float32)
    for block_number, block_start in enumerate(range(0, row_count, span_rows)):
        query_block, key_block, value_block, visible, scores = block_scores(block_start)
        probs = jnp.where(visible[None], jnp.exp(scores - lse_parts[block_number]), 0.0)
        grad_block = d_mixed_low.reshape(span_rows, HEADS, HEAD)
        d_probs = jnp.einsum(
            "qhd,khd->hqk", grad_block, value_block, preferred_element_type=jnp.float32
        )
        inner = jnp.sum(probs * d_probs, axis=-1, keepdims=True)
        d_scores = (probs * (d_probs - inner) * scaling).astype(jnp.bfloat16)
        dq_block = jnp.einsum(
            "hqk,khd->qhd", d_scores, key_block, preferred_element_type=jnp.float32
        )
        dq_parts.append(dq_block.reshape(span_rows, feature_width))
        d_keys = jnp.einsum(
            "hqk,qhd->khd", d_scores, query_block, preferred_element_type=jnp.float32
        ).reshape(key_rows, feature_width)
        d_values = jnp.einsum(
            "hqk,qhd->khd",
            probs.astype(jnp.bfloat16),
            grad_block,
            preferred_element_type=jnp.float32,
        ).reshape(key_rows, feature_width)
        grad_window = grad_window.at[:, block_start : block_start + key_rows].add(
            jnp.stack([d_keys, d_values])
        )
    own_grads = grad_window[:, reach_back * row_count :]
    for distance_back in range(1, reach_back + 1):
        lower_row = (reach_back - distance_back) * row_count
        own_grads = own_grads + from_behind(
            grad_window[:, lower_row : lower_row + row_count].astype(jnp.bfloat16),
            ("grp", "shard"),
            -distance_back,
        ).astype(jnp.float32)
    d_query_raw, d_key_raw, d_query_gain, d_key_gain = prepare_pull((dq_parts[0], own_grads[0]))
    d_query_low = d_query_raw.astype(jnp.bfloat16)
    d_key_low = d_key_raw.astype(jnp.bfloat16)
    d_value_low = own_grads[1].astype(jnp.bfloat16)
    pieces = lax.all_gather((w_query, w_key, w_value), "shard", axis=0, tiled=True)
    d_inputs = (
        along_last(d_query_low, pieces[0])
        + along_last(d_key_low, pieces[1])
        + along_last(d_value_low, pieces[2])
    )
    input_grad = d_resid + d_inputs
    qkv_term = along_first(inputs, jnp.concatenate([d_query_low, d_key_low, d_value_low], axis=1))
    out_term = along_first(mixed_low, d_branch_low)
    gain_term = jnp.stack([d_query_gain, d_key_gain, d_attn_gain, d_mlp_gain], axis=1)
    attn_sums = reduce_three(qkv_term, out_term, gain_term)
    gate_sum, up_sum, down_sum, qkv_sum, out_sum, gain_sum = (
        lax.psum(ffn_sums[0].astype(jnp.bfloat16), "grp").astype(jnp.float32),
        lax.psum(ffn_sums[1].astype(jnp.bfloat16), "grp").astype(jnp.float32),
        lax.psum(ffn_sums[2].astype(jnp.bfloat16), "grp").astype(jnp.float32),
        lax.psum(attn_sums[0].astype(jnp.bfloat16), "grp").astype(jnp.float32),
        lax.psum(attn_sums[1].astype(jnp.bfloat16), "grp").astype(jnp.float32),
        lax.psum(attn_sums[2].astype(jnp.bfloat16), "grp").astype(jnp.float32),
    )
    return (
        output,
        input_grad,
        qkv_sum[:, :feature_width],
        qkv_sum[:, feature_width : 2 * feature_width],
        qkv_sum[:, 2 * feature_width :],
        out_sum,
        gain_sum[:, 0],
        gain_sum[:, 1],
        gain_sum[:, 2],
        gate_sum,
        up_sum,
        down_sum,
        gain_sum[:, 3],
    )


LINE = 4
SQUARE = 4
X, Y, Z, FAR = 1, 2, 4, 8
ROWS = 128
BLOCKS = 16
SHARE = 256
SCALING = 1.0 / math.sqrt(HEAD)
LINES = [[SQUARE * z + r for z in range(LINE)] for r in range(SQUARE)]
SQUARES = [[SQUARE * z + r for r in range(SQUARE)] for z in range(LINE)]


def swap(value, bit):
    return lax.ppermute(value, "shard", [(source, source ^ bit) for source in range(BLOCKS)])


def swap_core(value):
    return lax.ppermute(value, "grp", [(0, 1), (1, 0)])


def along(bit):
    return lambda value: swap(value, bit)


def line_place():
    return lax.axis_index("shard") // SQUARE


def square_place():
    return lax.axis_index("shard") % SQUARE


def line_move(pairs):
    pairs = [(SQUARE * z + r, SQUARE * to + r) for z, to in pairs for r in range(SQUARE)]
    return lambda value: lax.ppermute(value, "shard", pairs)


RIGHT, LEFT = ((0, 1), (1, 2), (2, 3)), ((3, 2), (2, 1), (1, 0))


def line_step(distance):
    pairs = [(s, (s + SQUARE * distance) % BLOCKS) for s in range(BLOCKS)]
    return lambda value: lax.ppermute(value, "shard", pairs)


def hold(values, *later):
    return lax.optimization_barrier((values, later))[0]


def together(*values):
    return lax.optimization_barrier(values)


def run(*tracks):
    live, results = {}, {}

    def advance(name, generator, came):
        try:
            live[name] = (generator, generator.send(came))
        except StopIteration as end:
            live.pop(name, None)
            results[name] = end.value

    for name, generator in enumerate(tracks):
        advance(name, generator, None)
    while live:
        requests = [request for _, asked in live.values() for request in asked]
        given = lax.optimization_barrier(tuple(value for value, _ in requests))
        came = [move(value) for value, (_, move) in zip(given, requests)]
        came = list(lax.optimization_barrier(tuple(came)))
        for name, (generator, asked) in list(live.items()):
            mine, came = came[: len(asked)], came[len(asked) :]
            advance(name, generator, mine)
    return [results[name] for name in range(len(tracks))]


def one(value, move):
    (came,) = yield [(value, move)]
    return came


def alone(track):
    return run(track)[0]


def gather_first(value):
    right, left = yield [(value, line_move(RIGHT)), (value, line_move(LEFT))]
    return value, right, left


def gather_second(value, right, left):
    place = line_place()
    further = jnp.where(place == 1, right, left)
    rights, lefts, further = yield [
        (right, line_move(RIGHT[1:])),
        (left, line_move(LEFT[1:])),
        (further, line_move(((1, 3), (2, 0)))),
    ]
    rows, width = value.shape
    shape = jax.ShapeDtypeStruct((LINE * rows, width), value.dtype)
    arrays = [value, right, left, rights, lefts, further]
    return whole_call(gather_kernel, [shape], [place.astype(jnp.int32).reshape(1)], arrays)


def gather_kernel(place_ref, own_ref, right_ref, left_ref, rights_ref, lefts_ref, further_ref, out_ref):
    place, rows = place_ref[0], own_ref.shape[0]

    def put(slot, condition, ref):
        @pl.when(condition)
        def _():
            out_ref[slot * rows : (slot + 1) * rows, :] = ref[...]

    out_ref[:rows, :] = own_ref[...]
    put(1, place >= 1, right_ref)
    put(1, place == 0, further_ref)
    put(2, place >= 2, rights_ref)
    put(2, place < 2, lefts_ref)
    put(3, place == 3, further_ref)
    put(3, place < 3, left_ref)


def gather_line(value):
    came = yield from gather_first(value)
    return (yield from gather_second(*came))


def join_kernel(own_ref, other_ref, out_ref):
    rows = own_ref.shape[0]
    out_ref[:rows, :] = own_ref[...]
    out_ref[rows:, :] = other_ref[...]


def join(own, other):
    shape = jax.ShapeDtypeStruct((2 * own.shape[0], own.shape[1]), own.dtype)
    return whole_call(join_kernel, [shape], [], [own, other])


def both_cores(own):
    return join(own, swap_core(own))


def scatter_first(total):
    parts = total.reshape(LINE, -1, total.shape[-1])
    further = jnp.where(line_place() == 0, parts[1], parts[3])
    return (
        yield [
            (parts[2], line_move(RIGHT[:2])),
            (parts[2], line_move(LEFT[:2])),
            (further, line_move(((0, 2), (3, 1)))),
        ]
    )


def scatter_second(total, right, left, further):
    parts = total.reshape(LINE, -1, total.shape[-1])
    place, nothing = line_place(), jnp.zeros((), total.dtype)
    right, left = yield [
        (add_low(parts[3], right, jnp.where(place == 2, further, nothing)), line_move(RIGHT)),
        (add_low(parts[1], left, jnp.where(place == 1, further, nothing)), line_move(LEFT)),
    ]
    return add_wide(parts[0], right, left)


def scatter_line(total):
    came = yield from scatter_first(total)
    return (yield from scatter_second(total, *came))


def add_wide(*values):
    return sum(value.astype(jnp.float32) for value in values)


def add_low(*values):
    return add_wide(*values).astype(jnp.bfloat16)


def turn_line(block):
    return lax.all_to_all(block, "shard", 0, 0, tiled=True, axis_index_groups=LINES)


def to_slots(value):
    place = line_place()
    return jnp.stack(
        [lax.dynamic_index_in_dim(value, (place - k) % LINE, 0, keepdims=False) for k in range(LINE)]
    )


def in_two(value):
    return jnp.split(value, 2, axis=-1)


def square_first(value):
    first, second = in_two(value)
    return swap(first, X), swap(second, Y)


def square_track(value):
    came = yield [(part, along(bit)) for part, bit in zip(in_two(value), (X, Y))]
    return tuple(came)


def second_kernel(own_ref, first_ref, second_ref, to_first_ref, to_second_ref):
    half = own_ref.shape[-1] // 2
    to_first_ref[0] = own_ref[..., :half]
    to_first_ref[1] = first_ref[...]
    to_second_ref[0] = own_ref[..., half:]
    to_second_ref[1] = second_ref[...]


def second_parts(value, came):
    shape = jax.ShapeDtypeStruct((2,) + came[0].shape, value.dtype)
    return whole_call(second_kernel, [shape] * 2, [], [value, *came])


def square_second(value, came):
    first, second = second_parts(value, came)
    return swap(first, Y), swap(second, X)


def second_track(value, came):
    first, second = second_parts(value, came)
    later = yield [(first, along(Y)), (second, along(X))]
    return tuple(later)


def square_kernel(index_ref, own_ref, first_ref, second_ref, firsts_ref, seconds_ref, out_ref):
    half, count = own_ref.shape[-1] // 2, own_ref.shape[0]
    firsts = (own_ref, first_ref, firsts_ref.at[0], firsts_ref.at[1])
    seconds = (own_ref, seconds_ref.at[0], second_ref, seconds_ref.at[1])
    for corner in range(SQUARE):
        for number in range(count):
            target = index_ref[corner * count + number]
            out_ref[target, :, :half] = firsts[corner][number, :, :half]
            lanes = slice(half, None) if corner == 0 else slice(None)
            out_ref[target, :, half:] = seconds[corner][number, :, lanes]


def square_join(index, value, came, later):
    count, rows, width = value.shape
    shape = jax.ShapeDtypeStruct((SQUARE * count, rows, width), value.dtype)
    return whole_call(square_kernel, [shape], [index], [value, *came, *later])


def split_kernel(index_ref, *refs):
    *grad_refs, kept_first, sent_first, kept_second, sent_second = refs
    half, count = kept_first.shape[-1], kept_first.shape[1]
    firsts = ((kept_first, 0), (kept_first, 1), (sent_first, 0), (sent_first, 1))
    seconds = ((kept_second, 0), (sent_second, 0), (kept_second, 1), (sent_second, 1))
    for corner in range(SQUARE):
        for number in range(count):
            row = 0
            for grad_ref in grad_refs:
                block = grad_ref[index_ref[corner * count + number]]
                rows = slice(row, row + block.shape[0])
                row += block.shape[0]
                (target, place), (other, other_place) = firsts[corner], seconds[corner]
                target[place, number, rows, :] = block[:, :half]
                other[other_place, number, rows, :] = block[:, half:]


def sum_split(index, *grads):
    rows = sum(grad.shape[1] for grad in grads)
    shape = (2, grads[0].shape[0] // SQUARE, rows, grads[0].shape[2] // 2)
    shape = jax.ShapeDtypeStruct(shape, grads[0].dtype)
    return whole_call(split_kernel, [shape] * 4, [index], list(grads))


def sum_first(split):
    return swap(split[1], Y), swap(split[3], X)


def low_sum(first, second):
    return (first.astype(jnp.float32) + second.astype(jnp.float32)).astype(jnp.bfloat16)


def add_kernel(kept_first, came_first, kept_second, came_second, *targets):
    for number, (kept, came) in enumerate(((kept_first, came_first), (kept_second, came_second))):
        for place in range(2):
            for block in range(kept.shape[1]):
                targets[2 * number + place][block] = low_sum(kept[place, block], came[place, block])


def sum_later(split, came):
    shape = jax.ShapeDtypeStruct(came[0].shape[1:], jnp.bfloat16)
    arrays = [split[0], came[0], split[2], came[1]]
    first, to_first, second, to_second = whole_call(add_kernel, [shape] * 4, [], arrays)
    return (first, second), (to_first, to_second)


def sum_second(split, came):
    kept, sent = sum_later(split, came)
    return kept, (swap(sent[0], X), swap(sent[1], Y))


def end_kernel(first_ref, came_first, second_ref, came_second, out_ref):
    half = first_ref.shape[-1]
    for block in range(out_ref.shape[0]):
        out_ref[block, :, :half] = low_sum(first_ref[block], came_first[block])
        out_ref[block, :, half:] = low_sum(second_ref[block], came_second[block])


def sum_end(kept, came):
    count, rows, half = kept[0].shape
    shape = jax.ShapeDtypeStruct((count, rows, 2 * half), jnp.bfloat16)
    return whole_call(end_kernel, [shape], [], [kept[0], came[0], kept[1], came[1]])


def in_vmem(count, scalars=1):
    return [pl.BlockSpec(memory_space=pltpu.SMEM)] * scalars + [
        pl.BlockSpec(memory_space=pltpu.VMEM)
    ] * count


def whole_call(kernel, shapes, scalars, arrays, scratch=(), megabytes=40, cost=None):
    specs = [pl.BlockSpec(memory_space=pltpu.VMEM)] * len(shapes)
    single = len(shapes) == 1
    size = sum(array.size * array.dtype.itemsize for array in arrays)
    return pl.pallas_call(
        kernel,
        out_shape=shapes[0] if single else shapes,
        in_specs=in_vmem(len(arrays), len(scalars)),
        out_specs=specs[0] if single else specs,
        scratch_shapes=list(scratch),
        compiler_params=pltpu.CompilerParams(vmem_limit_bytes=megabytes * 2**20),
        cost_estimate=cost or pl.CostEstimate(flops=0, bytes_accessed=2 * size, transcendentals=0),
    )(*scalars, *arrays)


def column_start(columns, parts, place, part, core):
    return pl.multiple_of(place * (columns // LINE) + part * 2 * SHARE + core * SHARE, SHARE)


def pick_kernel(parts, core_ref, *refs):
    *weight_refs, block_ref = refs
    columns = weight_refs[0].shape[1]
    for place in range(LINE):
        for number, weight_ref in enumerate(weight_refs):
            for part in range(parts):
                start = column_start(columns, parts, place, part, core_ref[0])
                lane = (number * parts + part) * SHARE
                block_ref[place, :ROWS, lane : lane + SHARE] = weight_ref[:, pl.ds(start, SHARE)]


def pick_more_kernel(parts, core_ref, *refs):
    *weight_refs, more_ref, block_ref = refs
    pick_kernel(parts, core_ref, *weight_refs, block_ref)
    for place in range(LINE):
        for lane in range(0, block_ref.shape[2], HEAD):
            block_ref[place, ROWS:, lane : lane + HEAD] = more_ref[...]


def spread_kernel(parts, core_ref, mine_ref, came_ref, place_ref, *grad_refs):
    columns = grad_refs[0].shape[1]
    for slot in range(LINE):
        for number, grad_ref in enumerate(grad_refs):
            for part in range(parts):
                lane = (number * parts + part) * SHARE
                for source, core in ((mine_ref, core_ref[0]), (came_ref, 1 - core_ref[0])):
                    start = column_start(columns, parts, place_ref[slot], part, core)
                    grad_ref[:, pl.ds(start, SHARE)] = source[slot, :, lane : lane + SHARE].astype(
                        jnp.float32
                    )


def spread_scalars_kernel(parts, core_ref, place_ref, mine_ref, came_ref, *grad_refs):
    spread_kernel(parts, core_ref, mine_ref, came_ref, place_ref, *grad_refs)


def pick_columns(core_ref, weights, parts, more=None):
    rows, columns = weights[0].shape
    extra = [] if more is None else [more]
    rows += sum(array.shape[0] for array in extra)
    shape = jax.ShapeDtypeStruct((LINE, rows, len(weights) * columns // 8), jnp.bfloat16)
    kernel = functools.partial(pick_more_kernel if extra else pick_kernel, parts)
    return whole_call(kernel, [shape], [core_ref], [*weights, *extra])


def spread_columns(core_ref, place_ref, mine, came, count, parts):
    shape = jax.ShapeDtypeStruct((mine.shape[1], 8 * mine.shape[2] // count), jnp.float32)
    kernel = functools.partial(spread_scalars_kernel, parts)
    return whole_call(kernel, [shape] * count, [core_ref, place_ref], [mine, came])


def gated_grad_kernel(grad_ref, both_ref, out_ref):
    width = grad_ref.shape[1]
    gate, up, grad = both_ref[:, :width], both_ref[:, width:], grad_ref[...]
    sigma = 1.0 / (1.0 + jnp.exp(-gate))
    out_ref[:, :width] = (grad * up * sigma * (1.0 + gate * (1.0 - sigma))).astype(jnp.bfloat16)
    out_ref[:, width:] = (grad * gate * sigma).astype(jnp.bfloat16)


def gated_grad(grad, both):
    rows, width = grad.shape
    narrow, wide = (pl.BlockSpec((ROWS, w), lambda i: (i, 0)) for w in (width, 2 * width))
    return pl.pallas_call(
        gated_grad_kernel,
        out_shape=jax.ShapeDtypeStruct(both.shape, jnp.bfloat16),
        grid=(rows // ROWS,),
        in_specs=[narrow, wide],
        out_specs=wide,
        compiler_params=pltpu.CompilerParams(vmem_limit_bytes=32 * 2**20),
        cost_estimate=pl.CostEstimate(
            flops=20 * grad.size, bytes_accessed=16 * grad.size, transcendentals=grad.size
        ),
    )(grad, both)


def head_lanes(head):
    return slice(head * HEAD, (head + 1) * HEAD)


def halo_slots(place):
    return lax.rem(place + 2, LINE), lax.rem(place + 1, LINE)


def rotated(value, cosines, sines):
    return value * cosines + pltpu.roll(value, HEAD // 2, 1) * sines


def rotated_back(value, cosines, sines):
    return value * cosines - pltpu.roll(value, HEAD // 2, 1) * sines


def part_of(group, core):
    return core if group == 0 else 1 - core


def pack_kernel(core_ref, place_ref, raw_ref, scale_ref, gain_ref, cos_ref, sin_ref, out_ref):
    for group in range(2):
        part = part_of(group, core_ref[0])
        for head in range(2):
            target = 2 * group + head
            for slot in range(LINE):
                for number in range(2):
                    lanes = slice((2 * number + head) * HEAD, (2 * number + head + 1) * HEAD)
                    value = raw_ref[part, slot, :, lanes] * scale_ref[number, part, slot]
                    value = value * gain_ref[number : number + 1, head_lanes(head)]
                    value = rotated(value, cos_ref[part, slot], sin_ref[part, slot])
                    out_ref[target, LINE * number + slot] = value.astype(jnp.bfloat16)
                lanes = slice((4 + head) * HEAD, (5 + head) * HEAD)
                out_ref[target, 2 * LINE + slot] = raw_ref[part, slot, :, lanes].astype(jnp.bfloat16)
    for target in range(SQUARE):
        for number, slot in enumerate(halo_slots(place_ref[0])):
            out_ref[target, 12 + number] = out_ref[target % 2, LINE + slot]
            out_ref[target, 14 + number] = out_ref[target % 2, 2 * LINE + slot]


def unpack_kernel(core_ref, came_ref, out_ref):
    for group in range(2):
        part = core_ref[0] if group == 0 else 1 - core_ref[0]
        for head in range(2):
            for slot in range(LINE):
                out_ref[part, slot, :, head_lanes(head)] = came_ref[2 * group + head, slot]


def pack_grad_kernel(core_ref, grad_ref, out_ref):
    for group in range(2):
        part = core_ref[0] if group == 0 else 1 - core_ref[0]
        for head in range(2):
            for slot in range(LINE):
                out_ref[2 * group + head, slot] = grad_ref[part, slot, :, head_lanes(head)]


def unpack_grad_kernel(
    core_ref,
    place_ref,
    came_ref,
    raw_ref,
    scale_ref,
    gain_ref,
    cos_ref,
    sin_ref,
    grad_ref,
    value_ref,
    sums_ref,
    gain_grad_ref,
):
    core = core_ref[0]

    def summed(first, part, slot, head):
        total = came_ref[2 * part_of(part, core) + head, first + slot].astype(jnp.float32)
        for number, end_slot in enumerate(halo_slots(place_ref[0])):
            here = jnp.where((core == part) & (end_slot == slot), 1.0, 0.0)
            total += here * came_ref[2 + head, 10 + first // 2 + number].astype(jnp.float32)
        return total

    totals = [[jnp.zeros((1, HEAD), jnp.float32) for _ in range(2)] for _ in range(2)]
    for part in range(2):
        for slot in range(LINE):
            sums = [jnp.zeros((ROWS, 1), jnp.float32) for _ in range(2)]
            for head in range(2):
                lanes = head_lanes(head)
                value_ref[part, slot, :, lanes] = summed(8, part, slot, head).astype(jnp.bfloat16)
                d_query = came_ref[2 * part_of(part, core) + head, slot].astype(jnp.float32)
                for number, grad in ((0, d_query), (1, summed(4, part, slot, head))):
                    grad = rotated_back(grad, cos_ref[part, slot], sin_ref[part, slot])
                    raw_lanes = slice((2 * number + head) * HEAD, (2 * number + head + 1) * HEAD)
                    raw = raw_ref[part, slot, :, raw_lanes]
                    totals[number][head] += jnp.sum(
                        grad * raw * scale_ref[number, part, slot], axis=0, keepdims=True
                    )
                    grad = grad * gain_ref[number : number + 1, lanes]
                    sums[number] += jnp.sum(grad * raw, axis=1, keepdims=True)
                    grad_ref[number, part, slot, :, lanes] = grad
            for number in range(2):
                sums_ref[number, part, slot] = sums[number]
    for number in range(2):
        for head in range(2):
            gain_grad_ref[number : number + 1, head_lanes(head)] = totals[number][head]


def norm_grad_kernel(grad_ref, value_ref, raw_ref, scale_ref, mean_ref, out_ref):
    for part in range(2):
        for slot in range(LINE):
            for number in range(2):
                lanes = slice(2 * number * HEAD, 2 * (number + 1) * HEAD)
                scale = scale_ref[number, part, slot]
                grad = grad_ref[number, part, slot] * scale - raw_ref[part, slot, :, lanes] * (
                    scale * scale * scale * mean_ref[number, part, slot]
                )
                out_ref[part, slot, :, lanes] = grad.astype(jnp.bfloat16)
            out_ref[part, slot, :, 4 * HEAD :] = value_ref[part, slot]


def visible_of(seen):
    shape = (seen.shape[0], DOC_LEN + seen.shape[0])
    row = lax.broadcasted_iota(jnp.int32, shape, 0)
    column = lax.broadcasted_iota(jnp.int32, shape, 1)
    distance = row - column + DOC_LEN
    return (distance >= 0) & (distance <= seen)


def dot_last(left, right):
    return lax.dot_general(
        left, right, (((1,), (1,)), ((), ())), preferred_element_type=jnp.float32
    )


def stream_row(place, source, slot):
    block = lax.rem(place - slot + LINE, LINE) * SQUARE + source
    return block, pl.multiple_of(block * ROWS, ROWS)


def rows_at(start):
    return pl.ds(pl.multiple_of(start, ROWS), ROWS)


def fill(place, message_ref, keys, values):
    for source in range(SQUARE):
        for slot in range(LINE):
            _, start = stream_row(place, source, slot)
            keys[rows_at(start + DOC_LEN), :] = message_ref[source, LINE + slot]
            values[rows_at(start + DOC_LEN), :] = message_ref[source, 2 * LINE + slot]
        for number in range(2):
            start = (number * SQUARE + source) * ROWS
            keys[start : start + ROWS, :] = message_ref[source, 12 + number]
            values[start : start + ROWS, :] = message_ref[source, 14 + number]


def attend_kernel(place_ref, message_ref, pos_ref, o_ref, lse_ref, keys, values):
    place = place_ref[0]
    fill(place, message_ref, keys, values)

    def step(number, carry):
        count, rows_of = 2, 2 * ROWS
        first, slot = count * (number // LINE), number % LINE
        sources = pl.ds(first, count)
        block, start = stream_row(place, first, slot)
        rows = pl.ds(start, DOC_LEN + rows_of)
        query = message_ref[sources, slot].reshape(rows_of, HEAD)
        scores = dot_last(query, keys[rows, :]) * SCALING
        seen = pos_ref[pl.ds(block, count)].reshape(rows_of, 1)
        masked = jnp.where(visible_of(seen), scores, -jnp.inf)
        top = jnp.max(masked, axis=-1, keepdims=True)
        expo = jnp.exp(masked - top)
        total = jnp.sum(expo, axis=-1, keepdims=True)
        probs = (expo * (1.0 / total)).astype(jnp.bfloat16)
        mixed = jnp.dot(probs, values[rows, :], preferred_element_type=jnp.float32)
        o_ref[sources, slot] = mixed.astype(jnp.bfloat16).reshape(count, ROWS, HEAD)
        lse_ref[pl.ds(block, count)] = (top + jnp.log(total)).reshape(count, ROWS, 1)
        return carry

    lax.fori_loop(0, BLOCKS // 2, step, 0)


def attend_back_kernel(
    place_ref, message_ref, pos_ref, lse_ref, do_ref, out_ref, keys, values, d_keys, d_values
):
    place = place_ref[0]
    fill(place, message_ref, keys, values)
    d_keys[...] = jnp.zeros_like(d_keys)
    d_values[...] = jnp.zeros_like(d_values)

    def step(number, carry):
        count, rows_of = 4, 4 * ROWS
        first, slot = count * (number // LINE), number % LINE
        sources = pl.ds(first, count)
        block, start = stream_row(place, first, slot)
        rows = pl.ds(start, DOC_LEN + rows_of)
        query = message_ref[sources, slot].reshape(rows_of, HEAD)
        grad = do_ref[sources, slot].reshape(rows_of, HEAD)
        key, value = keys[rows, :], values[rows, :]
        scores = dot_last(query, key) * SCALING
        seen = pos_ref[pl.ds(block, count)].reshape(rows_of, 1)
        lse = lse_ref[pl.ds(block, count)].reshape(rows_of, 1)
        probs = jnp.where(visible_of(seen), jnp.exp(scores - lse), 0.0)
        d_probs = dot_last(grad, value)
        inner = jnp.sum(probs * d_probs, axis=-1, keepdims=True)
        d_scores = (probs * (d_probs - inner) * SCALING).astype(jnp.bfloat16)
        d_query = jnp.dot(d_scores, key, preferred_element_type=jnp.float32)
        out_ref[sources, slot] = d_query.astype(jnp.bfloat16).reshape(count, ROWS, HEAD)
        d_keys[rows, :] += along_first(d_scores, query)
        d_values[rows, :] += along_first(probs.astype(jnp.bfloat16), grad)
        return carry

    lax.fori_loop(0, BLOCKS // 4, step, 0)
    for source in range(SQUARE):
        for slot in range(LINE):
            _, start = stream_row(place, source, slot)
            out_ref[source, LINE + slot] = d_keys[rows_at(start + DOC_LEN), :].astype(jnp.bfloat16)
            out_ref[source, 2 * LINE + slot] = d_values[rows_at(start + DOC_LEN), :].astype(jnp.bfloat16)
        for number in range(2):
            start = (number * SQUARE + source) * ROWS
            out_ref[source, 12 + number] = d_keys[start : start + ROWS, :].astype(jnp.bfloat16)
            out_ref[source, 14 + number] = d_values[start : start + ROWS, :].astype(jnp.bfloat16)


KEPT = [pltpu.VMEM((3 * DOC_LEN, HEAD), jnp.bfloat16)] * 2
SUMMED = [pltpu.VMEM((3 * DOC_LEN, HEAD), jnp.float32)] * 2


def attend(place_ref, message, positions):
    shapes = [
        jax.ShapeDtypeStruct((SQUARE, LINE, ROWS, HEAD), jnp.bfloat16),
        jax.ShapeDtypeStruct((BLOCKS, ROWS, 1), jnp.float32),
    ]
    return whole_call(attend_kernel, shapes, [place_ref], [message, positions], KEPT)


def attend_back(place_ref, message, positions, lse, grad):
    shape = jax.ShapeDtypeStruct(message.shape, jnp.bfloat16)
    arrays = [message, positions, lse, grad]
    return whole_call(attend_back_kernel, [shape], [place_ref], arrays, KEPT + SUMMED)


def turn_square(message):
    return lax.all_to_all(message, "shard", 0, 0, tiled=True, axis_index_groups=SQUARES)


def turned_kernel(place_ref, block_ref, *refs):
    came_refs, (whole_ref, first_ref, second_ref) = refs[: LINE - 1], refs[LINE - 1 :]
    half = whole_ref.shape[-1] // 2
    own_ref = block_ref.at[place_ref[0]]
    for slot, ref in enumerate((own_ref, *came_refs)):
        whole_ref[slot] = ref[...]
        first_ref[slot] = ref[:, :half]
        second_ref[slot] = ref[:, half:]


def turned_line(place_ref, block, came):
    half = jax.ShapeDtypeStruct(block.shape[:-1] + (block.shape[-1] // 2,), block.dtype)
    whole = jax.ShapeDtypeStruct(block.shape, block.dtype)
    whole, *parts = whole_call(turned_kernel, [whole, half, half], [place_ref], [block, *came])
    return whole, parts


def local_line(
    inputs,
    positions,
    cotangent,
    w_query,
    w_key,
    w_value,
    w_out,
    query_gain,
    key_gain,
    attn_gain,
    w_gate,
    w_up,
    w_down,
    mlp_gain,
):
    bf16, f32 = jnp.bfloat16, jnp.float32
    width = inputs.shape[1]
    core_index = lax.axis_index("grp")
    shard_index = lax.axis_index("shard")
    core = core_index == 1
    place, corner = line_place(), square_place()
    core_ref = core_index.astype(jnp.int32).reshape(1)
    place_ref = place.astype(jnp.int32).reshape(1)
    slots = jnp.arange(LINE, dtype=jnp.int32)
    slot_places = (place - slots) % LINE
    hidden = w_down.shape[0] * 2
    tokens = 2 * LINE * ROWS
    part_tokens = tokens // 2
    heads = 2 * HEAD
    from_slots = (slot_places[None, :] * SQUARE + (corner ^ slots)[:, None]).reshape(-1)
    from_order = (slots[None, :] * SQUARE + (corner ^ slots)[:, None]).reshape(-1)
    from_corner = corner ^ slots

    def region(function, *given):
        shapes = jax.eval_shape(function, *given)
        empty = lambda *given: jax.tree.map(lambda leaf: jnp.zeros(leaf.shape, leaf.dtype), shapes)
        return lax.cond(positions[0] >= 0, function, empty, *given)

    def across_cores(left, right, product):
        other = swap_core(product(left[1], right).astype(bf16))
        own = together(product(left[0], right).astype(bf16))[0]
        return add_low(own, other)

    def parts_of(value):
        return value[:part_tokens], value[part_tokens:]

    def dot(left, right):
        return jnp.dot(left, right, preferred_element_type=f32)

    small = jnp.concatenate(
        [
            jnp.stack([query_gain, key_gain, attn_gain, mlp_gain]),
            jnp.stack([positions // 32, positions % 32]).astype(bf16),
            jnp.zeros((10, ROWS), bf16),
        ]
    )
    down_own = lax.dynamic_index_in_dim(w_down.reshape(2, 1, hidden // SQUARE, width), core_index, 0, keepdims=False)
    rows_own = jnp.concatenate([w_out[None], down_own], axis=1)
    head_block, rows_came = run(
        one(pick_columns(core_ref, (w_query, w_key, w_value), 1, small), turn_line),
        square_track(rows_own),
    )
    x_came, head_came = run(gather_first(inputs), square_track(head_block))
    x_own, head_later, rows_parts = run(
        gather_second(*x_came),
        second_track(head_block, head_came),
        one((rows_own, rows_came), lambda given: second_parts(*given)),
    )
    rows_later = swap(rows_parts[0], Y), swap(rows_parts[1], X)
    head_block = square_join(from_order, head_block, head_came, head_later)
    qkv_w = head_block[:, :ROWS].reshape(width, 3 * heads)
    gains = head_block[:, ROWS : ROWS + 4, :HEAD].astype(f32)
    first_head = place * SQUARE + core_index * 2
    head_gain = lax.dynamic_slice_in_dim(gains, first_head, 2, 0)[:, :2].transpose(1, 0, 2).reshape(2, heads)
    gains = gains.transpose(1, 0, 2).reshape(4, width)
    stream = head_block[:, ROWS + 4 : ROWS + 6, :HEAD].astype(jnp.int32)
    stream = stream[:, 0] * 32 + stream[:, 1]
    stream_other = swap_core(stream)
    query_places = jnp.where((corner >= 2) == core, stream, stream_other).reshape(BLOCKS, ROWS, 1)
    held = [
        to_slots(lax.dynamic_index_in_dim(part.reshape(LINE, SQUARE, ROWS), corner, 1, keepdims=False))
        for part in (stream, stream_other)
    ]
    middle = HEAD // 2
    frequency = jnp.power(500000.0, -2.0 * (jnp.arange(HEAD) % middle).astype(f32) / HEAD)
    def sums_track(value):
        for bit in (Z, FAR):
            (came,) = yield [(value, along(bit))]
            value = value + came
        (came,) = yield [(value, swap_core)]
        return value + jnp.flip(came, 2)

    def row_sums(sums):
        return to_slots(sums.transpose(2, 0, 1, 3))

    def row_means(sums):
        return to_slots(sums).transpose(1, 2, 0, 3)[..., None] / width

    def projected(x_own, qkv_w, *held):
        x_other = swap_core(x_own)
        raw = jnp.stack([dot(x_own, qkv_w), dot(x_other, qkv_w)]).reshape(2, LINE, ROWS, 3 * heads)
        squares = raw[..., : 2 * heads] * raw[..., : 2 * heads]
        sums = jnp.stack([jnp.sum(squares[..., :heads], axis=-1), jnp.sum(squares[..., heads:], axis=-1)])
        angles = jnp.stack(held).astype(f32)[..., None] * frequency
        sign = jnp.where(jnp.arange(HEAD) < middle, -1.0, 1.0)
        return x_other, raw, alone(sums_track(row_sums(sums))), jnp.cos(angles), jnp.sin(angles) * sign

    x_other, raw, sums, cosines, sines = region(projected, x_own, qkv_w, *held)
    raw, rows_later = together(raw, rows_later)
    scales = lax.rsqrt(row_means(sums) + 1e-06)

    hidden_block = hold(pick_columns(core_ref, (w_gate, w_up), SQUARE), sums)
    line_came = [
        line_step(k)(lax.dynamic_index_in_dim(hidden_block, (place + k) % LINE, 0, keepdims=False))
        for k in range(1, LINE)
    ]
    shape = (2, LINE, ROWS, heads)
    message_shape = jax.ShapeDtypeStruct((SQUARE, 16, ROWS, HEAD), bf16)
    heads_shape = jax.ShapeDtypeStruct((SQUARE, LINE, ROWS, HEAD), bf16)
    tokens_shape = jax.ShapeDtypeStruct(shape, bf16)

    tables = [head_gain, cosines, sines]

    def attended(raw, scales, *tables):
        message = whole_call(
            pack_kernel, [message_shape], [core_ref, place_ref], [raw, scales, *tables]
        )
        message = turn_square(message)
        mixed, lse = attend(place_ref, message, query_places)
        mixed = whole_call(unpack_kernel, [tokens_shape], [core_ref], [turn_square(mixed)])
        rows_w = square_join(from_corner, rows_own, rows_came, rows_later)
        return message, lse, mixed.reshape(tokens, heads), rows_w

    message, lse, mixed, rows_w = region(attended, raw, scales, *tables)
    mixed, line_came = together(mixed, line_came)
    out_w = lax.dynamic_slice(rows_w, (core_index * 2, 0, 0), (2, ROWS, width)).reshape(heads, width)
    hidden_own, parts = turned_line(place_ref, hidden_block, line_came)
    hidden_came = swap(parts[0], X), swap(parts[1], Y)

    branch = across_cores(parts_of(mixed), out_w, dot)
    branch, down_w = region(
        lambda total, rows: (alone(scatter_line(total)), rows[:, ROWS:].reshape(-1, width)), branch, rows_w
    )
    branch, hidden_came = together(branch, hidden_came)
    hidden_later = square_second(hidden_own, hidden_came)

    def state_of(branch):
        branch_scale = lax.rsqrt(jnp.mean(branch * branch, axis=-1, keepdims=True) + 1e-06)
        hidden_state = inputs.astype(f32) + branch * branch_scale * gains[2]
        state = alone(gather_line(hidden_state.astype(bf16)))
        return branch_scale, hidden_state, state

    branch_scale, hidden_state, state = region(state_of, branch)
    state, hidden_later = together(state, hidden_later)
    hidden_w = square_join(from_slots, hidden_own, hidden_came, hidden_later).reshape(width, -1)

    state = (state, swap_core(state))
    both = [dot(part, hidden_w) for part in state]
    active = [(jax.nn.silu(in_two(part)[0]) * in_two(part)[1]).astype(bf16) for part in both]
    mlp, (state, both, active) = run(
        scatter_line(across_cores(active, down_w, dot)),
        one((state, both, active), lambda pairs: [join(*pair) for pair in pairs]),
    )
    mlp_scale = lax.rsqrt(jnp.mean(mlp * mlp, axis=-1, keepdims=True) + 1e-06)
    cot = cotangent.astype(f32)
    scaled = cot * gains[3]
    d_mlp = mlp_scale * scaled - mlp * mlp_scale**3 * jnp.mean(mlp * scaled, axis=-1, keepdims=True)

    def finished(given):
        cotangent, hidden_state, mlp, mlp_scale = given
        normed = mlp * mlp_scale
        output = (hidden_state + normed * gains[3]).astype(bf16)
        return output, jnp.sum(cotangent.astype(f32) * normed, axis=0)

    d_mlp, (output, mlp_gain_part) = run(
        gather_line(d_mlp.astype(bf16)), one((cotangent, hidden_state, mlp, mlp_scale), finished)
    )
    d_mlp = both_cores(d_mlp)

    d_both = gated_grad(along_last(d_mlp, down_w), both)

    total = across_cores(parts_of(d_both), hidden_w, along_last)

    def d_state_begun(total, state, d_both):
        carried = alone(scatter_first(total))
        hidden_grad = along_first(state, d_both).astype(bf16).reshape(BLOCKS, ROWS, -1)
        return carried, sum_split(from_order, hidden_grad)

    carried, hidden_split = region(d_state_begun, total, state, d_both)
    hidden_came = sum_first(hidden_split)

    def d_branch_begun(total, carried):
        d_resid = cotangent.astype(f32) + alone(scatter_second(total, *carried))
        scaled = d_resid * gains[2]
        d_branch = branch_scale * scaled - branch * branch_scale**3 * jnp.mean(
            branch * scaled, axis=-1, keepdims=True
        )
        return d_resid, alone(gather_first(d_branch.astype(bf16)))

    def d_branch_of(d_branch, d_resid):
        d_branch = (d_branch, swap_core(d_branch))
        norms = jnp.stack([jnp.sum(d_resid * branch * branch_scale, axis=0), mlp_gain_part])
        return d_branch, jnp.stack([along_last(part, out_w).astype(bf16) for part in d_branch]), norms

    d_resid, d_branch = region(d_branch_begun, total, carried)
    d_branch, hidden_came = together(d_branch, hidden_came)
    hidden_kept, hidden_came = sum_second(hidden_split, hidden_came)
    d_branch, d_mixed, norms = region(d_branch_of, alone(gather_second(*d_branch)), d_resid)
    d_mixed, hidden_came = together(d_mixed, hidden_came)
    hidden_grad = sum_end(hidden_kept, hidden_came)
    line_came = [
        line_step(k)(lax.dynamic_index_in_dim(hidden_grad, (place + k) % LINE, 0, keepdims=False))
        for k in range(1, LINE)
    ]

    def attended_back(d_mixed, message, lse, d_branch, mixed, active, d_mlp, raw, scales, *tables):
        grad = whole_call(pack_grad_kernel, [heads_shape], [core_ref], [d_mixed.reshape(shape)])
        grads = attend_back(place_ref, message, query_places, lse, turn_square(grad))
        grads = turn_square(grads)
        down_grad = along_first(active, d_mlp).astype(bf16).reshape(SQUARE, -1, width)
        out_grad = sum(along_first(*pair) for pair in zip(parts_of(mixed), d_branch))
        out_grad = out_grad.reshape(1, 2, ROWS, width)
        out_grad = jnp.where(core == jnp.arange(2).reshape(2, 1, 1, 1), out_grad, 0.0).astype(bf16)
        shapes = [
            jax.ShapeDtypeStruct((2,) + shape, f32),
            tokens_shape,
            jax.ShapeDtypeStruct((2, 2, LINE, ROWS, 1), f32),
            jax.ShapeDtypeStruct((2, heads), f32),
        ]
        return (
            whole_call(
                unpack_grad_kernel,
                shapes,
                [core_ref, place_ref],
                [grads, raw, scales, *tables],
            ),
            sum_split(from_corner, out_grad.reshape(SQUARE, ROWS, width), down_grad),
        )

    (d_head, d_value, sums, head_part), rows_split = region(
        attended_back, d_mixed, message, lse, d_branch, mixed, active, d_mlp, raw, scales, *tables
    )
    d_head, sums, line_came = together(d_head, sums, line_came)
    hidden_grad, _ = turned_line(place_ref, hidden_grad, line_came)
    hidden_other = swap_core(hidden_grad)
    rows_grads_came = sum_first(rows_split)

    head_part = head_part.reshape(2, 1, 2, HEAD)
    head_part = jnp.where(core == jnp.arange(2).reshape(1, 2, 1, 1), head_part, 0.0)

    def gain_sums(norms, heads):
        for bit in (Z, FAR):
            (came,) = yield [(norms, along(bit))]
            norms = norms + came
        both = jnp.concatenate([norms.reshape(-1, ROWS), heads.reshape(-1, ROWS)])
        (came,) = yield [(both, swap_core)]
        return both + came

    def gains_to(bit):
        return lambda value: value + swap(value, bit)

    def d_qkv_of(sums, head_part, norms, d_head, d_value, raw, scales, *x_parts):
        sums, gain_grads, x_all = run(
            sums_track(row_sums(sums.reshape(2, 2, LINE, ROWS))),
            gain_sums(norms, head_part),
            one(x_parts, lambda parts: join(*parts)),
        )
        qkv_shape = jax.ShapeDtypeStruct(raw.shape, bf16)
        arrays = [d_head, d_value, raw, scales, row_means(sums)]
        d_qkv = whole_call(norm_grad_kernel, [qkv_shape], [], arrays).reshape(tokens, -1)
        total = across_cores(parts_of(d_qkv), qkv_w, along_last)
        qkv_grad = along_first(x_all, d_qkv).astype(bf16)
        qkv_grad = with_layout_constraint(qkv_grad, Layout(major_to_minor=(0, 1)))
        return total, sum_split(from_order, qkv_grad.reshape(BLOCKS, ROWS, -1)), gain_grads

    total, qkv_split, gain_grads = region(
        d_qkv_of, sums, head_part, norms, d_head, d_value, raw, scales, x_own, x_other
    )
    total, rows_grads_came = together(total, rows_grads_came)
    def first_track(split):
        return (yield [(split[1], along(Y)), (split[3], along(X))])

    def later_track(split, came):
        kept, (first, second) = sum_later(split, came)
        came = yield [(first, along(X)), (second, along(Y))]
        return sum_end(kept, came)

    def inputs_begun(total, split, hidden_grad, hidden_other, rows_split, rows_came):
        hidden_grads = spread_columns(core_ref, slot_places, hidden_grad, hidden_other, 2, SQUARE)
        rows_grads = sum_later(rows_split, rows_came)
        return run(scatter_first(total), first_track(split)), hidden_grads, rows_grads

    (carried, qkv_came), (gate_grad, up_grad), rows_grads = region(
        inputs_begun, total, qkv_split, hidden_grad, hidden_other, rows_split, rows_grads_came
    )
    def inputs_ended(total, *carried):
        return d_resid + (yield from scatter_second(total, *carried))

    input_grad, qkv_grad = region(
        lambda total, carried, split, came: (
            alone(inputs_ended(total, *carried)),
            alone(later_track(split, came)),
        ),
        total,
        carried,
        qkv_split,
        qkv_came,
    )
    qkv_grad = turn_line(qkv_grad)

    def rows_ended(kept, sent, gain_grads):
        *came, gain_grads = yield [(sent[0], along(X)), (sent[1], along(Y)), (gain_grads, gains_to(X))]
        mine = jnp.concatenate([add_low(*pair) for pair in zip(kept, came)], axis=-1)[0]
        other, gain_grads = yield [(mine, swap_core), (gain_grads, gains_to(Y))]
        out_grad = mine[:ROWS].astype(f32) + other[:ROWS].astype(f32)
        mine, other = mine[ROWS:], other[ROWS:]
        down_grad = jnp.concatenate([jnp.where(core, other, mine), jnp.where(core, mine, other)])
        return out_grad, down_grad.astype(f32), gain_grads

    rows_grads, gain_grads = hold((rows_grads, gain_grads), input_grad)
    out_grad, down_grad, gain_grads = region(
        lambda grads, gains: alone(rows_ended(*grads, gains)), rows_grads, gain_grads
    )
    qkv_grad, out_grad = together(qkv_grad, out_grad)
    qkv_other = swap_core(qkv_grad)
    norms, head_grads = (
        lax.dynamic_index_in_dim(part.reshape(2, -1, ROWS), number, 1, keepdims=False)
        for part, number in ((gain_grads[: 2 * BLOCKS], shard_index), (gain_grads[2 * BLOCKS :], corner))
    )
    query_grad, key_grad, value_grad = spread_columns(core_ref, slots, qkv_grad, qkv_other, 3, 1)
    return (
        output,
        input_grad,
        query_grad,
        key_grad,
        value_grad,
        out_grad,
        head_grads[0],
        head_grads[1],
        norms[0],
        gate_grad,
        up_grad,
        down_grad,
        norms[1],
    )


def solution(mesh):
    on_line = mesh.shape["grp"] == 2 and mesh.shape["shard"] == 16
    placed = (
        P(("grp", "shard"), None),
        P(("grp", "shard")),
        P(("grp", "shard"), None),
        P("shard", None),
        P("shard", None),
        P("shard", None),
        P("shard", None),
        P("shard"),
        P("shard"),
        P("shard"),
        P("shard", None),
        P("shard", None),
        P("shard", None),
        P("shard"),
    )
    return jax.shard_map(
        local_line if on_line else local_general,
        mesh=mesh,
        in_specs=placed,
        out_specs=(
            P(("grp", "shard"), None),
            P(("grp", "shard"), None),
            P("shard", None),
            P("shard", None),
            P("shard", None),
            P("shard", None),
            P("shard"),
            P("shard"),
            P("shard"),
            P("shard", None),
            P("shard", None),
            P("shard", None),
            P("shard"),
        ),
        check_vma=False,
    )
```

```python
import functools
import math

import jax
import jax.numpy as jnp
from jax import lax
from jax.experimental import pallas as pl
from jax.experimental.layout import Layout, with_layout_constraint
from jax.experimental.pallas import tpu as pltpu
from jax.sharding import PartitionSpec as P

HEADS = 16
HEAD = 128
DOC_LEN = 1024


def from_behind(value, axis, steps):
    count = lax.axis_size(axis)
    leading, last = (max(0, -steps), min(count, count - steps))
    return lax.ppermute(value, axis, [(source, source + steps) for source in range(leading, last)])


def norm_rows(values, scales):
    return values * lax.rsqrt(jnp.mean(values * values, axis=-1, keepdims=True) + 1e-06) * scales


def rotate(values, cosines, sines):
    row_count = values.shape[0]
    middle = HEAD // 2
    shaped = values.reshape(row_count, HEADS, HEAD)
    first_half = shaped[..., :middle]
    second_half = shaped[..., middle:]
    turned = jnp.concatenate(
        [first_half * cosines - second_half * sines, second_half * cosines + first_half * sines],
        axis=-1,
    )
    return turned.reshape(row_count, HEADS * HEAD)


def activate(gate_in, up_in):
    return jax.nn.silu(gate_in) * up_in


def along_last(left, right):
    return lax.dot_general(
        left, right, (((1,), (1,)), ((), ())), preferred_element_type=jnp.float32
    )


def along_first(left, right):
    return lax.dot_general(
        left, right, (((0,), (0,)), ((), ())), preferred_element_type=jnp.float32
    )


def reduce_three(first_term, second_term, third_term):
    return (
        lax.psum_scatter(first_term, "shard", scatter_dimension=0, tiled=True),
        lax.psum_scatter(second_term, "shard", scatter_dimension=0, tiled=True),
        lax.psum_scatter(third_term, "shard", scatter_dimension=0, tiled=True),
    )


def local_general(
    inputs,
    positions,
    cotangent,
    w_query,
    w_key,
    w_value,
    w_out,
    query_gain,
    key_gain,
    attn_gain,
    w_gate,
    w_up,
    w_down,
    mlp_gain,
):
    row_count, feature_width = inputs.shape
    reach_back = (DOC_LEN - 2) // row_count + 1
    span_rows = min(row_count, 512)
    key_rows = span_rows + reach_back * row_count
    scaling = 1.0 / math.sqrt(HEAD)
    middle = HEAD // 2
    frequency = jnp.power(500000.0, -2.0 * jnp.arange(middle).astype(jnp.float32) / HEAD)
    angles = positions.astype(jnp.float32)[:, None] * frequency[None, :]
    cosines = jnp.cos(angles)[:, None, :]
    sines = jnp.sin(angles)[:, None, :]
    pieces = (
        lax.all_gather(w_query, "shard", axis=0, tiled=True),
        lax.all_gather(w_key, "shard", axis=0, tiled=True),
        lax.all_gather(w_value, "shard", axis=0, tiled=True),
        lax.all_gather(w_out, "shard", axis=0, tiled=True),
        lax.all_gather(query_gain, "shard", axis=0, tiled=True),
        lax.all_gather(key_gain, "shard", axis=0, tiled=True),
        lax.all_gather(attn_gain, "shard", axis=0, tiled=True),
        lax.all_gather(mlp_gain, "shard", axis=0, tiled=True),
    )
    columns_in = inputs
    acc_query = jnp.dot(columns_in, pieces[0], preferred_element_type=jnp.float32)
    acc_key = jnp.dot(columns_in, pieces[1], preferred_element_type=jnp.float32)
    acc_value = jnp.dot(columns_in, pieces[2], preferred_element_type=jnp.float32)
    out_full = pieces[3]
    gain_block = jnp.stack([pieces[4], pieces[5], pieces[6], pieces[7]]).astype(jnp.float32)
    gain_table = gain_block
    q_raw, k_raw, v_raw, out_full, gain_table = (
        acc_query,
        acc_key,
        acc_value,
        out_full,
        gain_table,
    )

    def prepare(query_in, key_in, query_scale, key_scale):
        return (
            rotate(norm_rows(query_in, query_scale), cosines, sines),
            rotate(norm_rows(key_in, key_scale), cosines, sines),
        )

    rotated, prepare_pull = jax.vjp(prepare, q_raw, k_raw, gain_table[0], gain_table[1])
    query_low = rotated[0].astype(jnp.bfloat16)
    key_value = jnp.stack([rotated[1].astype(jnp.bfloat16), v_raw.astype(jnp.bfloat16)])
    earlier = [
        from_behind(key_value, ("grp", "shard"), distance_back)
        for distance_back in range(reach_back, 0, -1)
    ]
    key_window = jnp.concatenate(earlier + [key_value], axis=1)
    distance = (
        jnp.arange(span_rows)[:, None] + reach_back * row_count - jnp.arange(key_rows)[None, :]
    )

    def block_scores(block_start):
        query_block = query_low.reshape(span_rows, HEADS, HEAD)
        key_block = key_window[0, block_start : block_start + key_rows].reshape(
            key_rows, HEADS, HEAD
        )
        value_block = key_window[1, block_start : block_start + key_rows].reshape(
            key_rows, HEADS, HEAD
        )
        visible = (distance >= 0) & (distance <= positions[:, None])
        scores = (
            jnp.einsum("qhd,khd->hqk", query_block, key_block, preferred_element_type=jnp.float32)
            * scaling
        )
        return (query_block, key_block, value_block, visible, scores)

    block_start = 0
    query_block, key_block, value_block, visible, scores = block_scores(block_start)
    masked = jnp.where(visible[None], scores, -jnp.inf)
    top_score = jnp.max(masked, axis=-1, keepdims=True)
    expo = jnp.exp(masked - top_score)
    totals = jnp.sum(expo, axis=-1, keepdims=True)
    probs_low = (expo / totals).astype(jnp.bfloat16)
    lse_parts = [top_score + jnp.log(totals)]
    mixed = jnp.einsum("hqk,khd->qhd", probs_low, value_block, preferred_element_type=jnp.float32)
    mixed_parts = mixed.reshape(span_rows, feature_width)
    mixed_low = mixed_parts.astype(jnp.bfloat16)
    branch = jnp.dot(mixed_low, out_full, preferred_element_type=jnp.float32)
    branch_normed, attn_pull = jax.vjp(norm_rows, branch, gain_table[2])
    hidden_state = inputs.astype(jnp.float32) + branch_normed
    state_low = hidden_state.astype(jnp.bfloat16)
    pieces = (
        lax.all_gather(w_gate, "shard", axis=0, tiled=True),
        lax.all_gather(w_up, "shard", axis=0, tiled=True),
    )
    columns_in = state_low
    gate_val = jnp.dot(columns_in, pieces[0], preferred_element_type=jnp.float32)
    up_val = jnp.dot(columns_in, pieces[1], preferred_element_type=jnp.float32)
    activated, act_pull = jax.vjp(activate, gate_val, up_val)
    activated_low = activated.astype(jnp.bfloat16)
    columns_in = activated_low
    mlp_out = jnp.dot(
        columns_in,
        lax.all_gather(w_down, "shard", axis=0, tiled=True),
        preferred_element_type=jnp.float32,
    )
    mlp_normed, mlp_pull = jax.vjp(norm_rows, mlp_out, gain_table[3])
    output = (hidden_state + mlp_normed).astype(jnp.bfloat16)
    cot_float = cotangent.astype(jnp.float32)
    d_mlp, d_mlp_gain = mlp_pull(cot_float)
    d_mlp_low = d_mlp.astype(jnp.bfloat16)
    d_hidden = along_last(d_mlp_low, lax.all_gather(w_down, "shard", axis=0, tiled=True))
    d_gate, d_up = act_pull(d_hidden)
    d_gate_low = d_gate.astype(jnp.bfloat16)
    d_up_low = d_up.astype(jnp.bfloat16)
    pieces = lax.all_gather((w_gate, w_up), "shard", axis=0, tiled=True)
    d_state = along_last(d_gate_low, pieces[0]) + along_last(d_up_low, pieces[1])
    d_resid = cot_float + d_state
    gate_term = along_first(state_low, d_gate_low)
    up_term = along_first(state_low, d_up_low)
    down_term = along_first(activated_low, d_mlp_low)
    ffn_sums = reduce_three(gate_term, up_term, down_term)
    d_branch, d_attn_gain = attn_pull(d_resid)
    d_branch_low = d_branch.astype(jnp.bfloat16)
    d_mixed_low = along_last(
        d_branch_low, lax.all_gather(w_out, "shard", axis=0, tiled=True)
    ).astype(jnp.bfloat16)
    dq_parts = []
    grad_window = jnp.zeros((2, (reach_back + 1) * row_count, feature_width), jnp.float32)
    for block_number, block_start in enumerate(range(0, row_count, span_rows)):
        query_block, key_block, value_block, visible, scores = block_scores(block_start)
        probs = jnp.where(visible[None], jnp.exp(scores - lse_parts[block_number]), 0.0)
        grad_block = d_mixed_low.reshape(span_rows, HEADS, HEAD)
        d_probs = jnp.einsum(
            "qhd,khd->hqk", grad_block, value_block, preferred_element_type=jnp.float32
        )
        inner = jnp.sum(probs * d_probs, axis=-1, keepdims=True)
        d_scores = (probs * (d_probs - inner) * scaling).astype(jnp.bfloat16)
        dq_block = jnp.einsum(
            "hqk,khd->qhd", d_scores, key_block, preferred_element_type=jnp.float32
        )
        dq_parts.append(dq_block.reshape(span_rows, feature_width))
        d_keys = jnp.einsum(
            "hqk,qhd->khd", d_scores, query_block, preferred_element_type=jnp.float32
        ).reshape(key_rows, feature_width)
        d_values = jnp.einsum(
            "hqk,qhd->khd",
            probs.astype(jnp.bfloat16),
            grad_block,
            preferred_element_type=jnp.float32,
        ).reshape(key_rows, feature_width)
        grad_window = grad_window.at[:, block_start : block_start + key_rows].add(
            jnp.stack([d_keys, d_values])
        )
    own_grads = grad_window[:, reach_back * row_count :]
    for distance_back in range(1, reach_back + 1):
        lower_row = (reach_back - distance_back) * row_count
        own_grads = own_grads + from_behind(
            grad_window[:, lower_row : lower_row + row_count].astype(jnp.bfloat16),
            ("grp", "shard"),
            -distance_back,
        ).astype(jnp.float32)
    d_query_raw, d_key_raw, d_query_gain, d_key_gain = prepare_pull((dq_parts[0], own_grads[0]))
    d_query_low = d_query_raw.astype(jnp.bfloat16)
    d_key_low = d_key_raw.astype(jnp.bfloat16)
    d_value_low = own_grads[1].astype(jnp.bfloat16)
    pieces = lax.all_gather((w_query, w_key, w_value), "shard", axis=0, tiled=True)
    d_inputs = (
        along_last(d_query_low, pieces[0])
        + along_last(d_key_low, pieces[1])
        + along_last(d_value_low, pieces[2])
    )
    input_grad = d_resid + d_inputs
    qkv_term = along_first(inputs, jnp.concatenate([d_query_low, d_key_low, d_value_low], axis=1))
    out_term = along_first(mixed_low, d_branch_low)
    gain_term = jnp.stack([d_query_gain, d_key_gain, d_attn_gain, d_mlp_gain], axis=1)
    attn_sums = reduce_three(qkv_term, out_term, gain_term)
    gate_sum, up_sum, down_sum, qkv_sum, out_sum, gain_sum = (
        lax.psum(ffn_sums[0].astype(jnp.bfloat16), "grp").astype(jnp.float32),
        lax.psum(ffn_sums[1].astype(jnp.bfloat16), "grp").astype(jnp.float32),
        lax.psum(ffn_sums[2].astype(jnp.bfloat16), "grp").astype(jnp.float32),
        lax.psum(attn_sums[0].astype(jnp.bfloat16), "grp").astype(jnp.float32),
        lax.psum(attn_sums[1].astype(jnp.bfloat16), "grp").astype(jnp.float32),
        lax.psum(attn_sums[2].astype(jnp.bfloat16), "grp").astype(jnp.float32),
    )
    return (
        output,
        input_grad,
        qkv_sum[:, :feature_width],
        qkv_sum[:, feature_width : 2 * feature_width],
        qkv_sum[:, 2 * feature_width :],
        out_sum,
        gain_sum[:, 0],
        gain_sum[:, 1],
        gain_sum[:, 2],
        gate_sum,
        up_sum,
        down_sum,
        gain_sum[:, 3],
    )


LINE = 4
SQUARE = 4
X, Y, Z, FAR = 1, 2, 4, 8
ROWS = 128
BLOCKS = 16
SHARE = 256
SCALING = 1.0 / math.sqrt(HEAD)
LINES = [[SQUARE * z + r for z in range(LINE)] for r in range(SQUARE)]
SQUARES = [[SQUARE * z + r for r in range(SQUARE)] for z in range(LINE)]


def swap(value, bit):
    return lax.ppermute(value, "shard", [(source, source ^ bit) for source in range(BLOCKS)])


def swap_core(value):
    return lax.ppermute(value, "grp", [(0, 1), (1, 0)])


def along(bit):
    return lambda value: swap(value, bit)


def line_place():
    return lax.axis_index("shard") // SQUARE


def square_place():
    return lax.axis_index("shard") % SQUARE


def line_move(pairs):
    pairs = [(SQUARE * z + r, SQUARE * to + r) for z, to in pairs for r in range(SQUARE)]
    return lambda value: lax.ppermute(value, "shard", pairs)


RIGHT, LEFT = ((0, 1), (1, 2), (2, 3)), ((3, 2), (2, 1), (1, 0))


def line_step(distance):
    pairs = [(s, (s + SQUARE * distance) % BLOCKS) for s in range(BLOCKS)]
    return lambda value: lax.ppermute(value, "shard", pairs)


def hold(values, *later):
    return lax.optimization_barrier((values, later))[0]


def together(*values):
    return lax.optimization_barrier(values)


def run(*tracks):
    live, results = {}, {}

    def advance(name, generator, came):
        try:
            live[name] = (generator, generator.send(came))
        except StopIteration as end:
            live.pop(name, None)
            results[name] = end.value

    for name, generator in enumerate(tracks):
        advance(name, generator, None)
    while live:
        requests = [request for _, asked in live.values() for request in asked]
        given = lax.optimization_barrier(tuple(value for value, _ in requests))
        came = [move(value) for value, (_, move) in zip(given, requests)]
        came = list(lax.optimization_barrier(tuple(came)))
        for name, (generator, asked) in list(live.items()):
            mine, came = came[: len(asked)], came[len(asked) :]
            advance(name, generator, mine)
    return [results[name] for name in range(len(tracks))]


def one(value, move):
    (came,) = yield [(value, move)]
    return came


def alone(track):
    return run(track)[0]


def gather_first(value):
    right, left = yield [(value, line_move(RIGHT)), (value, line_move(LEFT))]
    return value, right, left


def gather_second(value, right, left):
    place = line_place()
    further = jnp.where(place == 1, right, left)
    rights, lefts, further = yield [
        (right, line_move(RIGHT[1:])),
        (left, line_move(LEFT[1:])),
        (further, line_move(((1, 3), (2, 0)))),
    ]
    rows, width = value.shape
    shape = jax.ShapeDtypeStruct((LINE * rows, width), value.dtype)
    arrays = [value, right, left, rights, lefts, further]
    return whole_call(gather_kernel, [shape], [place.astype(jnp.int32).reshape(1)], arrays)


def gather_kernel(place_ref, own_ref, right_ref, left_ref, rights_ref, lefts_ref, further_ref, out_ref):
    place, rows = place_ref[0], own_ref.shape[0]

    def put(slot, condition, ref):
        @pl.when(condition)
        def _():
            out_ref[slot * rows : (slot + 1) * rows, :] = ref[...]

    out_ref[:rows, :] = own_ref[...]
    put(1, place >= 1, right_ref)
    put(1, place == 0, further_ref)
    put(2, place >= 2, rights_ref)
    put(2, place < 2, lefts_ref)
    put(3, place == 3, further_ref)
    put(3, place < 3, left_ref)


def gather_line(value):
    came = yield from gather_first(value)
    return (yield from gather_second(*came))


def join_kernel(own_ref, other_ref, out_ref):
    rows = own_ref.shape[0]
    out_ref[:rows, :] = own_ref[...]
    out_ref[rows:, :] = other_ref[...]


def join(own, other):
    shape = jax.ShapeDtypeStruct((2 * own.shape[0], own.shape[1]), own.dtype)
    return whole_call(join_kernel, [shape], [], [own, other])


def both_cores(own):
    return join(own, swap_core(own))


def scatter_first(total):
    parts = total.reshape(LINE, -1, total.shape[-1])
    further = jnp.where(line_place() == 0, parts[1], parts[3])
    return (
        yield [
            (parts[2], line_move(RIGHT[:2])),
            (parts[2], line_move(LEFT[:2])),
            (further, line_move(((0, 2), (3, 1)))),
        ]
    )


def scatter_second(total, right, left, further):
    parts = total.reshape(LINE, -1, total.shape[-1])
    place, nothing = line_place(), jnp.zeros((), total.dtype)
    right, left = yield [
        (add_low(parts[3], right, jnp.where(place == 2, further, nothing)), line_move(RIGHT)),
        (add_low(parts[1], left, jnp.where(place == 1, further, nothing)), line_move(LEFT)),
    ]
    return add_wide(parts[0], right, left)


def scatter_line(total):
    came = yield from scatter_first(total)
    return (yield from scatter_second(total, *came))


def add_wide(*values):
    return sum(value.astype(jnp.float32) for value in values)


def add_low(*values):
    return add_wide(*values).astype(jnp.bfloat16)


def turn_line(block):
    return lax.all_to_all(block, "shard", 0, 0, tiled=True, axis_index_groups=LINES)


def to_slots(value):
    place = line_place()
    return jnp.stack(
        [lax.dynamic_index_in_dim(value, (place - k) % LINE, 0, keepdims=False) for k in range(LINE)]
    )


def in_two(value):
    return jnp.split(value, 2, axis=-1)


def square_first(value):
    first, second = in_two(value)
    return swap(first, X), swap(second, Y)


def square_track(value):
    came = yield [(part, along(bit)) for part, bit in zip(in_two(value), (X, Y))]
    return tuple(came)


def second_kernel(own_ref, first_ref, second_ref, to_first_ref, to_second_ref):
    half = own_ref.shape[-1] // 2
    to_first_ref[0] = own_ref[..., :half]
    to_first_ref[1] = first_ref[...]
    to_second_ref[0] = own_ref[..., half:]
    to_second_ref[1] = second_ref[...]


def second_parts(value, came):
    shape = jax.ShapeDtypeStruct((2,) + came[0].shape, value.dtype)
    return whole_call(second_kernel, [shape] * 2, [], [value, *came])


def square_second(value, came):
    first, second = second_parts(value, came)
    return swap(first, Y), swap(second, X)


def second_track(value, came):
    first, second = second_parts(value, came)
    later = yield [(first, along(Y)), (second, along(X))]
    return tuple(later)


def square_kernel(index_ref, own_ref, first_ref, second_ref, firsts_ref, seconds_ref, out_ref):
    half, count = own_ref.shape[-1] // 2, own_ref.shape[0]
    firsts = (own_ref, first_ref, firsts_ref.at[0], firsts_ref.at[1])
    seconds = (own_ref, seconds_ref.at[0], second_ref, seconds_ref.at[1])
    for corner in range(SQUARE):
        for number in range(count):
            target = index_ref[corner * count + number]
            out_ref[target, :, :half] = firsts[corner][number, :, :half]
            lanes = slice(half, None) if corner == 0 else slice(None)
            out_ref[target, :, half:] = seconds[corner][number, :, lanes]


def square_join(index, value, came, later):
    count, rows, width = value.shape
    shape = jax.ShapeDtypeStruct((SQUARE * count, rows, width), value.dtype)
    return whole_call(square_kernel, [shape], [index], [value, *came, *later])


def split_kernel(index_ref, *refs):
    *grad_refs, kept_first, sent_first, kept_second, sent_second = refs
    half, count = kept_first.shape[-1], kept_first.shape[1]
    firsts = ((kept_first, 0), (kept_first, 1), (sent_first, 0), (sent_first, 1))
    seconds = ((kept_second, 0), (sent_second, 0), (kept_second, 1), (sent_second, 1))
    for corner in range(SQUARE):
        for number in range(count):
            row = 0
            for grad_ref in grad_refs:
                block = grad_ref[index_ref[corner * count + number]]
                rows = slice(row, row + block.shape[0])
                row += block.shape[0]
                (target, place), (other, other_place) = firsts[corner], seconds[corner]
                target[place, number, rows, :] = block[:, :half]
                other[other_place, number, rows, :] = block[:, half:]


def sum_split(index, *grads):
    rows = sum(grad.shape[1] for grad in grads)
    shape = (2, grads[0].shape[0] // SQUARE, rows, grads[0].shape[2] // 2)
    shape = jax.ShapeDtypeStruct(shape, grads[0].dtype)
    return whole_call(split_kernel, [shape] * 4, [index], list(grads))


def sum_first(split):
    return swap(split[1], Y), swap(split[3], X)


def low_sum(first, second):
    return (first.astype(jnp.float32) + second.astype(jnp.float32)).astype(jnp.bfloat16)


def add_kernel(kept_first, came_first, kept_second, came_second, *targets):
    for number, (kept, came) in enumerate(((kept_first, came_first), (kept_second, came_second))):
        for place in range(2):
            for block in range(kept.shape[1]):
                targets[2 * number + place][block] = low_sum(kept[place, block], came[place, block])


def sum_later(split, came):
    shape = jax.ShapeDtypeStruct(came[0].shape[1:], jnp.bfloat16)
    arrays = [split[0], came[0], split[2], came[1]]
    first, to_first, second, to_second = whole_call(add_kernel, [shape] * 4, [], arrays)
    return (first, second), (to_first, to_second)


def sum_second(split, came):
    kept, sent = sum_later(split, came)
    return kept, (swap(sent[0], X), swap(sent[1], Y))


def end_kernel(first_ref, came_first, second_ref, came_second, out_ref):
    half = first_ref.shape[-1]
    for block in range(out_ref.shape[0]):
        out_ref[block, :, :half] = low_sum(first_ref[block], came_first[block])
        out_ref[block, :, half:] = low_sum(second_ref[block], came_second[block])


def sum_end(kept, came):
    count, rows, half = kept[0].shape
    shape = jax.ShapeDtypeStruct((count, rows, 2 * half), jnp.bfloat16)
    return whole_call(end_kernel, [shape], [], [kept[0], came[0], kept[1], came[1]])


def in_vmem(count, scalars=1):
    return [pl.BlockSpec(memory_space=pltpu.SMEM)] * scalars + [
        pl.BlockSpec(memory_space=pltpu.VMEM)
    ] * count


def whole_call(kernel, shapes, scalars, arrays, scratch=(), megabytes=40, cost=None):
    specs = [pl.BlockSpec(memory_space=pltpu.VMEM)] * len(shapes)
    single = len(shapes) == 1
    size = sum(array.size * array.dtype.itemsize for array in arrays)
    return pl.pallas_call(
        kernel,
        out_shape=shapes[0] if single else shapes,
        in_specs=in_vmem(len(arrays), len(scalars)),
        out_specs=specs[0] if single else specs,
        scratch_shapes=list(scratch),
        compiler_params=pltpu.CompilerParams(vmem_limit_bytes=megabytes * 2**20),
        cost_estimate=cost or pl.CostEstimate(flops=0, bytes_accessed=2 * size, transcendentals=0),
    )(*scalars, *arrays)


def column_start(columns, parts, place, part, core):
    return pl.multiple_of(place * (columns // LINE) + part * 2 * SHARE + core * SHARE, SHARE)


def pick_kernel(parts, core_ref, *refs):
    *weight_refs, block_ref = refs
    columns = weight_refs[0].shape[1]
    for place in range(LINE):
        for number, weight_ref in enumerate(weight_refs):
            for part in range(parts):
                start = column_start(columns, parts, place, part, core_ref[0])
                lane = (number * parts + part) * SHARE
                block_ref[place, :ROWS, lane : lane + SHARE] = weight_ref[:, pl.ds(start, SHARE)]


def pick_more_kernel(parts, core_ref, *refs):
    *weight_refs, more_ref, block_ref = refs
    pick_kernel(parts, core_ref, *weight_refs, block_ref)
    for place in range(LINE):
        for lane in range(0, block_ref.shape[2], HEAD):
            block_ref[place, ROWS:, lane : lane + HEAD] = more_ref[...]


def spread_kernel(parts, core_ref, mine_ref, came_ref, place_ref, *grad_refs):
    columns = grad_refs[0].shape[1]
    for slot in range(LINE):
        for number, grad_ref in enumerate(grad_refs):
            for part in range(parts):
                lane = (number * parts + part) * SHARE
                for source, core in ((mine_ref, core_ref[0]), (came_ref, 1 - core_ref[0])):
                    start = column_start(columns, parts, place_ref[slot], part, core)
                    grad_ref[:, pl.ds(start, SHARE)] = source[slot, :, lane : lane + SHARE].astype(
                        jnp.float32
                    )


def spread_scalars_kernel(parts, core_ref, place_ref, mine_ref, came_ref, *grad_refs):
    spread_kernel(parts, core_ref, mine_ref, came_ref, place_ref, *grad_refs)


def pick_columns(core_ref, weights, parts, more=None):
    rows, columns = weights[0].shape
    extra = [] if more is None else [more]
    rows += sum(array.shape[0] for array in extra)
    shape = jax.ShapeDtypeStruct((LINE, rows, len(weights) * columns // 8), jnp.bfloat16)
    kernel = functools.partial(pick_more_kernel if extra else pick_kernel, parts)
    return whole_call(kernel, [shape], [core_ref], [*weights, *extra])


def spread_columns(core_ref, place_ref, mine, came, count, parts):
    shape = jax.ShapeDtypeStruct((mine.shape[1], 8 * mine.shape[2] // count), jnp.float32)
    kernel = functools.partial(spread_scalars_kernel, parts)
    return whole_call(kernel, [shape] * count, [core_ref, place_ref], [mine, came])


def gated_grad_kernel(grad_ref, both_ref, out_ref):
    width = grad_ref.shape[1]
    gate, up, grad = both_ref[:, :width], both_ref[:, width:], grad_ref[...]
    sigma = 1.0 / (1.0 + jnp.exp(-gate))
    out_ref[:, :width] = (grad * up * sigma * (1.0 + gate * (1.0 - sigma))).astype(jnp.bfloat16)
    out_ref[:, width:] = (grad * gate * sigma).astype(jnp.bfloat16)


def gated_grad(grad, both):
    rows, width = grad.shape
    narrow, wide = (pl.BlockSpec((ROWS, w), lambda i: (i, 0)) for w in (width, 2 * width))
    return pl.pallas_call(
        gated_grad_kernel,
        out_shape=jax.ShapeDtypeStruct(both.shape, jnp.bfloat16),
        grid=(rows // ROWS,),
        in_specs=[narrow, wide],
        out_specs=wide,
        compiler_params=pltpu.CompilerParams(vmem_limit_bytes=32 * 2**20),
        cost_estimate=pl.CostEstimate(
            flops=20 * grad.size, bytes_accessed=16 * grad.size, transcendentals=grad.size
        ),
    )(grad, both)


def head_lanes(head):
    return slice(head * HEAD, (head + 1) * HEAD)


def halo_slots(place):
    return lax.rem(place + 2, LINE), lax.rem(place + 1, LINE)


def rotated(value, cosines, sines):
    return value * cosines + pltpu.roll(value, HEAD // 2, 1) * sines


def rotated_back(value, cosines, sines):
    return value * cosines - pltpu.roll(value, HEAD // 2, 1) * sines


def part_of(group, core):
    return core if group == 0 else 1 - core


def pack_kernel(core_ref, place_ref, raw_ref, scale_ref, gain_ref, cos_ref, sin_ref, out_ref):
    for group in range(2):
        part = part_of(group, core_ref[0])
        for head in range(2):
            target = 2 * group + head
            for slot in range(LINE):
                for number in range(2):
                    lanes = slice((2 * number + head) * HEAD, (2 * number + head + 1) * HEAD)
                    value = raw_ref[part, slot, :, lanes] * scale_ref[number, part, slot]
                    value = value * gain_ref[number : number + 1, head_lanes(head)]
                    value = rotated(value, cos_ref[part, slot], sin_ref[part, slot])
                    out_ref[target, LINE * number + slot] = value.astype(jnp.bfloat16)
                lanes = slice((4 + head) * HEAD, (5 + head) * HEAD)
                out_ref[target, 2 * LINE + slot] = raw_ref[part, slot, :, lanes].astype(jnp.bfloat16)
    for target in range(SQUARE):
        for number, slot in enumerate(halo_slots(place_ref[0])):
            out_ref[target, 12 + number] = out_ref[target % 2, LINE + slot]
            out_ref[target, 14 + number] = out_ref[target % 2, 2 * LINE + slot]


def unpack_kernel(core_ref, came_ref, out_ref):
    for group in range(2):
        part = core_ref[0] if group == 0 else 1 - core_ref[0]
        for head in range(2):
            for slot in range(LINE):
                out_ref[part, slot, :, head_lanes(head)] = came_ref[2 * group + head, slot]


def pack_grad_kernel(core_ref, grad_ref, out_ref):
    for group in range(2):
        part = core_ref[0] if group == 0 else 1 - core_ref[0]
        for head in range(2):
            for slot in range(LINE):
                out_ref[2 * group + head, slot] = grad_ref[part, slot, :, head_lanes(head)]


def unpack_grad_kernel(
    core_ref,
    place_ref,
    came_ref,
    raw_ref,
    scale_ref,
    gain_ref,
    cos_ref,
    sin_ref,
    grad_ref,
    value_ref,
    sums_ref,
    gain_grad_ref,
):
    core = core_ref[0]

    def summed(first, part, slot, head):
        total = came_ref[2 * part_of(part, core) + head, first + slot].astype(jnp.float32)
        for number, end_slot in enumerate(halo_slots(place_ref[0])):
            here = jnp.where((core == part) & (end_slot == slot), 1.0, 0.0)
            total += here * came_ref[2 + head, 10 + first // 2 + number].astype(jnp.float32)
        return total

    totals = [[jnp.zeros((1, HEAD), jnp.float32) for _ in range(2)] for _ in range(2)]
    for part in range(2):
        for slot in range(LINE):
            sums = [jnp.zeros((ROWS, 1), jnp.float32) for _ in range(2)]
            for head in range(2):
                lanes = head_lanes(head)
                value_ref[part, slot, :, lanes] = summed(8, part, slot, head).astype(jnp.bfloat16)
                d_query = came_ref[2 * part_of(part, core) + head, slot].astype(jnp.float32)
                for number, grad in ((0, d_query), (1, summed(4, part, slot, head))):
                    grad = rotated_back(grad, cos_ref[part, slot], sin_ref[part, slot])
                    raw_lanes = slice((2 * number + head) * HEAD, (2 * number + head + 1) * HEAD)
                    raw = raw_ref[part, slot, :, raw_lanes]
                    totals[number][head] += jnp.sum(
                        grad * raw * scale_ref[number, part, slot], axis=0, keepdims=True
                    )
                    grad = grad * gain_ref[number : number + 1, lanes]
                    sums[number] += jnp.sum(grad * raw, axis=1, keepdims=True)
                    grad_ref[number, part, slot, :, lanes] = grad
            for number in range(2):
                sums_ref[number, part, slot] = sums[number]
    for number in range(2):
        for head in range(2):
            gain_grad_ref[number : number + 1, head_lanes(head)] = totals[number][head]


def norm_grad_kernel(grad_ref, value_ref, raw_ref, scale_ref, mean_ref, out_ref):
    for part in range(2):
        for slot in range(LINE):
            for number in range(2):
                lanes = slice(2 * number * HEAD, 2 * (number + 1) * HEAD)
                scale = scale_ref[number, part, slot]
                grad = grad_ref[number, part, slot] * scale - raw_ref[part, slot, :, lanes] * (
                    scale * scale * scale * mean_ref[number, part, slot]
                )
                out_ref[part, slot, :, lanes] = grad.astype(jnp.bfloat16)
            out_ref[part, slot, :, 4 * HEAD :] = value_ref[part, slot]


def visible_of(seen):
    shape = (seen.shape[0], DOC_LEN + seen.shape[0])
    row = lax.broadcasted_iota(jnp.int32, shape, 0)
    column = lax.broadcasted_iota(jnp.int32, shape, 1)
    distance = row - column + DOC_LEN
    return (distance >= 0) & (distance <= seen)


def dot_last(left, right):
    return lax.dot_general(
        left, right, (((1,), (1,)), ((), ())), preferred_element_type=jnp.float32
    )


def stream_row(place, source, slot):
    block = lax.rem(place - slot + LINE, LINE) * SQUARE + source
    return block, pl.multiple_of(block * ROWS, ROWS)


def rows_at(start):
    return pl.ds(pl.multiple_of(start, ROWS), ROWS)


def fill(place, message_ref, keys, values):
    for source in range(SQUARE):
        for slot in range(LINE):
            _, start = stream_row(place, source, slot)
            keys[rows_at(start + DOC_LEN), :] = message_ref[source, LINE + slot]
            values[rows_at(start + DOC_LEN), :] = message_ref[source, 2 * LINE + slot]
        for number in range(2):
            start = (number * SQUARE + source) * ROWS
            keys[start : start + ROWS, :] = message_ref[source, 12 + number]
            values[start : start + ROWS, :] = message_ref[source, 14 + number]


def attend_kernel(place_ref, message_ref, pos_ref, o_ref, lse_ref, keys, values):
    place = place_ref[0]
    fill(place, message_ref, keys, values)

    def step(number, carry):
        count, rows_of = 2, 2 * ROWS
        first, slot = count * (number // LINE), number % LINE
        sources = pl.ds(first, count)
        block, start = stream_row(place, first, slot)
        rows = pl.ds(start, DOC_LEN + rows_of)
        query = message_ref[sources, slot].reshape(rows_of, HEAD)
        scores = dot_last(query, keys[rows, :]) * SCALING
        seen = pos_ref[pl.ds(block, count)].reshape(rows_of, 1)
        masked = jnp.where(visible_of(seen), scores, -jnp.inf)
        top = jnp.max(masked, axis=-1, keepdims=True)
        expo = jnp.exp(masked - top)
        total = jnp.sum(expo, axis=-1, keepdims=True)
        probs = (expo * (1.0 / total)).astype(jnp.bfloat16)
        mixed = jnp.dot(probs, values[rows, :], preferred_element_type=jnp.float32)
        o_ref[sources, slot] = mixed.astype(jnp.bfloat16).reshape(count, ROWS, HEAD)
        lse_ref[pl.ds(block, count)] = (top + jnp.log(total)).reshape(count, ROWS, 1)
        return carry

    lax.fori_loop(0, BLOCKS // 2, step, 0)


def attend_back_kernel(
    place_ref, message_ref, pos_ref, lse_ref, do_ref, out_ref, keys, values, d_keys, d_values
):
    place = place_ref[0]
    fill(place, message_ref, keys, values)
    d_keys[...] = jnp.zeros_like(d_keys)
    d_values[...] = jnp.zeros_like(d_values)

    def step(number, carry):
        count, rows_of = 4, 4 * ROWS
        first, slot = count * (number // LINE), number % LINE
        sources = pl.ds(first, count)
        block, start = stream_row(place, first, slot)
        rows = pl.ds(start, DOC_LEN + rows_of)
        query = message_ref[sources, slot].reshape(rows_of, HEAD)
        grad = do_ref[sources, slot].reshape(rows_of, HEAD)
        key, value = keys[rows, :], values[rows, :]
        scores = dot_last(query, key) * SCALING
        seen = pos_ref[pl.ds(block, count)].reshape(rows_of, 1)
        lse = lse_ref[pl.ds(block, count)].reshape(rows_of, 1)
        probs = jnp.where(visible_of(seen), jnp.exp(scores - lse), 0.0)
        d_probs = dot_last(grad, value)
        inner = jnp.sum(probs * d_probs, axis=-1, keepdims=True)
        d_scores = (probs * (d_probs - inner) * SCALING).astype(jnp.bfloat16)
        d_query = jnp.dot(d_scores, key, preferred_element_type=jnp.float32)
        out_ref[sources, slot] = d_query.astype(jnp.bfloat16).reshape(count, ROWS, HEAD)
        d_keys[rows, :] += along_first(d_scores, query)
        d_values[rows, :] += along_first(probs.astype(jnp.bfloat16), grad)
        return carry

    lax.fori_loop(0, BLOCKS // 4, step, 0)
    for source in range(SQUARE):
        for slot in range(LINE):
            _, start = stream_row(place, source, slot)
            out_ref[source, LINE + slot] = d_keys[rows_at(start + DOC_LEN), :].astype(jnp.bfloat16)
            out_ref[source, 2 * LINE + slot] = d_values[rows_at(start + DOC_LEN), :].astype(jnp.bfloat16)
        for number in range(2):
            start = (number * SQUARE + source) * ROWS
            out_ref[source, 12 + number] = d_keys[start : start + ROWS, :].astype(jnp.bfloat16)
            out_ref[source, 14 + number] = d_values[start : start + ROWS, :].astype(jnp.bfloat16)


KEPT = [pltpu.VMEM((3 * DOC_LEN, HEAD), jnp.bfloat16)] * 2
SUMMED = [pltpu.VMEM((3 * DOC_LEN, HEAD), jnp.float32)] * 2


def attend(place_ref, message, positions):
    shapes = [
        jax.ShapeDtypeStruct((SQUARE, LINE, ROWS, HEAD), jnp.bfloat16),
        jax.ShapeDtypeStruct((BLOCKS, ROWS, 1), jnp.float32),
    ]
    return whole_call(attend_kernel, shapes, [place_ref], [message, positions], KEPT)


def attend_back(place_ref, message, positions, lse, grad):
    shape = jax.ShapeDtypeStruct(message.shape, jnp.bfloat16)
    arrays = [message, positions, lse, grad]
    return whole_call(attend_back_kernel, [shape], [place_ref], arrays, KEPT + SUMMED)


def turn_square(message):
    return lax.all_to_all(message, "shard", 0, 0, tiled=True, axis_index_groups=SQUARES)


def turned_kernel(place_ref, block_ref, *refs):
    came_refs, (whole_ref, first_ref, second_ref) = refs[: LINE - 1], refs[LINE - 1 :]
    half = whole_ref.shape[-1] // 2
    own_ref = block_ref.at[place_ref[0]]
    for slot, ref in enumerate((own_ref, *came_refs)):
        whole_ref[slot] = ref[...]
        first_ref[slot] = ref[:, :half]
        second_ref[slot] = ref[:, half:]


def turned_line(place_ref, block, came):
    half = jax.ShapeDtypeStruct(block.shape[:-1] + (block.shape[-1] // 2,), block.dtype)
    whole = jax.ShapeDtypeStruct(block.shape, block.dtype)
    whole, *parts = whole_call(turned_kernel, [whole, half, half], [place_ref], [block, *came])
    return whole, parts


def local_line(
    inputs,
    positions,
    cotangent,
    w_query,
    w_key,
    w_value,
    w_out,
    query_gain,
    key_gain,
    attn_gain,
    w_gate,
    w_up,
    w_down,
    mlp_gain,
):
    bf16, f32 = jnp.bfloat16, jnp.float32
    width = inputs.shape[1]
    core_index = lax.axis_index("grp")
    shard_index = lax.axis_index("shard")
    core = core_index == 1
    place, corner = line_place(), square_place()
    core_ref = core_index.astype(jnp.int32).reshape(1)
    place_ref = place.astype(jnp.int32).reshape(1)
    slots = jnp.arange(LINE, dtype=jnp.int32)
    slot_places = (place - slots) % LINE
    hidden = w_down.shape[0] * 2
    tokens = 2 * LINE * ROWS
    part_tokens = tokens // 2
    heads = 2 * HEAD
    from_slots = (slot_places[None, :] * SQUARE + (corner ^ slots)[:, None]).reshape(-1)
    from_order = (slots[None, :] * SQUARE + (corner ^ slots)[:, None]).reshape(-1)
    from_corner = corner ^ slots

    def region(function, *given):
        shapes = jax.eval_shape(function, *given)
        empty = lambda *given: jax.tree.map(lambda leaf: jnp.zeros(leaf.shape, leaf.dtype), shapes)
        return lax.cond(positions[0] >= 0, function, empty, *given)

    def across_cores(left, right, product):
        other = swap_core(product(left[1], right).astype(bf16))
        own = together(product(left[0], right).astype(bf16))[0]
        return add_low(own, other)

    def parts_of(value):
        return value[:part_tokens], value[part_tokens:]

    def dot(left, right):
        return jnp.dot(left, right, preferred_element_type=f32)

    small = jnp.concatenate(
        [
            jnp.stack([query_gain, key_gain, attn_gain, mlp_gain]),
            jnp.stack([positions // 32, positions % 32]).astype(bf16),
            jnp.zeros((10, ROWS), bf16),
        ]
    )
    down_own = lax.dynamic_index_in_dim(w_down.reshape(2, 1, hidden // SQUARE, width), core_index, 0, keepdims=False)
    rows_own = jnp.concatenate([w_out[None], down_own], axis=1)
    head_block, rows_came = run(
        one(pick_columns(core_ref, (w_query, w_key, w_value), 1, small), turn_line),
        square_track(rows_own),
    )
    x_came, head_came = run(gather_first(inputs), square_track(head_block))
    x_own, head_later, rows_parts = run(
        gather_second(*x_came),
        second_track(head_block, head_came),
        one((rows_own, rows_came), lambda given: second_parts(*given)),
    )
    rows_later = swap(rows_parts[0], Y), swap(rows_parts[1], X)
    head_block = square_join(from_order, head_block, head_came, head_later)
    qkv_w = head_block[:, :ROWS].reshape(width, 3 * heads)
    gains = head_block[:, ROWS : ROWS + 4, :HEAD].astype(f32)
    first_head = place * SQUARE + core_index * 2
    head_gain = lax.dynamic_slice_in_dim(gains, first_head, 2, 0)[:, :2].transpose(1, 0, 2).reshape(2, heads)
    gains = gains.transpose(1, 0, 2).reshape(4, width)
    stream = head_block[:, ROWS + 4 : ROWS + 6, :HEAD].astype(jnp.int32)
    stream = stream[:, 0] * 32 + stream[:, 1]
    stream_other = swap_core(stream)
    query_places = jnp.where((corner >= 2) == core, stream, stream_other).reshape(BLOCKS, ROWS, 1)
    held = [
        to_slots(lax.dynamic_index_in_dim(part.reshape(LINE, SQUARE, ROWS), corner, 1, keepdims=False))
        for part in (stream, stream_other)
    ]
    middle = HEAD // 2
    frequency = jnp.power(500000.0, -2.0 * (jnp.arange(HEAD) % middle).astype(f32) / HEAD)
    def sums_track(value):
        for bit in (Z, FAR):
            (came,) = yield [(value, along(bit))]
            value = value + came
        (came,) = yield [(value, swap_core)]
        return value + jnp.flip(came, 2)

    def row_sums(sums):
        return to_slots(sums.transpose(2, 0, 1, 3))

    def row_means(sums):
        return to_slots(sums).transpose(1, 2, 0, 3)[..., None] / width

    def projected(x_own, qkv_w, *held):
        x_other = swap_core(x_own)
        raw = jnp.stack([dot(x_own, qkv_w), dot(x_other, qkv_w)]).reshape(2, LINE, ROWS, 3 * heads)
        squares = raw[..., : 2 * heads] * raw[..., : 2 * heads]
        sums = jnp.stack([jnp.sum(squares[..., :heads], axis=-1), jnp.sum(squares[..., heads:], axis=-1)])
        angles = jnp.stack(held).astype(f32)[..., None] * frequency
        sign = jnp.where(jnp.arange(HEAD) < middle, -1.0, 1.0)
        return x_other, raw, alone(sums_track(row_sums(sums))), jnp.cos(angles), jnp.sin(angles) * sign

    x_other, raw, sums, cosines, sines = region(projected, x_own, qkv_w, *held)
    scales = lax.rsqrt(row_means(sums) + 1e-06)

    hidden_block = hold(pick_columns(core_ref, (w_gate, w_up), SQUARE), sums)
    line_came = [
        line_step(k)(lax.dynamic_index_in_dim(hidden_block, (place + k) % LINE, 0, keepdims=False))
        for k in range(1, LINE)
    ]
    shape = (2, LINE, ROWS, heads)
    message_shape = jax.ShapeDtypeStruct((SQUARE, 16, ROWS, HEAD), bf16)
    heads_shape = jax.ShapeDtypeStruct((SQUARE, LINE, ROWS, HEAD), bf16)
    tokens_shape = jax.ShapeDtypeStruct(shape, bf16)

    tables = [head_gain, cosines, sines]

    def attended(message):
        message = turn_square(message)
        mixed, lse = attend(place_ref, message, query_places)
        mixed = whole_call(unpack_kernel, [tokens_shape], [core_ref], [turn_square(mixed)])
        rows_w = square_join(from_corner, rows_own, rows_came, rows_later)
        return message, lse, mixed.reshape(tokens, heads), rows_w

    packed = whole_call(pack_kernel, [message_shape], [core_ref, place_ref], [raw, scales, *tables])
    packed, rows_later = together(packed, rows_later)
    message, lse, mixed, rows_w = region(attended, packed)
    mixed, line_came = together(mixed, line_came)
    out_w = lax.dynamic_slice(rows_w, (core_index * 2, 0, 0), (2, ROWS, width)).reshape(heads, width)
    hidden_own, parts = turned_line(place_ref, hidden_block, line_came)
    hidden_came = swap(parts[0], X), swap(parts[1], Y)

    branch = across_cores(parts_of(mixed), out_w, dot)
    branch, down_w = region(
        lambda total, rows: (alone(scatter_line(total)), rows[:, ROWS:].reshape(-1, width)), branch, rows_w
    )
    branch, hidden_came = together(branch, hidden_came)
    hidden_later = square_second(hidden_own, hidden_came)

    def state_of(branch):
        branch_scale = lax.rsqrt(jnp.mean(branch * branch, axis=-1, keepdims=True) + 1e-06)
        hidden_state = inputs.astype(f32) + branch * branch_scale * gains[2]
        state = alone(gather_line(hidden_state.astype(bf16)))
        return branch_scale, hidden_state, state

    branch_scale, hidden_state, state = region(state_of, branch)
    state, hidden_later = together(state, hidden_later)
    hidden_w = square_join(from_slots, hidden_own, hidden_came, hidden_later).reshape(width, -1)

    state = (state, swap_core(state))
    both = [dot(part, hidden_w) for part in state]
    active = [(jax.nn.silu(in_two(part)[0]) * in_two(part)[1]).astype(bf16) for part in both]
    mlp, (state, both, active) = run(
        scatter_line(across_cores(active, down_w, dot)),
        one((state, both, active), lambda pairs: [join(*pair) for pair in pairs]),
    )
    mlp_scale = lax.rsqrt(jnp.mean(mlp * mlp, axis=-1, keepdims=True) + 1e-06)
    cot = cotangent.astype(f32)
    scaled = cot * gains[3]
    d_mlp = mlp_scale * scaled - mlp * mlp_scale**3 * jnp.mean(mlp * scaled, axis=-1, keepdims=True)

    def finished(given):
        cotangent, hidden_state, mlp, mlp_scale = given
        normed = mlp * mlp_scale
        output = (hidden_state + normed * gains[3]).astype(bf16)
        return output, jnp.sum(cotangent.astype(f32) * normed, axis=0)

    d_mlp, (output, mlp_gain_part) = run(
        gather_line(d_mlp.astype(bf16)), one((cotangent, hidden_state, mlp, mlp_scale), finished)
    )
    d_mlp = both_cores(d_mlp)

    d_both = gated_grad(along_last(d_mlp, down_w), both)

    total = across_cores(parts_of(d_both), hidden_w, along_last)

    def d_state_begun(total, state, d_both):
        carried = alone(scatter_first(total))
        hidden_grad = along_first(state, d_both).astype(bf16).reshape(BLOCKS, ROWS, -1)
        return carried, sum_split(from_order, hidden_grad)

    carried, hidden_split = region(d_state_begun, total, state, d_both)
    hidden_came = sum_first(hidden_split)

    def d_branch_begun(total, carried):
        d_resid = cotangent.astype(f32) + alone(scatter_second(total, *carried))
        scaled = d_resid * gains[2]
        d_branch = branch_scale * scaled - branch * branch_scale**3 * jnp.mean(
            branch * scaled, axis=-1, keepdims=True
        )
        return d_resid, alone(gather_first(d_branch.astype(bf16)))

    def d_branch_of(d_branch, d_resid):
        d_branch = (d_branch, swap_core(d_branch))
        norms = jnp.stack([jnp.sum(d_resid * branch * branch_scale, axis=0), mlp_gain_part])
        return d_branch, jnp.stack([along_last(part, out_w).astype(bf16) for part in d_branch]), norms

    d_resid, d_branch = region(d_branch_begun, total, carried)
    d_branch, hidden_came = together(d_branch, hidden_came)
    hidden_kept, hidden_came = sum_second(hidden_split, hidden_came)
    d_branch, d_mixed, norms = region(d_branch_of, alone(gather_second(*d_branch)), d_resid)
    d_mixed, hidden_came = together(d_mixed, hidden_came)
    hidden_grad = sum_end(hidden_kept, hidden_came)
    line_came = [
        line_step(k)(lax.dynamic_index_in_dim(hidden_grad, (place + k) % LINE, 0, keepdims=False))
        for k in range(1, LINE)
    ]

    def attended_back(d_mixed, message, lse, d_branch, mixed, active, d_mlp, raw, scales, *tables):
        grad = whole_call(pack_grad_kernel, [heads_shape], [core_ref], [d_mixed.reshape(shape)])
        grads = attend_back(place_ref, message, query_places, lse, turn_square(grad))
        grads = turn_square(grads)
        down_grad = along_first(active, d_mlp).astype(bf16).reshape(SQUARE, -1, width)
        out_grad = sum(along_first(*pair) for pair in zip(parts_of(mixed), d_branch))
        out_grad = out_grad.reshape(1, 2, ROWS, width)
        out_grad = jnp.where(core == jnp.arange(2).reshape(2, 1, 1, 1), out_grad, 0.0).astype(bf16)
        shapes = [
            jax.ShapeDtypeStruct((2,) + shape, f32),
            tokens_shape,
            jax.ShapeDtypeStruct((2, 2, LINE, ROWS, 1), f32),
            jax.ShapeDtypeStruct((2, heads), f32),
        ]
        return (
            whole_call(
                unpack_grad_kernel,
                shapes,
                [core_ref, place_ref],
                [grads, raw, scales, *tables],
            ),
            sum_split(from_corner, out_grad.reshape(SQUARE, ROWS, width), down_grad),
        )

    (d_head, d_value, sums, head_part), rows_split = region(
        attended_back, d_mixed, message, lse, d_branch, mixed, active, d_mlp, raw, scales, *tables
    )
    d_head, sums, line_came = together(d_head, sums, line_came)
    hidden_grad, _ = turned_line(place_ref, hidden_grad, line_came)
    hidden_other = swap_core(hidden_grad)
    rows_grads_came = sum_first(rows_split)

    head_part = head_part.reshape(2, 1, 2, HEAD)
    head_part = jnp.where(core == jnp.arange(2).reshape(1, 2, 1, 1), head_part, 0.0)

    def gain_sums(norms, heads):
        for bit in (Z, FAR):
            (came,) = yield [(norms, along(bit))]
            norms = norms + came
        both = jnp.concatenate([norms.reshape(-1, ROWS), heads.reshape(-1, ROWS)])
        (came,) = yield [(both, swap_core)]
        return both + came

    def gains_to(bit):
        return lambda value: value + swap(value, bit)

    def d_qkv_of(sums, head_part, norms, d_head, d_value, raw, scales, *x_parts):
        sums, gain_grads, x_all = run(
            sums_track(row_sums(sums.reshape(2, 2, LINE, ROWS))),
            gain_sums(norms, head_part),
            one(x_parts, lambda parts: join(*parts)),
        )
        qkv_shape = jax.ShapeDtypeStruct(raw.shape, bf16)
        arrays = [d_head, d_value, raw, scales, row_means(sums)]
        d_qkv = whole_call(norm_grad_kernel, [qkv_shape], [], arrays).reshape(tokens, -1)
        total = across_cores(parts_of(d_qkv), qkv_w, along_last)
        qkv_grad = along_first(x_all, d_qkv).astype(bf16)
        qkv_grad = with_layout_constraint(qkv_grad, Layout(major_to_minor=(0, 1)))
        return total, sum_split(from_order, qkv_grad.reshape(BLOCKS, ROWS, -1)), gain_grads

    total, qkv_split, gain_grads = region(
        d_qkv_of, sums, head_part, norms, d_head, d_value, raw, scales, x_own, x_other
    )
    total, rows_grads_came = together(total, rows_grads_came)
    def first_track(split):
        return (yield [(split[1], along(Y)), (split[3], along(X))])

    def later_track(split, came):
        kept, (first, second) = sum_later(split, came)
        came = yield [(first, along(X)), (second, along(Y))]
        return sum_end(kept, came)

    def inputs_begun(total, split, hidden_grad, hidden_other, rows_split, rows_came):
        hidden_grads = spread_columns(core_ref, slot_places, hidden_grad, hidden_other, 2, SQUARE)
        rows_grads = sum_later(rows_split, rows_came)
        return run(scatter_first(total), first_track(split)), hidden_grads, rows_grads

    (carried, qkv_came), (gate_grad, up_grad), rows_grads = region(
        inputs_begun, total, qkv_split, hidden_grad, hidden_other, rows_split, rows_grads_came
    )
    def inputs_ended(total, *carried):
        return d_resid + (yield from scatter_second(total, *carried))

    input_grad, qkv_grad = region(
        lambda total, carried, split, came: (
            alone(inputs_ended(total, *carried)),
            alone(later_track(split, came)),
        ),
        total,
        carried,
        qkv_split,
        qkv_came,
    )
    qkv_grad = turn_line(qkv_grad)

    def rows_ended(kept, sent, gain_grads):
        *came, gain_grads = yield [(sent[0], along(X)), (sent[1], along(Y)), (gain_grads, gains_to(X))]
        mine = jnp.concatenate([add_low(*pair) for pair in zip(kept, came)], axis=-1)[0]
        other, gain_grads = yield [(mine, swap_core), (gain_grads, gains_to(Y))]
        out_grad = mine[:ROWS].astype(f32) + other[:ROWS].astype(f32)
        mine, other = mine[ROWS:], other[ROWS:]
        down_grad = jnp.concatenate([jnp.where(core, other, mine), jnp.where(core, mine, other)])
        return out_grad, down_grad.astype(f32), gain_grads

    rows_grads, gain_grads = hold((rows_grads, gain_grads), input_grad)
    out_grad, down_grad, gain_grads = region(
        lambda grads, gains: alone(rows_ended(*grads, gains)), rows_grads, gain_grads
    )
    qkv_grad, out_grad = together(qkv_grad, out_grad)
    qkv_other = swap_core(qkv_grad)
    norms, head_grads = (
        lax.dynamic_index_in_dim(part.reshape(2, -1, ROWS), number, 1, keepdims=False)
        for part, number in ((gain_grads[: 2 * BLOCKS], shard_index), (gain_grads[2 * BLOCKS :], corner))
    )
    query_grad, key_grad, value_grad = spread_columns(core_ref, slots, qkv_grad, qkv_other, 3, 1)
    return (
        output,
        input_grad,
        query_grad,
        key_grad,
        value_grad,
        out_grad,
        head_grads[0],
        head_grads[1],
        norms[0],
        gate_grad,
        up_grad,
        down_grad,
        norms[1],
    )


def solution(mesh):
    on_line = mesh.shape["grp"] == 2 and mesh.shape["shard"] == 16
    placed = (
        P(("grp", "shard"), None),
        P(("grp", "shard")),
        P(("grp", "shard"), None),
        P("shard", None),
        P("shard", None),
        P("shard", None),
        P("shard", None),
        P("shard"),
        P("shard"),
        P("shard"),
        P("shard", None),
        P("shard", None),
        P("shard", None),
        P("shard"),
    )
    return jax.shard_map(
        local_line if on_line else local_general,
        mesh=mesh,
        in_specs=placed,
        out_specs=(
            P(("grp", "shard"), None),
            P(("grp", "shard"), None),
            P("shard", None),
            P("shard", None),
            P("shard", None),
            P("shard", None),
            P("shard"),
            P("shard"),
            P("shard"),
            P("shard", None),
            P("shard", None),
            P("shard", None),
            P("shard"),
        ),
        check_vma=False,
    )
```

```python
import functools
import math

import jax
import jax.numpy as jnp
from jax import lax
from jax.experimental import pallas as pl
from jax.experimental.layout import Layout, with_layout_constraint
from jax.experimental.pallas import tpu as pltpu
from jax.sharding import PartitionSpec as P

HEADS = 16
HEAD = 128
DOC_LEN = 1024


def from_behind(value, axis, steps):
    count = lax.axis_size(axis)
    leading, last = (max(0, -steps), min(count, count - steps))
    return lax.ppermute(value, axis, [(source, source + steps) for source in range(leading, last)])


def norm_rows(values, scales):
    return values * lax.rsqrt(jnp.mean(values * values, axis=-1, keepdims=True) + 1e-06) * scales


def rotate(values, cosines, sines):
    row_count = values.shape[0]
    middle = HEAD // 2
    shaped = values.reshape(row_count, HEADS, HEAD)
    first_half = shaped[..., :middle]
    second_half = shaped[..., middle:]
    turned = jnp.concatenate(
        [first_half * cosines - second_half * sines, second_half * cosines + first_half * sines],
        axis=-1,
    )
    return turned.reshape(row_count, HEADS * HEAD)


def activate(gate_in, up_in):
    return jax.nn.silu(gate_in) * up_in


def along_last(left, right):
    return lax.dot_general(
        left, right, (((1,), (1,)), ((), ())), preferred_element_type=jnp.float32
    )


def along_first(left, right):
    return lax.dot_general(
        left, right, (((0,), (0,)), ((), ())), preferred_element_type=jnp.float32
    )


def reduce_three(first_term, second_term, third_term):
    return (
        lax.psum_scatter(first_term, "shard", scatter_dimension=0, tiled=True),
        lax.psum_scatter(second_term, "shard", scatter_dimension=0, tiled=True),
        lax.psum_scatter(third_term, "shard", scatter_dimension=0, tiled=True),
    )


def local_general(
    inputs,
    positions,
    cotangent,
    w_query,
    w_key,
    w_value,
    w_out,
    query_gain,
    key_gain,
    attn_gain,
    w_gate,
    w_up,
    w_down,
    mlp_gain,
):
    row_count, feature_width = inputs.shape
    reach_back = (DOC_LEN - 2) // row_count + 1
    span_rows = min(row_count, 512)
    key_rows = span_rows + reach_back * row_count
    scaling = 1.0 / math.sqrt(HEAD)
    middle = HEAD // 2
    frequency = jnp.power(500000.0, -2.0 * jnp.arange(middle).astype(jnp.float32) / HEAD)
    angles = positions.astype(jnp.float32)[:, None] * frequency[None, :]
    cosines = jnp.cos(angles)[:, None, :]
    sines = jnp.sin(angles)[:, None, :]
    pieces = (
        lax.all_gather(w_query, "shard", axis=0, tiled=True),
        lax.all_gather(w_key, "shard", axis=0, tiled=True),
        lax.all_gather(w_value, "shard", axis=0, tiled=True),
        lax.all_gather(w_out, "shard", axis=0, tiled=True),
        lax.all_gather(query_gain, "shard", axis=0, tiled=True),
        lax.all_gather(key_gain, "shard", axis=0, tiled=True),
        lax.all_gather(attn_gain, "shard", axis=0, tiled=True),
        lax.all_gather(mlp_gain, "shard", axis=0, tiled=True),
    )
    columns_in = inputs
    acc_query = jnp.dot(columns_in, pieces[0], preferred_element_type=jnp.float32)
    acc_key = jnp.dot(columns_in, pieces[1], preferred_element_type=jnp.float32)
    acc_value = jnp.dot(columns_in, pieces[2], preferred_element_type=jnp.float32)
    out_full = pieces[3]
    gain_block = jnp.stack([pieces[4], pieces[5], pieces[6], pieces[7]]).astype(jnp.float32)
    gain_table = gain_block
    q_raw, k_raw, v_raw, out_full, gain_table = (
        acc_query,
        acc_key,
        acc_value,
        out_full,
        gain_table,
    )

    def prepare(query_in, key_in, query_scale, key_scale):
        return (
            rotate(norm_rows(query_in, query_scale), cosines, sines),
            rotate(norm_rows(key_in, key_scale), cosines, sines),
        )

    rotated, prepare_pull = jax.vjp(prepare, q_raw, k_raw, gain_table[0], gain_table[1])
    query_low = rotated[0].astype(jnp.bfloat16)
    key_value = jnp.stack([rotated[1].astype(jnp.bfloat16), v_raw.astype(jnp.bfloat16)])
    earlier = [
        from_behind(key_value, ("grp", "shard"), distance_back)
        for distance_back in range(reach_back, 0, -1)
    ]
    key_window = jnp.concatenate(earlier + [key_value], axis=1)
    distance = (
        jnp.arange(span_rows)[:, None] + reach_back * row_count - jnp.arange(key_rows)[None, :]
    )

    def block_scores(block_start):
        query_block = query_low.reshape(span_rows, HEADS, HEAD)
        key_block = key_window[0, block_start : block_start + key_rows].reshape(
            key_rows, HEADS, HEAD
        )
        value_block = key_window[1, block_start : block_start + key_rows].reshape(
            key_rows, HEADS, HEAD
        )
        visible = (distance >= 0) & (distance <= positions[:, None])
        scores = (
            jnp.einsum("qhd,khd->hqk", query_block, key_block, preferred_element_type=jnp.float32)
            * scaling
        )
        return (query_block, key_block, value_block, visible, scores)

    block_start = 0
    query_block, key_block, value_block, visible, scores = block_scores(block_start)
    masked = jnp.where(visible[None], scores, -jnp.inf)
    top_score = jnp.max(masked, axis=-1, keepdims=True)
    expo = jnp.exp(masked - top_score)
    totals = jnp.sum(expo, axis=-1, keepdims=True)
    probs_low = (expo / totals).astype(jnp.bfloat16)
    lse_parts = [top_score + jnp.log(totals)]
    mixed = jnp.einsum("hqk,khd->qhd", probs_low, value_block, preferred_element_type=jnp.float32)
    mixed_parts = mixed.reshape(span_rows, feature_width)
    mixed_low = mixed_parts.astype(jnp.bfloat16)
    branch = jnp.dot(mixed_low, out_full, preferred_element_type=jnp.float32)
    branch_normed, attn_pull = jax.vjp(norm_rows, branch, gain_table[2])
    hidden_state = inputs.astype(jnp.float32) + branch_normed
    state_low = hidden_state.astype(jnp.bfloat16)
    pieces = (
        lax.all_gather(w_gate, "shard", axis=0, tiled=True),
        lax.all_gather(w_up, "shard", axis=0, tiled=True),
    )
    columns_in = state_low
    gate_val = jnp.dot(columns_in, pieces[0], preferred_element_type=jnp.float32)
    up_val = jnp.dot(columns_in, pieces[1], preferred_element_type=jnp.float32)
    activated, act_pull = jax.vjp(activate, gate_val, up_val)
    activated_low = activated.astype(jnp.bfloat16)
    columns_in = activated_low
    mlp_out = jnp.dot(
        columns_in,
        lax.all_gather(w_down, "shard", axis=0, tiled=True),
        preferred_element_type=jnp.float32,
    )
    mlp_normed, mlp_pull = jax.vjp(norm_rows, mlp_out, gain_table[3])
    output = (hidden_state + mlp_normed).astype(jnp.bfloat16)
    cot_float = cotangent.astype(jnp.float32)
    d_mlp, d_mlp_gain = mlp_pull(cot_float)
    d_mlp_low = d_mlp.astype(jnp.bfloat16)
    d_hidden = along_last(d_mlp_low, lax.all_gather(w_down, "shard", axis=0, tiled=True))
    d_gate, d_up = act_pull(d_hidden)
    d_gate_low = d_gate.astype(jnp.bfloat16)
    d_up_low = d_up.astype(jnp.bfloat16)
    pieces = lax.all_gather((w_gate, w_up), "shard", axis=0, tiled=True)
    d_state = along_last(d_gate_low, pieces[0]) + along_last(d_up_low, pieces[1])
    d_resid = cot_float + d_state
    gate_term = along_first(state_low, d_gate_low)
    up_term = along_first(state_low, d_up_low)
    down_term = along_first(activated_low, d_mlp_low)
    ffn_sums = reduce_three(gate_term, up_term, down_term)
    d_branch, d_attn_gain = attn_pull(d_resid)
    d_branch_low = d_branch.astype(jnp.bfloat16)
    d_mixed_low = along_last(
        d_branch_low, lax.all_gather(w_out, "shard", axis=0, tiled=True)
    ).astype(jnp.bfloat16)
    dq_parts = []
    grad_window = jnp.zeros((2, (reach_back + 1) * row_count, feature_width), jnp.float32)
    for block_number, block_start in enumerate(range(0, row_count, span_rows)):
        query_block, key_block, value_block, visible, scores = block_scores(block_start)
        probs = jnp.where(visible[None], jnp.exp(scores - lse_parts[block_number]), 0.0)
        grad_block = d_mixed_low.reshape(span_rows, HEADS, HEAD)
        d_probs = jnp.einsum(
            "qhd,khd->hqk", grad_block, value_block, preferred_element_type=jnp.float32
        )
        inner = jnp.sum(probs * d_probs, axis=-1, keepdims=True)
        d_scores = (probs * (d_probs - inner) * scaling).astype(jnp.bfloat16)
        dq_block = jnp.einsum(
            "hqk,khd->qhd", d_scores, key_block, preferred_element_type=jnp.float32
        )
        dq_parts.append(dq_block.reshape(span_rows, feature_width))
        d_keys = jnp.einsum(
            "hqk,qhd->khd", d_scores, query_block, preferred_element_type=jnp.float32
        ).reshape(key_rows, feature_width)
        d_values = jnp.einsum(
            "hqk,qhd->khd",
            probs.astype(jnp.bfloat16),
            grad_block,
            preferred_element_type=jnp.float32,
        ).reshape(key_rows, feature_width)
        grad_window = grad_window.at[:, block_start : block_start + key_rows].add(
            jnp.stack([d_keys, d_values])
        )
    own_grads = grad_window[:, reach_back * row_count :]
    for distance_back in range(1, reach_back + 1):
        lower_row = (reach_back - distance_back) * row_count
        own_grads = own_grads + from_behind(
            grad_window[:, lower_row : lower_row + row_count].astype(jnp.bfloat16),
            ("grp", "shard"),
            -distance_back,
        ).astype(jnp.float32)
    d_query_raw, d_key_raw, d_query_gain, d_key_gain = prepare_pull((dq_parts[0], own_grads[0]))
    d_query_low = d_query_raw.astype(jnp.bfloat16)
    d_key_low = d_key_raw.astype(jnp.bfloat16)
    d_value_low = own_grads[1].astype(jnp.bfloat16)
    pieces = lax.all_gather((w_query, w_key, w_value), "shard", axis=0, tiled=True)
    d_inputs = (
        along_last(d_query_low, pieces[0])
        + along_last(d_key_low, pieces[1])
        + along_last(d_value_low, pieces[2])
    )
    input_grad = d_resid + d_inputs
    qkv_term = along_first(inputs, jnp.concatenate([d_query_low, d_key_low, d_value_low], axis=1))
    out_term = along_first(mixed_low, d_branch_low)
    gain_term = jnp.stack([d_query_gain, d_key_gain, d_attn_gain, d_mlp_gain], axis=1)
    attn_sums = reduce_three(qkv_term, out_term, gain_term)
    gate_sum, up_sum, down_sum, qkv_sum, out_sum, gain_sum = (
        lax.psum(ffn_sums[0].astype(jnp.bfloat16), "grp").astype(jnp.float32),
        lax.psum(ffn_sums[1].astype(jnp.bfloat16), "grp").astype(jnp.float32),
        lax.psum(ffn_sums[2].astype(jnp.bfloat16), "grp").astype(jnp.float32),
        lax.psum(attn_sums[0].astype(jnp.bfloat16), "grp").astype(jnp.float32),
        lax.psum(attn_sums[1].astype(jnp.bfloat16), "grp").astype(jnp.float32),
        lax.psum(attn_sums[2].astype(jnp.bfloat16), "grp").astype(jnp.float32),
    )
    return (
        output,
        input_grad,
        qkv_sum[:, :feature_width],
        qkv_sum[:, feature_width : 2 * feature_width],
        qkv_sum[:, 2 * feature_width :],
        out_sum,
        gain_sum[:, 0],
        gain_sum[:, 1],
        gain_sum[:, 2],
        gate_sum,
        up_sum,
        down_sum,
        gain_sum[:, 3],
    )


LINE = 4
SQUARE = 4
X, Y, Z, FAR = 1, 2, 4, 8
ROWS = 128
BLOCKS = 16
SHARE = 256
SCALING = 1.0 / math.sqrt(HEAD)
LINES = [[SQUARE * z + r for z in range(LINE)] for r in range(SQUARE)]
SQUARES = [[SQUARE * z + r for r in range(SQUARE)] for z in range(LINE)]


def swap(value, bit):
    return lax.ppermute(value, "shard", [(source, source ^ bit) for source in range(BLOCKS)])


def swap_core(value):
    return lax.ppermute(value, "grp", [(0, 1), (1, 0)])


def along(bit):
    return lambda value: swap(value, bit)


def line_place():
    return lax.axis_index("shard") // SQUARE


def square_place():
    return lax.axis_index("shard") % SQUARE


def line_move(pairs):
    pairs = [(SQUARE * z + r, SQUARE * to + r) for z, to in pairs for r in range(SQUARE)]
    return lambda value: lax.ppermute(value, "shard", pairs)


RIGHT, LEFT = ((0, 1), (1, 2), (2, 3)), ((3, 2), (2, 1), (1, 0))


def line_step(distance):
    pairs = [(s, (s + SQUARE * distance) % BLOCKS) for s in range(BLOCKS)]
    return lambda value: lax.ppermute(value, "shard", pairs)


def hold(values, *later):
    return lax.optimization_barrier((values, later))[0]


def together(*values):
    return lax.optimization_barrier(values)


def run(*tracks):
    live, results = {}, {}

    def advance(name, generator, came):
        try:
            live[name] = (generator, generator.send(came))
        except StopIteration as end:
            live.pop(name, None)
            results[name] = end.value

    for name, generator in enumerate(tracks):
        advance(name, generator, None)
    while live:
        requests = [request for _, asked in live.values() for request in asked]
        given = lax.optimization_barrier(tuple(value for value, _ in requests))
        came = [move(value) for value, (_, move) in zip(given, requests)]
        came = list(lax.optimization_barrier(tuple(came)))
        for name, (generator, asked) in list(live.items()):
            mine, came = came[: len(asked)], came[len(asked) :]
            advance(name, generator, mine)
    return [results[name] for name in range(len(tracks))]


def one(value, move):
    (came,) = yield [(value, move)]
    return came


def alone(track):
    return run(track)[0]


def gather_first(value):
    right, left = yield [(value, line_move(RIGHT)), (value, line_move(LEFT))]
    return value, right, left


def gather_second(value, right, left):
    return gather_whole(*(yield from gather_pieces(value, right, left)))


def gather_pieces(value, right, left):
    place = line_place()
    further = jnp.where(place == 1, right, left)
    rights, lefts, further = yield [
        (right, line_move(RIGHT[1:])),
        (left, line_move(LEFT[1:])),
        (further, line_move(((1, 3), (2, 0)))),
    ]
    return value, right, left, rights, lefts, further


def gather_whole(*pieces):
    rows, width = pieces[0].shape
    shape = jax.ShapeDtypeStruct((LINE * rows, width), pieces[0].dtype)
    return whole_call(gather_kernel, [shape], [line_place().astype(jnp.int32).reshape(1)], list(pieces))


def gather_kernel(place_ref, own_ref, right_ref, left_ref, rights_ref, lefts_ref, further_ref, out_ref):
    place, rows = place_ref[0], own_ref.shape[0]

    def put(slot, condition, ref):
        @pl.when(condition)
        def _():
            out_ref[slot * rows : (slot + 1) * rows, :] = ref[...]

    out_ref[:rows, :] = own_ref[...]
    put(1, place >= 1, right_ref)
    put(1, place == 0, further_ref)
    put(2, place >= 2, rights_ref)
    put(2, place < 2, lefts_ref)
    put(3, place == 3, further_ref)
    put(3, place < 3, left_ref)


def gather_line(value):
    came = yield from gather_first(value)
    return (yield from gather_second(*came))


def join_kernel(own_ref, other_ref, out_ref):
    rows = own_ref.shape[0]
    out_ref[:rows, :] = own_ref[...]
    out_ref[rows:, :] = other_ref[...]


def join(own, other):
    shape = jax.ShapeDtypeStruct((2 * own.shape[0], own.shape[1]), own.dtype)
    return whole_call(join_kernel, [shape], [], [own, other])


def both_cores(own):
    return join(own, swap_core(own))


def scatter_further(total):
    parts = total.reshape(LINE, -1, total.shape[-1])
    return jnp.where(line_place() == 0, parts[1], parts[3])


def scatter_first(total, further=None):
    parts = total.reshape(LINE, -1, total.shape[-1])
    further = scatter_further(total) if further is None else further
    return (
        yield [
            (parts[2], line_move(RIGHT[:2])),
            (parts[2], line_move(LEFT[:2])),
            (further, line_move(((0, 2), (3, 1)))),
        ]
    )


def scatter_second(total, right, left, further):
    parts = total.reshape(LINE, -1, total.shape[-1])
    place, nothing = line_place(), jnp.zeros((), total.dtype)
    right, left = yield [
        (add_low(parts[3], right, jnp.where(place == 2, further, nothing)), line_move(RIGHT)),
        (add_low(parts[1], left, jnp.where(place == 1, further, nothing)), line_move(LEFT)),
    ]
    return add_wide(parts[0], right, left)


def scatter_line(total, further=None):
    came = yield from scatter_first(total, further)
    return (yield from scatter_second(total, *came))


def add_wide(*values):
    return sum(value.astype(jnp.float32) for value in values)


def add_low(*values):
    return add_wide(*values).astype(jnp.bfloat16)


def turn_line(block):
    return lax.all_to_all(block, "shard", 0, 0, tiled=True, axis_index_groups=LINES)


def to_slots(value):
    place = line_place()
    return jnp.stack(
        [lax.dynamic_index_in_dim(value, (place - k) % LINE, 0, keepdims=False) for k in range(LINE)]
    )


def in_two(value):
    return jnp.split(value, 2, axis=-1)


def square_first(value):
    first, second = in_two(value)
    return swap(first, X), swap(second, Y)


def square_track(value):
    came = yield [(part, along(bit)) for part, bit in zip(in_two(value), (X, Y))]
    return tuple(came)


def second_kernel(own_ref, first_ref, second_ref, to_first_ref, to_second_ref):
    half = own_ref.shape[-1] // 2
    to_first_ref[0] = own_ref[..., :half]
    to_first_ref[1] = first_ref[...]
    to_second_ref[0] = own_ref[..., half:]
    to_second_ref[1] = second_ref[...]


def second_parts(value, came):
    shape = jax.ShapeDtypeStruct((2,) + came[0].shape, value.dtype)
    return whole_call(second_kernel, [shape] * 2, [], [value, *came])


def square_second(value, came):
    first, second = second_parts(value, came)
    return swap(first, Y), swap(second, X)


def second_track(value, came):
    first, second = second_parts(value, came)
    later = yield [(first, along(Y)), (second, along(X))]
    return tuple(later)


def square_kernel(index_ref, own_ref, first_ref, second_ref, firsts_ref, seconds_ref, out_ref):
    half, count = own_ref.shape[-1] // 2, own_ref.shape[0]
    firsts = (own_ref, first_ref, firsts_ref.at[0], firsts_ref.at[1])
    seconds = (own_ref, seconds_ref.at[0], second_ref, seconds_ref.at[1])
    for corner in range(SQUARE):
        for number in range(count):
            target = index_ref[corner * count + number]
            out_ref[target, :, :half] = firsts[corner][number, :, :half]
            lanes = slice(half, None) if corner == 0 else slice(None)
            out_ref[target, :, half:] = seconds[corner][number, :, lanes]


def square_join(index, value, came, later):
    count, rows, width = value.shape
    shape = jax.ShapeDtypeStruct((SQUARE * count, rows, width), value.dtype)
    return whole_call(square_kernel, [shape], [index], [value, *came, *later])


def split_kernel(index_ref, *refs):
    *grad_refs, kept_first, sent_first, kept_second, sent_second = refs
    half, count = kept_first.shape[-1], kept_first.shape[1]
    firsts = ((kept_first, 0), (kept_first, 1), (sent_first, 0), (sent_first, 1))
    seconds = ((kept_second, 0), (sent_second, 0), (kept_second, 1), (sent_second, 1))
    for corner in range(SQUARE):
        for number in range(count):
            row = 0
            for grad_ref in grad_refs:
                block = grad_ref[index_ref[corner * count + number]]
                rows = slice(row, row + block.shape[0])
                row += block.shape[0]
                (target, place), (other, other_place) = firsts[corner], seconds[corner]
                target[place, number, rows, :] = block[:, :half]
                other[other_place, number, rows, :] = block[:, half:]


def sum_split(index, *grads):
    rows = sum(grad.shape[1] for grad in grads)
    shape = (2, grads[0].shape[0] // SQUARE, rows, grads[0].shape[2] // 2)
    shape = jax.ShapeDtypeStruct(shape, grads[0].dtype)
    return whole_call(split_kernel, [shape] * 4, [index], list(grads))


def sum_first(split):
    return swap(split[1], Y), swap(split[3], X)


def low_sum(first, second):
    return (first.astype(jnp.float32) + second.astype(jnp.float32)).astype(jnp.bfloat16)


def add_kernel(kept_first, came_first, kept_second, came_second, *targets):
    for number, (kept, came) in enumerate(((kept_first, came_first), (kept_second, came_second))):
        for place in range(2):
            for block in range(kept.shape[1]):
                targets[2 * number + place][block] = low_sum(kept[place, block], came[place, block])


def sum_later(split, came):
    shape = jax.ShapeDtypeStruct(came[0].shape[1:], jnp.bfloat16)
    arrays = [split[0], came[0], split[2], came[1]]
    first, to_first, second, to_second = whole_call(add_kernel, [shape] * 4, [], arrays)
    return (first, second), (to_first, to_second)


def sum_second(split, came):
    kept, sent = sum_later(split, came)
    return kept, (swap(sent[0], X), swap(sent[1], Y))


def end_kernel(first_ref, came_first, second_ref, came_second, out_ref):
    half = first_ref.shape[-1]
    for block in range(out_ref.shape[0]):
        out_ref[block, :, :half] = low_sum(first_ref[block], came_first[block])
        out_ref[block, :, half:] = low_sum(second_ref[block], came_second[block])


def sum_end(kept, came):
    count, rows, half = kept[0].shape
    shape = jax.ShapeDtypeStruct((count, rows, 2 * half), jnp.bfloat16)
    return whole_call(end_kernel, [shape], [], [kept[0], came[0], kept[1], came[1]])


def in_vmem(count, scalars=1):
    return [pl.BlockSpec(memory_space=pltpu.SMEM)] * scalars + [
        pl.BlockSpec(memory_space=pltpu.VMEM)
    ] * count


def whole_call(kernel, shapes, scalars, arrays, scratch=(), megabytes=40, cost=None):
    specs = [pl.BlockSpec(memory_space=pltpu.VMEM)] * len(shapes)
    single = len(shapes) == 1
    size = sum(array.size * array.dtype.itemsize for array in arrays)
    return pl.pallas_call(
        kernel,
        out_shape=shapes[0] if single else shapes,
        in_specs=in_vmem(len(arrays), len(scalars)),
        out_specs=specs[0] if single else specs,
        scratch_shapes=list(scratch),
        compiler_params=pltpu.CompilerParams(vmem_limit_bytes=megabytes * 2**20),
        cost_estimate=cost or pl.CostEstimate(flops=0, bytes_accessed=2 * size, transcendentals=0),
    )(*scalars, *arrays)


def column_start(columns, parts, place, part, core):
    return pl.multiple_of(place * (columns // LINE) + part * 2 * SHARE + core * SHARE, SHARE)


def pick_kernel(parts, core_ref, *refs):
    *weight_refs, block_ref = refs
    columns = weight_refs[0].shape[1]
    for place in range(LINE):
        for number, weight_ref in enumerate(weight_refs):
            for part in range(parts):
                start = column_start(columns, parts, place, part, core_ref[0])
                lane = (number * parts + part) * SHARE
                block_ref[place, :ROWS, lane : lane + SHARE] = weight_ref[:, pl.ds(start, SHARE)]


def pick_more_kernel(parts, core_ref, *refs):
    *weight_refs, more_ref, block_ref = refs
    pick_kernel(parts, core_ref, *weight_refs, block_ref)
    for place in range(LINE):
        for lane in range(0, block_ref.shape[2], HEAD):
            block_ref[place, ROWS:, lane : lane + HEAD] = more_ref[...]


def spread_kernel(parts, core_ref, mine_ref, came_ref, place_ref, *grad_refs):
    columns = grad_refs[0].shape[1]
    for slot in range(LINE):
        for number, grad_ref in enumerate(grad_refs):
            for part in range(parts):
                lane = (number * parts + part) * SHARE
                for source, core in ((mine_ref, core_ref[0]), (came_ref, 1 - core_ref[0])):
                    start = column_start(columns, parts, place_ref[slot], part, core)
                    grad_ref[:, pl.ds(start, SHARE)] = source[slot, :, lane : lane + SHARE].astype(
                        jnp.float32
                    )


def spread_scalars_kernel(parts, core_ref, place_ref, mine_ref, came_ref, *grad_refs):
    spread_kernel(parts, core_ref, mine_ref, came_ref, place_ref, *grad_refs)


def pick_columns(core_ref, weights, parts, more=None):
    rows, columns = weights[0].shape
    extra = [] if more is None else [more]
    rows += sum(array.shape[0] for array in extra)
    shape = jax.ShapeDtypeStruct((LINE, rows, len(weights) * columns // 8), jnp.bfloat16)
    kernel = functools.partial(pick_more_kernel if extra else pick_kernel, parts)
    return whole_call(kernel, [shape], [core_ref], [*weights, *extra])


def spread_columns(core_ref, place_ref, mine, came, count, parts):
    shape = jax.ShapeDtypeStruct((mine.shape[1], 8 * mine.shape[2] // count), jnp.float32)
    kernel = functools.partial(spread_scalars_kernel, parts)
    return whole_call(kernel, [shape] * count, [core_ref, place_ref], [mine, came])


def gated_grad_kernel(grad_ref, both_ref, out_ref):
    width = grad_ref.shape[1]
    gate, up, grad = both_ref[:, :width], both_ref[:, width:], grad_ref[...]
    sigma = 1.0 / (1.0 + jnp.exp(-gate))
    out_ref[:, :width] = (grad * up * sigma * (1.0 + gate * (1.0 - sigma))).astype(jnp.bfloat16)
    out_ref[:, width:] = (grad * gate * sigma).astype(jnp.bfloat16)


def gated_grad(grad, both):
    rows, width = grad.shape
    narrow, wide = (pl.BlockSpec((ROWS, w), lambda i: (i, 0)) for w in (width, 2 * width))
    return pl.pallas_call(
        gated_grad_kernel,
        out_shape=jax.ShapeDtypeStruct(both.shape, jnp.bfloat16),
        grid=(rows // ROWS,),
        in_specs=[narrow, wide],
        out_specs=wide,
        compiler_params=pltpu.CompilerParams(vmem_limit_bytes=32 * 2**20),
        cost_estimate=pl.CostEstimate(
            flops=20 * grad.size, bytes_accessed=16 * grad.size, transcendentals=grad.size
        ),
    )(grad, both)


def head_lanes(head):
    return slice(head * HEAD, (head + 1) * HEAD)


def halo_slots(place):
    return lax.rem(place + 2, LINE), lax.rem(place + 1, LINE)


def rotated(value, cosines, sines):
    return value * cosines + pltpu.roll(value, HEAD // 2, 1) * sines


def rotated_back(value, cosines, sines):
    return value * cosines - pltpu.roll(value, HEAD // 2, 1) * sines


def part_of(group, core):
    return core if group == 0 else 1 - core


def pack_kernel(core_ref, place_ref, raw_ref, scale_ref, gain_ref, cos_ref, sin_ref, out_ref):
    for group in range(2):
        part = part_of(group, core_ref[0])
        for head in range(2):
            target = 2 * group + head
            for slot in range(LINE):
                for number in range(2):
                    lanes = slice((2 * number + head) * HEAD, (2 * number + head + 1) * HEAD)
                    value = raw_ref[part, slot, :, lanes] * scale_ref[number, part, slot]
                    value = value * gain_ref[number : number + 1, head_lanes(head)]
                    value = rotated(value, cos_ref[part, slot], sin_ref[part, slot])
                    out_ref[target, LINE * number + slot] = value.astype(jnp.bfloat16)
                lanes = slice((4 + head) * HEAD, (5 + head) * HEAD)
                out_ref[target, 2 * LINE + slot] = raw_ref[part, slot, :, lanes].astype(jnp.bfloat16)
    for target in range(SQUARE):
        for number, slot in enumerate(halo_slots(place_ref[0])):
            out_ref[target, 12 + number] = out_ref[target % 2, LINE + slot]
            out_ref[target, 14 + number] = out_ref[target % 2, 2 * LINE + slot]


def unpack_kernel(core_ref, came_ref, out_ref):
    for group in range(2):
        part = core_ref[0] if group == 0 else 1 - core_ref[0]
        for head in range(2):
            for slot in range(LINE):
                out_ref[part, slot, :, head_lanes(head)] = came_ref[2 * group + head, slot]


def pack_grad_kernel(core_ref, grad_ref, out_ref):
    for group in range(2):
        part = core_ref[0] if group == 0 else 1 - core_ref[0]
        for head in range(2):
            for slot in range(LINE):
                out_ref[2 * group + head, slot] = grad_ref[part, slot, :, head_lanes(head)]


def unpack_grad_kernel(
    core_ref,
    place_ref,
    came_ref,
    raw_ref,
    scale_ref,
    gain_ref,
    cos_ref,
    sin_ref,
    grad_ref,
    value_ref,
    sums_ref,
    gain_grad_ref,
):
    core = core_ref[0]

    def summed(first, part, slot, head):
        total = came_ref[2 * part_of(part, core) + head, first + slot].astype(jnp.float32)
        for number, end_slot in enumerate(halo_slots(place_ref[0])):
            here = jnp.where((core == part) & (end_slot == slot), 1.0, 0.0)
            total += here * came_ref[2 + head, 10 + first // 2 + number].astype(jnp.float32)
        return total

    totals = [[jnp.zeros((1, HEAD), jnp.float32) for _ in range(2)] for _ in range(2)]
    for part in range(2):
        for slot in range(LINE):
            sums = [jnp.zeros((ROWS, 1), jnp.float32) for _ in range(2)]
            for head in range(2):
                lanes = head_lanes(head)
                value_ref[part, slot, :, lanes] = summed(8, part, slot, head).astype(jnp.bfloat16)
                d_query = came_ref[2 * part_of(part, core) + head, slot].astype(jnp.float32)
                for number, grad in ((0, d_query), (1, summed(4, part, slot, head))):
                    grad = rotated_back(grad, cos_ref[part, slot], sin_ref[part, slot])
                    raw_lanes = slice((2 * number + head) * HEAD, (2 * number + head + 1) * HEAD)
                    raw = raw_ref[part, slot, :, raw_lanes]
                    totals[number][head] += jnp.sum(
                        grad * raw * scale_ref[number, part, slot], axis=0, keepdims=True
                    )
                    grad = grad * gain_ref[number : number + 1, lanes]
                    sums[number] += jnp.sum(grad * raw, axis=1, keepdims=True)
                    grad_ref[number, part, slot, :, lanes] = grad
            for number in range(2):
                sums_ref[number, part, slot] = sums[number]
    for number in range(2):
        for head in range(2):
            gain_grad_ref[number : number + 1, head_lanes(head)] = totals[number][head]


def norm_grad_kernel(grad_ref, value_ref, raw_ref, scale_ref, mean_ref, out_ref):
    for part in range(2):
        for slot in range(LINE):
            for number in range(2):
                lanes = slice(2 * number * HEAD, 2 * (number + 1) * HEAD)
                scale = scale_ref[number, part, slot]
                grad = grad_ref[number, part, slot] * scale - raw_ref[part, slot, :, lanes] * (
                    scale * scale * scale * mean_ref[number, part, slot]
                )
                out_ref[part, slot, :, lanes] = grad.astype(jnp.bfloat16)
            out_ref[part, slot, :, 4 * HEAD :] = value_ref[part, slot]


def visible_of(seen):
    shape = (seen.shape[0], DOC_LEN + seen.shape[0])
    row = lax.broadcasted_iota(jnp.int32, shape, 0)
    column = lax.broadcasted_iota(jnp.int32, shape, 1)
    distance = row - column + DOC_LEN
    return (distance >= 0) & (distance <= seen)


def dot_last(left, right):
    return lax.dot_general(
        left, right, (((1,), (1,)), ((), ())), preferred_element_type=jnp.float32
    )


def stream_row(place, source, slot):
    block = lax.rem(place - slot + LINE, LINE) * SQUARE + source
    return block, pl.multiple_of(block * ROWS, ROWS)


def rows_at(start):
    return pl.ds(pl.multiple_of(start, ROWS), ROWS)


def fill(place, message_ref, keys, values):
    for source in range(SQUARE):
        for slot in range(LINE):
            _, start = stream_row(place, source, slot)
            keys[rows_at(start + DOC_LEN), :] = message_ref[source, LINE + slot]
            values[rows_at(start + DOC_LEN), :] = message_ref[source, 2 * LINE + slot]
        for number in range(2):
            start = (number * SQUARE + source) * ROWS
            keys[start : start + ROWS, :] = message_ref[source, 12 + number]
            values[start : start + ROWS, :] = message_ref[source, 14 + number]


def attend_kernel(place_ref, message_ref, pos_ref, o_ref, lse_ref, keys, values):
    place = place_ref[0]
    fill(place, message_ref, keys, values)

    def step(number, carry):
        count, rows_of = 2, 2 * ROWS
        first, slot = count * (number // LINE), number % LINE
        sources = pl.ds(first, count)
        block, start = stream_row(place, first, slot)
        rows = pl.ds(start, DOC_LEN + rows_of)
        query = message_ref[sources, slot].reshape(rows_of, HEAD)
        scores = dot_last(query, keys[rows, :]) * SCALING
        seen = pos_ref[pl.ds(block, count)].reshape(rows_of, 1)
        masked = jnp.where(visible_of(seen), scores, -jnp.inf)
        top = jnp.max(masked, axis=-1, keepdims=True)
        expo = jnp.exp(masked - top)
        total = jnp.sum(expo, axis=-1, keepdims=True)
        probs = (expo * (1.0 / total)).astype(jnp.bfloat16)
        mixed = jnp.dot(probs, values[rows, :], preferred_element_type=jnp.float32)
        o_ref[sources, slot] = mixed.astype(jnp.bfloat16).reshape(count, ROWS, HEAD)
        lse_ref[pl.ds(block, count)] = (top + jnp.log(total)).reshape(count, ROWS, 1)
        return carry

    lax.fori_loop(0, BLOCKS // 2, step, 0)


def attend_back_kernel(
    place_ref, message_ref, pos_ref, lse_ref, do_ref, out_ref, keys, values, d_keys, d_values
):
    place = place_ref[0]
    fill(place, message_ref, keys, values)
    d_keys[...] = jnp.zeros_like(d_keys)
    d_values[...] = jnp.zeros_like(d_values)

    def step(number, carry):
        count, rows_of = 4, 4 * ROWS
        first, slot = count * (number // LINE), number % LINE
        sources = pl.ds(first, count)
        block, start = stream_row(place, first, slot)
        rows = pl.ds(start, DOC_LEN + rows_of)
        query = message_ref[sources, slot].reshape(rows_of, HEAD)
        grad = do_ref[sources, slot].reshape(rows_of, HEAD)
        key, value = keys[rows, :], values[rows, :]
        scores = dot_last(query, key) * SCALING
        seen = pos_ref[pl.ds(block, count)].reshape(rows_of, 1)
        lse = lse_ref[pl.ds(block, count)].reshape(rows_of, 1)
        probs = jnp.where(visible_of(seen), jnp.exp(scores - lse), 0.0)
        d_probs = dot_last(grad, value)
        inner = jnp.sum(probs * d_probs, axis=-1, keepdims=True)
        d_scores = (probs * (d_probs - inner) * SCALING).astype(jnp.bfloat16)
        d_query = jnp.dot(d_scores, key, preferred_element_type=jnp.float32)
        out_ref[sources, slot] = d_query.astype(jnp.bfloat16).reshape(count, ROWS, HEAD)
        d_keys[rows, :] += along_first(d_scores, query)
        d_values[rows, :] += along_first(probs.astype(jnp.bfloat16), grad)
        return carry

    lax.fori_loop(0, BLOCKS // 4, step, 0)
    for source in range(SQUARE):
        for slot in range(LINE):
            _, start = stream_row(place, source, slot)
            out_ref[source, LINE + slot] = d_keys[rows_at(start + DOC_LEN), :].astype(jnp.bfloat16)
            out_ref[source, 2 * LINE + slot] = d_values[rows_at(start + DOC_LEN), :].astype(jnp.bfloat16)
        for number in range(2):
            start = (number * SQUARE + source) * ROWS
            out_ref[source, 12 + number] = d_keys[start : start + ROWS, :].astype(jnp.bfloat16)
            out_ref[source, 14 + number] = d_values[start : start + ROWS, :].astype(jnp.bfloat16)


KEPT = [pltpu.VMEM((3 * DOC_LEN, HEAD), jnp.bfloat16)] * 2
SUMMED = [pltpu.VMEM((3 * DOC_LEN, HEAD), jnp.float32)] * 2


def attend(place_ref, message, positions):
    shapes = [
        jax.ShapeDtypeStruct((SQUARE, LINE, ROWS, HEAD), jnp.bfloat16),
        jax.ShapeDtypeStruct((BLOCKS, ROWS, 1), jnp.float32),
    ]
    return whole_call(attend_kernel, shapes, [place_ref], [message, positions], KEPT)


def attend_back(place_ref, message, positions, lse, grad):
    shape = jax.ShapeDtypeStruct(message.shape, jnp.bfloat16)
    arrays = [message, positions, lse, grad]
    return whole_call(attend_back_kernel, [shape], [place_ref], arrays, KEPT + SUMMED)


def turn_square(message):
    return lax.all_to_all(message, "shard", 0, 0, tiled=True, axis_index_groups=SQUARES)


def turned_kernel(place_ref, block_ref, *refs):
    came_refs, (whole_ref, first_ref, second_ref) = refs[: LINE - 1], refs[LINE - 1 :]
    half = whole_ref.shape[-1] // 2
    own_ref = block_ref.at[place_ref[0]]
    for slot, ref in enumerate((own_ref, *came_refs)):
        whole_ref[slot] = ref[...]
        first_ref[slot] = ref[:, :half]
        second_ref[slot] = ref[:, half:]


def turned_line(place_ref, block, came):
    half = jax.ShapeDtypeStruct(block.shape[:-1] + (block.shape[-1] // 2,), block.dtype)
    whole = jax.ShapeDtypeStruct(block.shape, block.dtype)
    whole, *parts = whole_call(turned_kernel, [whole, half, half], [place_ref], [block, *came])
    return whole, parts


def local_line(
    inputs,
    positions,
    cotangent,
    w_query,
    w_key,
    w_value,
    w_out,
    query_gain,
    key_gain,
    attn_gain,
    w_gate,
    w_up,
    w_down,
    mlp_gain,
):
    bf16, f32 = jnp.bfloat16, jnp.float32
    width = inputs.shape[1]
    core_index = lax.axis_index("grp")
    shard_index = lax.axis_index("shard")
    core = core_index == 1
    place, corner = line_place(), square_place()
    core_ref = core_index.astype(jnp.int32).reshape(1)
    place_ref = place.astype(jnp.int32).reshape(1)
    slots = jnp.arange(LINE, dtype=jnp.int32)
    slot_places = (place - slots) % LINE
    hidden = w_down.shape[0] * 2
    tokens = 2 * LINE * ROWS
    part_tokens = tokens // 2
    heads = 2 * HEAD
    from_slots = (slot_places[None, :] * SQUARE + (corner ^ slots)[:, None]).reshape(-1)
    from_order = (slots[None, :] * SQUARE + (corner ^ slots)[:, None]).reshape(-1)
    from_corner = corner ^ slots

    def region(function, *given):
        shapes = jax.eval_shape(function, *given)
        empty = lambda *given: jax.tree.map(lambda leaf: jnp.zeros(leaf.shape, leaf.dtype), shapes)
        return lax.cond(positions[0] >= 0, function, empty, *given)

    def across_cores(left, right, product):
        other = swap_core(product(left[1], right).astype(bf16))
        own = together(product(left[0], right).astype(bf16))[0]
        return add_low(own, other)

    def parts_of(value):
        return value[:part_tokens], value[part_tokens:]

    def dot(left, right):
        return jnp.dot(left, right, preferred_element_type=f32)

    small = jnp.concatenate(
        [
            jnp.stack([query_gain, key_gain, attn_gain, mlp_gain]),
            jnp.stack([positions // 32, positions % 32]).astype(bf16),
            jnp.zeros((10, ROWS), bf16),
        ]
    )
    down_own = lax.dynamic_index_in_dim(w_down.reshape(2, 1, hidden // SQUARE, width), core_index, 0, keepdims=False)
    rows_own = jnp.concatenate([w_out[None], down_own], axis=1)
    head_block, rows_came = run(
        one(pick_columns(core_ref, (w_query, w_key, w_value), 1, small), turn_line),
        square_track(rows_own),
    )
    x_came, head_came = run(gather_first(inputs), square_track(head_block))
    x_own, head_later, rows_parts = run(
        gather_second(*x_came),
        second_track(head_block, head_came),
        one((rows_own, rows_came), lambda given: second_parts(*given)),
    )
    rows_later = swap(rows_parts[0], Y), swap(rows_parts[1], X)
    head_block = square_join(from_order, head_block, head_came, head_later)
    qkv_w = head_block[:, :ROWS].reshape(width, 3 * heads)
    gains = head_block[:, ROWS : ROWS + 4, :HEAD].astype(f32)
    first_head = place * SQUARE + core_index * 2
    head_gain = lax.dynamic_slice_in_dim(gains, first_head, 2, 0)[:, :2].transpose(1, 0, 2).reshape(2, heads)
    gains = gains.transpose(1, 0, 2).reshape(4, width)
    stream = head_block[:, ROWS + 4 : ROWS + 6, :HEAD].astype(jnp.int32)
    stream = stream[:, 0] * 32 + stream[:, 1]
    stream_other = swap_core(stream)
    query_places = jnp.where((corner >= 2) == core, stream, stream_other).reshape(BLOCKS, ROWS, 1)
    held = [
        to_slots(lax.dynamic_index_in_dim(part.reshape(LINE, SQUARE, ROWS), corner, 1, keepdims=False))
        for part in (stream, stream_other)
    ]
    middle = HEAD // 2
    frequency = jnp.power(500000.0, -2.0 * (jnp.arange(HEAD) % middle).astype(f32) / HEAD)
    def sums_track(value):
        for bit in (Z, FAR):
            (came,) = yield [(value, along(bit))]
            value = value + came
        (came,) = yield [(value, swap_core)]
        return value + jnp.flip(came, 2)

    def row_sums(sums):
        return to_slots(sums.transpose(2, 0, 1, 3))

    def row_means(sums):
        return to_slots(sums).transpose(1, 2, 0, 3)[..., None] / width

    def projected(x_own, qkv_w, *held):
        x_other = swap_core(x_own)
        raw = jnp.stack([dot(x_own, qkv_w), dot(x_other, qkv_w)]).reshape(2, LINE, ROWS, 3 * heads)
        squares = raw[..., : 2 * heads] * raw[..., : 2 * heads]
        sums = jnp.stack([jnp.sum(squares[..., :heads], axis=-1), jnp.sum(squares[..., heads:], axis=-1)])
        angles = jnp.stack(held).astype(f32)[..., None] * frequency
        sign = jnp.where(jnp.arange(HEAD) < middle, -1.0, 1.0)
        return x_other, raw, alone(sums_track(row_sums(sums))), jnp.cos(angles), jnp.sin(angles) * sign

    x_other, raw, sums, cosines, sines = region(projected, x_own, qkv_w, *held)
    scales = lax.rsqrt(row_means(sums) + 1e-06)

    hidden_block = hold(pick_columns(core_ref, (w_gate, w_up), SQUARE), sums)
    line_came = [
        line_step(k)(lax.dynamic_index_in_dim(hidden_block, (place + k) % LINE, 0, keepdims=False))
        for k in range(1, LINE)
    ]
    shape = (2, LINE, ROWS, heads)
    message_shape = jax.ShapeDtypeStruct((SQUARE, 16, ROWS, HEAD), bf16)
    heads_shape = jax.ShapeDtypeStruct((SQUARE, LINE, ROWS, HEAD), bf16)
    tokens_shape = jax.ShapeDtypeStruct(shape, bf16)

    tables = [head_gain, cosines, sines]

    def attended(message):
        message = turn_square(message)
        mixed, lse = attend(place_ref, message, query_places)
        mixed = whole_call(unpack_kernel, [tokens_shape], [core_ref], [turn_square(mixed)])
        rows_w = square_join(from_corner, rows_own, rows_came, rows_later)
        return message, lse, mixed.reshape(tokens, heads), rows_w

    packed = whole_call(pack_kernel, [message_shape], [core_ref, place_ref], [raw, scales, *tables])
    packed, rows_later = together(packed, rows_later)
    message, lse, mixed, rows_w = region(attended, packed)
    mixed, line_came = together(mixed, line_came)
    out_w = lax.dynamic_slice(rows_w, (core_index * 2, 0, 0), (2, ROWS, width)).reshape(heads, width)
    hidden_own, parts = turned_line(place_ref, hidden_block, line_came)
    hidden_came = swap(parts[0], X), swap(parts[1], Y)

    branch = across_cores(parts_of(mixed), out_w, dot)
    branch, down_w = region(
        lambda total, further, rows: (alone(scatter_line(total, further)), rows[:, ROWS:].reshape(-1, width)), branch, scatter_further(branch), rows_w
    )
    branch, hidden_came = together(branch, hidden_came)
    hidden_later = square_second(hidden_own, hidden_came)

    def state_of(branch):
        branch_scale = lax.rsqrt(jnp.mean(branch * branch, axis=-1, keepdims=True) + 1e-06)
        hidden_state = inputs.astype(f32) + branch * branch_scale * gains[2]
        state = alone(gather_pieces(*alone(gather_first(hidden_state.astype(bf16)))))
        return branch_scale, hidden_state, state

    branch_scale, hidden_state, state = region(state_of, branch)
    state, hidden_later = together(state, hidden_later)
    hidden_w = square_join(from_slots, hidden_own, hidden_came, hidden_later).reshape(width, -1)

    state = gather_whole(*state)
    state = (state, swap_core(state))
    both = [dot(part, hidden_w) for part in state]
    active = [(jax.nn.silu(in_two(part)[0]) * in_two(part)[1]).astype(bf16) for part in both]
    mlp, (state, both, active) = run(
        scatter_line(across_cores(active, down_w, dot)),
        one((state, both, active), lambda pairs: [join(*pair) for pair in pairs]),
    )
    mlp_scale = lax.rsqrt(jnp.mean(mlp * mlp, axis=-1, keepdims=True) + 1e-06)
    cot = cotangent.astype(f32)
    scaled = cot * gains[3]
    d_mlp = mlp_scale * scaled - mlp * mlp_scale**3 * jnp.mean(mlp * scaled, axis=-1, keepdims=True)

    def finished(given):
        cotangent, hidden_state, mlp, mlp_scale = given
        normed = mlp * mlp_scale
        output = (hidden_state + normed * gains[3]).astype(bf16)
        return output, jnp.sum(cotangent.astype(f32) * normed, axis=0)

    d_mlp, (output, mlp_gain_part) = run(
        gather_line(d_mlp.astype(bf16)), one((cotangent, hidden_state, mlp, mlp_scale), finished)
    )
    d_mlp = both_cores(d_mlp)

    d_both = gated_grad(along_last(d_mlp, down_w), both)

    total = across_cores(parts_of(d_both), hidden_w, along_last)

    def d_state_begun(total, state, d_both):
        carried = alone(scatter_first(total))
        hidden_grad = along_first(state, d_both).astype(bf16).reshape(BLOCKS, ROWS, -1)
        return carried, sum_split(from_order, hidden_grad)

    carried, hidden_split = region(d_state_begun, total, state, d_both)
    hidden_came = sum_first(hidden_split)

    def d_branch_begun(total, carried):
        d_resid = cotangent.astype(f32) + alone(scatter_second(total, *carried))
        scaled = d_resid * gains[2]
        d_branch = branch_scale * scaled - branch * branch_scale**3 * jnp.mean(
            branch * scaled, axis=-1, keepdims=True
        )
        return d_resid, alone(gather_first(d_branch.astype(bf16)))

    def d_branch_of(d_branch, d_resid):
        d_branch = (d_branch, swap_core(d_branch))
        norms = jnp.stack([jnp.sum(d_resid * branch * branch_scale, axis=0), mlp_gain_part])
        return d_branch, jnp.stack([along_last(part, out_w).astype(bf16) for part in d_branch]), norms

    d_resid, d_branch = region(d_branch_begun, total, carried)
    d_branch, hidden_came = together(d_branch, hidden_came)
    hidden_kept, hidden_came = sum_second(hidden_split, hidden_came)
    d_branch, d_mixed, norms = region(d_branch_of, alone(gather_second(*d_branch)), d_resid)
    d_mixed, hidden_came = together(d_mixed, hidden_came)
    hidden_grad = sum_end(hidden_kept, hidden_came)
    line_came = [
        line_step(k)(lax.dynamic_index_in_dim(hidden_grad, (place + k) % LINE, 0, keepdims=False))
        for k in range(1, LINE)
    ]

    def attended_back(d_mixed, message, lse, d_branch, mixed, active, d_mlp, raw, scales, *tables):
        grad = whole_call(pack_grad_kernel, [heads_shape], [core_ref], [d_mixed.reshape(shape)])
        grads = attend_back(place_ref, message, query_places, lse, turn_square(grad))
        grads = turn_square(grads)
        down_grad = along_first(active, d_mlp).astype(bf16).reshape(SQUARE, -1, width)
        out_grad = sum(along_first(*pair) for pair in zip(parts_of(mixed), d_branch))
        out_grad = out_grad.reshape(1, 2, ROWS, width)
        out_grad = jnp.where(core == jnp.arange(2).reshape(2, 1, 1, 1), out_grad, 0.0).astype(bf16)
        shapes = [
            jax.ShapeDtypeStruct((2,) + shape, f32),
            tokens_shape,
            jax.ShapeDtypeStruct((2, 2, LINE, ROWS, 1), f32),
            jax.ShapeDtypeStruct((2, heads), f32),
        ]
        return (
            whole_call(
                unpack_grad_kernel,
                shapes,
                [core_ref, place_ref],
                [grads, raw, scales, *tables],
            ),
            sum_split(from_corner, out_grad.reshape(SQUARE, ROWS, width), down_grad),
        )

    (d_head, d_value, sums, head_part), rows_split = region(
        attended_back, d_mixed, message, lse, d_branch, mixed, active, d_mlp, raw, scales, *tables
    )
    d_head, sums, line_came = together(d_head, sums, line_came)
    hidden_grad, _ = turned_line(place_ref, hidden_grad, line_came)
    hidden_other = swap_core(hidden_grad)
    rows_grads_came = sum_first(rows_split)

    head_part = head_part.reshape(2, 1, 2, HEAD)
    head_part = jnp.where(core == jnp.arange(2).reshape(1, 2, 1, 1), head_part, 0.0)

    def gain_sums(norms, heads):
        for bit in (Z, FAR):
            (came,) = yield [(norms, along(bit))]
            norms = norms + came
        both = jnp.concatenate([norms.reshape(-1, ROWS), heads.reshape(-1, ROWS)])
        (came,) = yield [(both, swap_core)]
        return both + came

    def gains_to(bit):
        return lambda value: value + swap(value, bit)

    def d_qkv_of(sums, head_part, norms, d_head, d_value, raw, scales, *x_parts):
        sums, gain_grads, x_all = run(
            sums_track(row_sums(sums.reshape(2, 2, LINE, ROWS))),
            gain_sums(norms, head_part),
            one(x_parts, lambda parts: join(*parts)),
        )
        qkv_shape = jax.ShapeDtypeStruct(raw.shape, bf16)
        arrays = [d_head, d_value, raw, scales, row_means(sums)]
        d_qkv = whole_call(norm_grad_kernel, [qkv_shape], [], arrays).reshape(tokens, -1)
        total = across_cores(parts_of(d_qkv), qkv_w, along_last)
        qkv_grad = along_first(x_all, d_qkv).astype(bf16)
        qkv_grad = with_layout_constraint(qkv_grad, Layout(major_to_minor=(0, 1)))
        return total, sum_split(from_order, qkv_grad.reshape(BLOCKS, ROWS, -1)), gain_grads

    total, qkv_split, gain_grads = region(
        d_qkv_of, sums, head_part, norms, d_head, d_value, raw, scales, x_own, x_other
    )
    total, rows_grads_came = together(total, rows_grads_came)
    def first_track(split):
        return (yield [(split[1], along(Y)), (split[3], along(X))])

    def later_track(split, came):
        kept, (first, second) = sum_later(split, came)
        came = yield [(first, along(X)), (second, along(Y))]
        return sum_end(kept, came)

    def inputs_begun(total, split, hidden_grad, hidden_other, rows_split, rows_came):
        hidden_grads = spread_columns(core_ref, slot_places, hidden_grad, hidden_other, 2, SQUARE)
        rows_grads = sum_later(rows_split, rows_came)
        return run(scatter_first(total), first_track(split)), hidden_grads, rows_grads

    (carried, qkv_came), (gate_grad, up_grad), rows_grads = region(
        inputs_begun, total, qkv_split, hidden_grad, hidden_other, rows_split, rows_grads_came
    )
    def inputs_ended(total, *carried):
        return d_resid + (yield from scatter_second(total, *carried))

    input_grad, qkv_grad = region(
        lambda total, carried, split, came: (
            alone(inputs_ended(total, *carried)),
            alone(later_track(split, came)),
        ),
        total,
        carried,
        qkv_split,
        qkv_came,
    )
    qkv_grad = turn_line(qkv_grad)

    def rows_ended(kept, sent, gain_grads):
        *came, gain_grads = yield [(sent[0], along(X)), (sent[1], along(Y)), (gain_grads, gains_to(X))]
        mine = jnp.concatenate([add_low(*pair) for pair in zip(kept, came)], axis=-1)[0]
        other, gain_grads = yield [(mine, swap_core), (gain_grads, gains_to(Y))]
        out_grad = mine[:ROWS].astype(f32) + other[:ROWS].astype(f32)
        mine, other = mine[ROWS:], other[ROWS:]
        down_grad = jnp.concatenate([jnp.where(core, other, mine), jnp.where(core, mine, other)])
        return out_grad, down_grad.astype(f32), gain_grads

    rows_grads, gain_grads = hold((rows_grads, gain_grads), input_grad)
    out_grad, down_grad, gain_grads = region(
        lambda grads, gains: alone(rows_ended(*grads, gains)), rows_grads, gain_grads
    )
    qkv_grad, out_grad = together(qkv_grad, out_grad)
    qkv_other = swap_core(qkv_grad)
    norms, head_grads = (
        lax.dynamic_index_in_dim(part.reshape(2, -1, ROWS), number, 1, keepdims=False)
        for part, number in ((gain_grads[: 2 * BLOCKS], shard_index), (gain_grads[2 * BLOCKS :], corner))
    )
    query_grad, key_grad, value_grad = spread_columns(core_ref, slots, qkv_grad, qkv_other, 3, 1)
    return (
        output,
        input_grad,
        query_grad,
        key_grad,
        value_grad,
        out_grad,
        head_grads[0],
        head_grads[1],
        norms[0],
        gate_grad,
        up_grad,
        down_grad,
        norms[1],
    )


def solution(mesh):
    on_line = mesh.shape["grp"] == 2 and mesh.shape["shard"] == 16
    placed = (
        P(("grp", "shard"), None),
        P(("grp", "shard")),
        P(("grp", "shard"), None),
        P("shard", None),
        P("shard", None),
        P("shard", None),
        P("shard", None),
        P("shard"),
        P("shard"),
        P("shard"),
        P("shard", None),
        P("shard", None),
        P("shard", None),
        P("shard"),
    )
    return jax.shard_map(
        local_line if on_line else local_general,
        mesh=mesh,
        in_specs=placed,
        out_specs=(
            P(("grp", "shard"), None),
            P(("grp", "shard"), None),
            P("shard", None),
            P("shard", None),
            P("shard", None),
            P("shard", None),
            P("shard"),
            P("shard"),
            P("shard"),
            P("shard", None),
            P("shard", None),
            P("shard", None),
            P("shard"),
        ),
        check_vma=False,
    )
```
